32 devices in a mesh: patch: 2 (over x), wrow: 4 (over z), wcol: 4 (over y, core).
Axes of the slice: x: 2, y: 2, z: 4, core: 2. Of those that a mesh axis runs over, the one named last changes fastest.
Arguments:
- hidden_states: bfloat16 [4, 1024, 1536], P('wrow', ('patch', 'wcol')), may hold values from -6 to 6
- modulation: float32 [4, 3, 1536], P('wrow'), may hold values from -4 to 4
- w_qkv: bfloat16 [1536, 3, 1536], P('wrow', None, 'wcol'), may hold values from -1 to 1
- w_out: bfloat16 [1536, 1536], P('wcol', 'wrow'), may hold values from -0.15625 to 0.15625
- lengths: int32 [4], P('wrow'), may hold values from 1 to 1024, 2560 in all
Outputs:
- updated: bfloat16 [4, 1024, 1536], P('wrow', ('patch', 'wcol'))
The draws below stay inside these ranges and needn't reach their ends.
Inputs may be any that keep to these rules, and one draw needn't show every extreme that they name: lengths[v] real tokens in video v, padding after them; the longest video fills all 1024 slots.
All inputs are finite; a program needn't handle non-finite values. No bound on the sum of `lengths` on one device may be relied on, other than what follows from the above.
Results may differ from the reference program's by a relative error of at most 0.015.
The reference program's roundings to bfloat16 on the way count: a program that leaves them out, or rounds other values in their place, can miss the bound.
Values may be sent and summed in bfloat16 or wider, within the bound.
No kernel may reach another device: no remote copies, remote signals or barrier semaphores. Data moves between devices by JAX's collectives and lax.ppermute only.
A program may use at most 64 MiB of HBM per device.

```python
import math
import jax
import jax.numpy as jnp
import numpy as np
from jax import lax

D = 1536
HEADS = 12
HD = 128
SEQ = 1024
VIDEOS = 4


def draw_w_qkv(key, part):
    key_query, key_key, key_value = jax.random.split(key, 3)
    base = D ** (-0.5)
    query_w = jax.random.normal(key_query, (D, D), jnp.float32) * base
    key_w = jax.random.normal(key_key, (D, D), jnp.float32) * base
    value_w = jax.random.normal(key_value, (D, D), jnp.float32) * base
    stacked = jnp.stack([query_w, key_w, value_w], axis=1)
    return jnp.clip(stacked, -1.0, 1.0).astype(jnp.bfloat16)


def block_scale(own_key, dims, pieces, least, top_value):
    def one(position, blocks):
        steps = jax.random.uniform(jax.random.fold_in(jax.random.fold_in(own_key, 6), position), (blocks,), jnp.float32, least / len(pieces), top_value / len(pieces))
        return jnp.repeat(jnp.exp(steps), dims[position] // blocks).reshape((-1,) + (1,) * (len(dims) - position - 1))

    gain = one(*pieces[0])
    for cut in pieces[1:]:
        gain = gain * one(*cut)
    return gain


def split_up(number_of, total, most, slope):
    loads = [(1 << 20) // math.isqrt(rank ** slope) + 1 for rank in range(2, number_of + 1)]
    spare, given = total - most - (number_of - 1), [1] * (number_of - 1)
    while spare > 0:
        movable = [i for i in range(number_of - 1) if given[i] < most]
        whole, remaining = sum([loads[i] for i in movable]), spare
        for i in movable:
            extra = min(most - given[i], max(1, remaining * loads[i] // whole), spare)
            given[i] = given[i] + extra
            spare = spare - extra
    return np.array([most] + given)


def uneven(key, number_of, total, most, lean):
    if number_of == 2:
        one = jax.random.randint(key, (), max(1, total - most), min(most, total - 1) + 1)
        return jnp.stack([one, total - one])
    tallies = jnp.asarray(split_up(number_of, total, most, lean), jnp.int32)
    couples = (number_of - 1) // 2
    giver, sink = tallies[1:1 + 2 * couples:2], tallies[2:2 + 2 * couples:2]
    room = jnp.minimum(giver - 1, most - sink)
    passed = jax.random.randint(jax.random.fold_in(key, 1), (couples,), 0, 1 << 20) % (room + 1)
    tallies = tallies.at[1:1 + 2 * couples:2].set(giver - passed).at[2:2 + 2 * couples:2].set(sink + passed)
    return tallies[jax.random.permutation(jax.random.fold_in(key, 2), number_of)]


def gaussian(rng, dims, scale, most, cuts=(), held_as=jnp.bfloat16):
    result = scale * jax.random.normal(rng, dims, jnp.float32)
    if cuts:
        result = result * block_scale(rng, dims, cuts, -0.22, 0.18)
    return jnp.clip(result, -most, most).astype(held_as)


def setup_inputs(seed: int = 0) -> dict:
    seeds = jax.random.split(jax.random.key(seed), 6)
    hidden_states = gaussian(seeds[0], (VIDEOS, SEQ, D), 1.0, 6.0, ((0, 4), (1, 8)))
    modulation = gaussian(seeds[1], (VIDEOS, 3, D), 1.0, 4.0, ((0, 4),), jnp.float32)
    w_qkv = draw_w_qkv(jax.random.fold_in(seeds[5], 71), 0)
    w_out = gaussian(seeds[3], (D, D), D ** -0.5, 0.15625, ((0, 4), (1, 4)))
    lengths = uneven(seeds[4], VIDEOS, VIDEOS * SEQ * 5 // 8, SEQ, 2).astype(jnp.int32)
    return dict(hidden_states=hidden_states, modulation=modulation, w_qkv=w_qkv, w_out=w_out, lengths=lengths)


EPSILON = 1e-06
FLOOR = -1e+30

def modulated_norm(states, shift, scale):
    values = states.astype(jnp.float32)
    center = lax.optimization_barrier(jnp.mean(values, axis=-1, keepdims=True))
    spread = lax.optimization_barrier(jnp.mean(jnp.square(values - center), axis=-1, keepdims=True))
    return ((values - center) * lax.rsqrt(spread + EPSILON) * (1.0 + scale) + shift).astype(jnp.bfloat16)

def reference(hidden_states, modulation, w_qkv, w_out, lengths):
    shift = modulation[:, 0][:, None, :]
    scale = modulation[:, 1][:, None, :]
    gate = modulation[:, 2][:, None, :]
    normed = modulated_norm(hidden_states, shift, scale)
    mixed = jnp.dot(normed.reshape(VIDEOS * SEQ, D), w_qkv.reshape(D, 3 * D), preferred_element_type=jnp.float32)
    mixed = mixed.astype(jnp.bfloat16).reshape(VIDEOS, SEQ, 3, HEADS, HD)
    block_rows = math.gcd(SEQ, 512)

    def one_video(items):
        queries, keys, values, limit = items
        valid = jnp.arange(SEQ, dtype=jnp.int32) < limit
        valid_f = valid.astype(jnp.float32)[None, None, :]
        key_f = keys.astype(jnp.float32)
        value_f = values.astype(jnp.float32)

        def one_block(block_queries):
            scores = jnp.einsum('qhd,khd->hqk', block_queries.astype(jnp.float32), key_f) * HD ** (-0.5)
            scores = jnp.where(valid[None, None, :], scores, FLOOR)
            peak = lax.optimization_barrier(jnp.max(scores, axis=-1, keepdims=True))
            probs = jnp.exp(scores - peak) * valid_f
            weight_sum = lax.optimization_barrier(jnp.sum(probs, axis=-1))
            rounded = lax.optimization_barrier(probs.astype(jnp.bfloat16))
            numer = jnp.einsum('hqk,khd->qhd', rounded.astype(jnp.float32), value_f)
            return (numer / jnp.transpose(weight_sum)[:, :, None]).astype(jnp.bfloat16)
        blocks = lax.map(one_block, queries.reshape(SEQ // block_rows, block_rows, HEADS, HD))
        return blocks.reshape(SEQ, D)
    attended = lax.map(one_video, (mixed[:, :, 0], mixed[:, :, 1], mixed[:, :, 2], lengths))
    out_proj = jnp.dot(attended.reshape(VIDEOS * SEQ, D), w_out, preferred_element_type=jnp.float32)
    out_proj = out_proj.reshape(VIDEOS, SEQ, D)
    return (hidden_states.astype(jnp.float32) + gate * out_proj).astype(jnp.bfloat16)
```

```python
import functools
import math

import jax
import jax.numpy as jnp
from jax import lax
from jax.experimental import pallas as pl
from jax.experimental.pallas import tpu as pltpu
from jax.sharding import PartitionSpec as P

HD = 128


EPSILON = 1e-06
FLOOR = -1e30


def modulated_norm(states, shift, scale):
    values = states.astype(jnp.float32)
    center = jnp.mean(values, axis=-1, keepdims=True)
    spread = jnp.mean(jnp.square(values - center), axis=-1, keepdims=True)
    return ((values - center) * lax.rsqrt(spread + EPSILON) * (1.0 + scale) + shift).astype(
        jnp.bfloat16
    )


def absorb(carry, keys, values, first, queries, limits):
    peak, weight_sum, numer = carry
    videos_here = keys.shape[0]
    count = keys.shape[1]
    heads_here = queries.shape[2]
    head_size = queries.shape[3]
    key_heads = keys.reshape(videos_here, count, heads_here, head_size)
    value_heads = values.reshape(videos_here, count, heads_here, head_size)
    scores = jnp.einsum(
        "vqhd,vkhd->vhqk", queries, key_heads, preferred_element_type=jnp.float32
    ) * head_size ** (-0.5)
    position = first + jnp.arange(count, dtype=jnp.int32)
    valid = (position[None, :] < limits[:, None])[:, None, None, :]
    scores = jnp.where(valid, scores, FLOOR)
    new_peak = jnp.maximum(peak, jnp.max(scores, axis=-1))
    factor = jnp.exp(peak - new_peak)
    probs = jnp.exp(scores - new_peak[..., None]) * valid.astype(jnp.float32)
    weight_sum = weight_sum * factor + jnp.sum(probs, axis=-1)
    numer = numer * factor[..., None] + jnp.einsum(
        "vhqk,vkhd->vhqd",
        probs.astype(jnp.bfloat16),
        value_heads,
        preferred_element_type=jnp.float32,
    )
    return (new_peak, weight_sum, numer)


def general_body(hidden_states, modulation, w_qkv, w_out, lengths):
    videos_here = hidden_states.shape[0]
    width = hidden_states.shape[2]
    shift = modulation[:, 0][:, None, :]
    scale = modulation[:, 1][:, None, :]
    gate = modulation[:, 2][:, None, :]
    normed = modulated_norm(hidden_states, shift, scale)
    tile_rows = lax.all_gather(normed, "wcol", axis=1, tiled=True)
    tile_len = tile_rows.shape[1]
    local_cols = w_qkv.shape[2]
    flat_rows = tile_rows.reshape(videos_here * tile_len, width)
    piece = lax.all_gather(w_qkv, "wrow", axis=0, tiled=True)
    mixed = jnp.dot(
        flat_rows, piece.reshape(piece.shape[0], 3 * local_cols), preferred_element_type=jnp.float32
    )
    mixed = mixed.reshape(videos_here, tile_len, 3 * local_cols)
    mixed = mixed.astype(jnp.bfloat16).reshape(videos_here, tile_len, 3, local_cols)
    heads_here = local_cols // HD
    queries = mixed[:, :, 0].reshape(videos_here, tile_len, heads_here, HD)
    keys = mixed[:, :, 1]
    values = mixed[:, :, 2]
    start_peak = jnp.full((videos_here, heads_here, tile_len), FLOOR, jnp.float32)
    start_sum = jnp.zeros((videos_here, heads_here, tile_len), jnp.float32)
    start_numer = jnp.zeros((videos_here, heads_here, tile_len, HD), jnp.float32)
    key_piece = lax.all_gather(keys, "patch", axis=1, tiled=True)
    value_piece = lax.all_gather(values, "patch", axis=1, tiled=True)
    count = key_piece.shape[1]
    block_len = 512

    def one_block(index, inner):
        offset = index * block_len
        key_block = lax.dynamic_slice_in_dim(key_piece, offset, block_len, 1)
        value_block = lax.dynamic_slice_in_dim(value_piece, offset, block_len, 1)
        return absorb(inner, key_block, value_block, offset, queries, lengths)

    peak, weight_sum, numer = lax.fori_loop(
        0, count // block_len, one_block, (start_peak, start_sum, start_numer)
    )
    attended = (numer / weight_sum[..., None]).astype(jnp.bfloat16)
    attended = jnp.transpose(attended, (0, 2, 1, 3)).reshape(videos_here * tile_len, local_cols)
    partial_out = jnp.dot(
        attended,
        lax.all_gather(w_out, "wrow", axis=1, tiled=True),
        preferred_element_type=jnp.float32,
    )
    partial_out = partial_out.reshape(videos_here, tile_len, width)
    out_proj = lax.psum_scatter(
        partial_out.astype(jnp.bfloat16), "wcol", scatter_dimension=1, tiled=True
    ).astype(jnp.float32)
    return (hidden_states.astype(jnp.float32) + gate * out_proj).astype(jnp.bfloat16)


SHIFTS = ((0, 0, 0), (0, 1, 0), (1, 0, 0), (1, 1, 0), (0, 0, 1), (0, 1, 1), (1, 0, 1), (1, 1, 1))
VMEM_LIMIT = 40 * 1024 * 1024


def norm_kernel(states_ref, mod_ref, out_ref):
    values = states_ref[...].astype(jnp.float32)
    center = jnp.mean(values, axis=-1, keepdims=True)
    spread = jnp.mean(jnp.square(values - center), axis=-1, keepdims=True)
    shift = mod_ref[0:1, :]
    scale = mod_ref[1:2, :]
    out_ref[...] = (
        (values - center) * lax.rsqrt(spread + EPSILON) * (1.0 + scale) + shift
    ).astype(jnp.bfloat16)


def attend_kernel(spot_ref, len_ref, *refs):
    tiles = refs[0:8]
    first = refs[8:12]
    second = refs[12:16]
    own_ref, other_ref = refs[16:18]
    rows_ref, weight_ref, mixed_ref, value_ref, tile_sem, weight_sem = refs[18:]
    tile_len = tiles[0].shape[0]
    count = 8 * tile_len
    depth = first[0].shape[1]
    x, y, z, core = spot_ref[0], spot_ref[1], spot_ref[2], spot_ref[3]
    owner = x == core

    def tile_copy(i):
        return pltpu.make_async_copy(
            tiles[i], rows_ref.at[pl.ds(i * tile_len, tile_len)], tile_sem.at[i]
        )

    def weight_copy(shards, d, kind, column):
        start = pl.multiple_of((z ^ d) * depth, depth)
        return pltpu.make_async_copy(
            shards[d].at[kind],
            weight_ref.at[pl.ds(start, depth), pl.ds(column, HD)],
            weight_sem.at[column // HD, d],
        )

    copies = [tile_copy(i) for i in range(8)]
    copies += [weight_copy(first, d, k, k * HD) for d in range(4) for k in range(3)]
    extra = [weight_copy(second, d, k, (3 + k) * HD) for d in range(4) for k in range(3)]
    for copy in copies:
        copy.start()

    @pl.when(owner)
    def _():
        for copy in extra:
            copy.start()

    limit = len_ref[0]
    lane = lax.broadcasted_iota(jnp.int32, (1, tile_len), 1)
    bias = []
    for dx, dy, dc in SHIFTS:
        base = ((x ^ dx) * 4 + (y ^ dy) * 2 + (core ^ dc)) * tile_len
        bias.append(jnp.where(base + lane < limit, 0.0, FLOOR))
    bias = jnp.concatenate(bias, axis=1)
    value_ref[:, HD:] = jnp.ones((count, HD), jnp.bfloat16)
    for copy in copies:
        copy.wait()

    step = 2 * tile_len
    rate = HD ** (-0.5) * math.log2(math.e)

    def one_head(column):
        for r in range(count // step):
            span = pl.ds(r * step, step)
            mixed_ref[span, :] = jnp.dot(
                rows_ref[span, :],
                weight_ref[:, column : column + 3 * HD],
                preferred_element_type=jnp.float32,
            ).astype(jnp.bfloat16)
        value_ref[:, :HD] = mixed_ref[:, 2 * HD :]
        keys = mixed_ref[:, HD : 2 * HD]
        for r in range(count // step):
            scores = lax.dot_general(
                mixed_ref[pl.ds(r * step, step), :HD],
                keys,
                (((1,), (1,)), ((), ())),
                preferred_element_type=jnp.float32,
            )
            scores = scores + bias
            peak = jnp.max(scores, axis=-1, keepdims=True)
            probs = jnp.exp2((scores - peak) * rate).astype(jnp.bfloat16)
            sums = jnp.dot(probs, value_ref[...], preferred_element_type=jnp.float32)
            result = (sums[:, :HD] / sums[:, HD:]).astype(jnp.bfloat16)
            half = count // step // 2
            out = own_ref if r < half else other_ref
            at = column // 3
            out[pl.ds((r % half) * step, step), at : at + HD] = result

    one_head(0)

    @pl.when(owner)
    def _():
        for copy in extra:
            copy.wait()
        one_head(3 * HD)

    @pl.when(jnp.logical_not(owner))
    def _():
        own_ref[:, HD:] = jnp.zeros((count // 2, HD), jnp.bfloat16)
        other_ref[:, HD:] = jnp.zeros((count // 2, HD), jnp.bfloat16)


def project_kernel(spot_ref, own_ref, recv_ref, *refs):
    here = refs[0:4]
    sent = refs[4:8]
    outs = refs[8:12]
    weight_ref, joined_ref, sem = refs[12:]
    tile_len = outs[0].shape[0]
    width = here[0].shape[1]
    z = spot_ref[2]
    owner = spot_ref[0] == spot_ref[3]

    def weight_copy(shards, d):
        start = pl.multiple_of((z ^ d) * width, width)
        return pltpu.make_async_copy(shards[d], weight_ref.at[:, pl.ds(start, width)], sem.at[d])

    @pl.when(owner)
    def _():
        for d in range(4):
            weight_copy(here, d).start()
        joined_ref[:, 0:HD] = own_ref[:, :HD]
        joined_ref[:, HD : 2 * HD] = recv_ref[:, :HD]
        joined_ref[:, 2 * HD :] = own_ref[:, HD:]

    @pl.when(jnp.logical_not(owner))
    def _():
        for d in range(4):
            weight_copy(sent, d).start()
        joined_ref[:, 0:HD] = recv_ref[:, :HD]
        joined_ref[:, HD : 2 * HD] = own_ref[:, :HD]
        joined_ref[:, 2 * HD :] = recv_ref[:, HD:]

    for d in range(4):
        weight_copy(here, d).wait()
    for i, out in enumerate(outs):
        out[...] = jnp.dot(
            joined_ref[pl.ds(i * tile_len, tile_len), :],
            weight_ref[...],
            preferred_element_type=jnp.float32,
        ).astype(out.dtype)


def tiled_body(hidden_states, modulation, w_qkv, w_out, lengths):
    tile_len, width = hidden_states.shape[1:]
    depth, _, local_cols = w_qkv.shape
    states = hidden_states[0]
    x = lax.axis_index("patch")
    z = lax.axis_index("wrow")
    w = lax.axis_index("wcol")
    core = w % 2
    owner = x == core
    spot = jnp.stack([x, w // 2, z, core]).astype(jnp.int32)
    everywhere = ("patch", "wrow", "wcol")

    def index(a, b, c):
        return (a * 4 + b) * 4 + c

    def swap(array, axis, d, n):
        return lax.ppermute(array, axis, [(i, i ^ d) for i in range(n)])

    def owners_swap(array, d):
        pairs = [
            (index(a, b, c), index(a, b ^ d, c))
            for a in range(2)
            for b in range(4)
            for c in range(4)
            if c % 2 == a
        ]
        return lax.ppermute(array, everywhere, pairs)

    def to_other_core(array):
        pairs = [
            (index(a, b, c), index(a, b, c ^ 1))
            for a in range(2)
            for b in range(4)
            for c in range(4)
            if c % 2 == a
        ]
        return lax.ppermute(array, everywhere, pairs)

    kinds = jnp.transpose(w_qkv, (1, 0, 2))
    head_a, head_b, head_c = (kinds[:, :, i * HD : (i + 1) * HD] for i in range(3))
    second = [head_c, None, owners_swap(head_c, 2), None]
    mine = jnp.where(owner, head_a, to_other_core(head_b))
    first = [mine, None, swap(mine, "wrow", 2, 4), None]
    second[1] = owners_swap(head_c, 1)
    first[1] = swap(mine, "wrow", 1, 4)
    second[3] = owners_swap(second[2], 1)
    first[3] = swap(first[2], "wrow", 1, 4)

    full = pl.BlockSpec(memory_space=pltpu.VMEM)
    scalar = pl.BlockSpec(memory_space=pltpu.SMEM)
    anywhere = pl.BlockSpec(memory_space=pl.ANY)
    normed = pl.pallas_call(
        norm_kernel,
        out_shape=jax.ShapeDtypeStruct((tile_len, width), jnp.bfloat16),
        in_specs=[full, full],
        out_specs=full,
        name="norm",
    )(states, modulation[0])
    along_x = swap(normed, "patch", 1, 2)
    along_y = swap(normed, "wcol", 2, 4)
    along_xy = swap(along_x, "wcol", 2, 4)
    tiles = [normed, along_y, along_x, along_xy]
    tiles = tiles + [swap(tile, "wcol", 1, 4) for tile in tiles]

    count = 8 * tile_len
    half = jax.ShapeDtypeStruct((count // 2, 2 * HD), jnp.bfloat16)
    att_own, att_other = pl.pallas_call(
        attend_kernel,
        out_shape=(half, half),
        in_specs=[scalar, scalar] + [anywhere] * 16,
        out_specs=(full, full),
        scratch_shapes=[
            pltpu.VMEM((count, width), jnp.bfloat16),
            pltpu.VMEM((width, 6 * HD), jnp.bfloat16),
            pltpu.VMEM((count, 3 * HD), jnp.bfloat16),
            pltpu.VMEM((count, 2 * HD), jnp.bfloat16),
            pltpu.SemaphoreType.DMA((8,)),
            pltpu.SemaphoreType.DMA((6, 4)),
        ],
        compiler_params=pltpu.CompilerParams(vmem_limit_bytes=VMEM_LIMIT),
        name="attend",
    )(spot, lengths, *tiles, *first, *second)

    out_here = [w_out, owners_swap(w_out, 1), owners_swap(w_out, 2), None]
    out_here[3] = owners_swap(out_here[2], 1)
    out_sent = [to_other_core(shard) for shard in out_here]
    att_recv = swap(att_other, "wcol", 1, 4)
    sent = jax.ShapeDtypeStruct((tile_len, width), jnp.bfloat16)
    part_own, part_y, part_x, part_xy = pl.pallas_call(
        project_kernel,
        out_shape=(jax.ShapeDtypeStruct((tile_len, width), jnp.float32), sent, sent, sent),
        in_specs=[scalar, full, full] + [anywhere] * 8,
        out_specs=(full,) * 4,
        scratch_shapes=[
            pltpu.VMEM((local_cols, width), jnp.bfloat16),
            pltpu.VMEM((count // 2, local_cols), jnp.bfloat16),
            pltpu.SemaphoreType.DMA((4,)),
        ],
        compiler_params=pltpu.CompilerParams(vmem_limit_bytes=VMEM_LIMIT),
        name="project",
    )(spot, att_own, att_recv, *out_here, *out_sent)
    diagonal = [
        (a * 4 + c, (a ^ 1) * 4 + (c ^ 2)) for a in range(2) for c in range(4)
    ]
    got_xy = lax.ppermute(part_xy, ("patch", "wcol"), diagonal)
    got_x = swap(part_x, "patch", 1, 2)
    got_y = swap(part_y, "wcol", 2, 4)
    out_proj = (
        part_own
        + got_x.astype(jnp.float32)
        + got_y.astype(jnp.float32)
        + got_xy.astype(jnp.float32)
    )
    updated = states.astype(jnp.float32) + modulation[0, 2][None, :] * out_proj
    return updated.astype(jnp.bfloat16)[None]


def body(hidden_states, modulation, w_qkv, w_out, lengths, *, sizes):
    fits = sizes == (2, 4, 4) and hidden_states.shape[0] == 1 and w_qkv.shape[2] == 3 * HD
    if fits and hidden_states.shape[1] % HD == 0:
        return tiled_body(hidden_states, modulation, w_qkv, w_out, lengths)
    return general_body(hidden_states, modulation, w_qkv, w_out, lengths)


def solution(mesh):
    placed = (
        P("wrow", ("patch", "wcol"), None),
        P("wrow", None, None),
        P("wrow", None, "wcol"),
        P("wcol", "wrow"),
        P("wrow"),
    )
    sizes = tuple(mesh.shape[name] for name in ("patch", "wrow", "wcol"))
    return jax.shard_map(
        functools.partial(body, sizes=sizes),
        mesh=mesh,
        in_specs=placed,
        out_specs=P("wrow", ("patch", "wcol"), None),
        check_vma=False,
    )
```

```python
import functools
import math

import jax
import jax.numpy as jnp
from jax import lax
from jax.experimental import pallas as pl
from jax.experimental.pallas import tpu as pltpu
from jax.sharding import PartitionSpec as P

HD = 128


EPSILON = 1e-06
FLOOR = -1e30


def modulated_norm(states, shift, scale):
    values = states.astype(jnp.float32)
    center = jnp.mean(values, axis=-1, keepdims=True)
    spread = jnp.mean(jnp.square(values - center), axis=-1, keepdims=True)
    return ((values - center) * lax.rsqrt(spread + EPSILON) * (1.0 + scale) + shift).astype(
        jnp.bfloat16
    )


def absorb(carry, keys, values, first, queries, limits):
    peak, weight_sum, numer = carry
    videos_here = keys.shape[0]
    count = keys.shape[1]
    heads_here = queries.shape[2]
    head_size = queries.shape[3]
    key_heads = keys.reshape(videos_here, count, heads_here, head_size)
    value_heads = values.reshape(videos_here, count, heads_here, head_size)
    scores = jnp.einsum(
        "vqhd,vkhd->vhqk", queries, key_heads, preferred_element_type=jnp.float32
    ) * head_size ** (-0.5)
    position = first + jnp.arange(count, dtype=jnp.int32)
    valid = (position[None, :] < limits[:, None])[:, None, None, :]
    scores = jnp.where(valid, scores, FLOOR)
    new_peak = jnp.maximum(peak, jnp.max(scores, axis=-1))
    factor = jnp.exp(peak - new_peak)
    probs = jnp.exp(scores - new_peak[..., None]) * valid.astype(jnp.float32)
    weight_sum = weight_sum * factor + jnp.sum(probs, axis=-1)
    numer = numer * factor[..., None] + jnp.einsum(
        "vhqk,vkhd->vhqd",
        probs.astype(jnp.bfloat16),
        value_heads,
        preferred_element_type=jnp.float32,
    )
    return (new_peak, weight_sum, numer)


def general_body(hidden_states, modulation, w_qkv, w_out, lengths):
    videos_here = hidden_states.shape[0]
    width = hidden_states.shape[2]
    shift = modulation[:, 0][:, None, :]
    scale = modulation[:, 1][:, None, :]
    gate = modulation[:, 2][:, None, :]
    normed = modulated_norm(hidden_states, shift, scale)
    tile_rows = lax.all_gather(normed, "wcol", axis=1, tiled=True)
    tile_len = tile_rows.shape[1]
    local_cols = w_qkv.shape[2]
    flat_rows = tile_rows.reshape(videos_here * tile_len, width)
    piece = lax.all_gather(w_qkv, "wrow", axis=0, tiled=True)
    mixed = jnp.dot(
        flat_rows, piece.reshape(piece.shape[0], 3 * local_cols), preferred_element_type=jnp.float32
    )
    mixed = mixed.reshape(videos_here, tile_len, 3 * local_cols)
    mixed = mixed.astype(jnp.bfloat16).reshape(videos_here, tile_len, 3, local_cols)
    heads_here = local_cols // HD
    queries = mixed[:, :, 0].reshape(videos_here, tile_len, heads_here, HD)
    keys = mixed[:, :, 1]
    values = mixed[:, :, 2]
    start_peak = jnp.full((videos_here, heads_here, tile_len), FLOOR, jnp.float32)
    start_sum = jnp.zeros((videos_here, heads_here, tile_len), jnp.float32)
    start_numer = jnp.zeros((videos_here, heads_here, tile_len, HD), jnp.float32)
    key_piece = lax.all_gather(keys, "patch", axis=1, tiled=True)
    value_piece = lax.all_gather(values, "patch", axis=1, tiled=True)
    count = key_piece.shape[1]
    block_len = 512

    def one_block(index, inner):
        offset = index * block_len
        key_block = lax.dynamic_slice_in_dim(key_piece, offset, block_len, 1)
        value_block = lax.dynamic_slice_in_dim(value_piece, offset, block_len, 1)
        return absorb(inner, key_block, value_block, offset, queries, lengths)

    peak, weight_sum, numer = lax.fori_loop(
        0, count // block_len, one_block, (start_peak, start_sum, start_numer)
    )
    attended = (numer / weight_sum[..., None]).astype(jnp.bfloat16)
    attended = jnp.transpose(attended, (0, 2, 1, 3)).reshape(videos_here * tile_len, local_cols)
    partial_out = jnp.dot(
        attended,
        lax.all_gather(w_out, "wrow", axis=1, tiled=True),
        preferred_element_type=jnp.float32,
    )
    partial_out = partial_out.reshape(videos_here, tile_len, width)
    out_proj = lax.psum_scatter(
        partial_out.astype(jnp.bfloat16), "wcol", scatter_dimension=1, tiled=True
    ).astype(jnp.float32)
    return (hidden_states.astype(jnp.float32) + gate * out_proj).astype(jnp.bfloat16)


SHIFTS = ((0, 0, 0), (0, 1, 0), (1, 0, 0), (1, 1, 0), (0, 0, 1), (0, 1, 1), (1, 0, 1), (1, 1, 1))
VMEM_LIMIT = 16 * 1024 * 1024


def norm_kernel(states_ref, mod_ref, out_ref):
    values = states_ref[...].astype(jnp.float32)
    center = jnp.mean(values, axis=-1, keepdims=True)
    spread = jnp.mean(jnp.square(values - center), axis=-1, keepdims=True)
    shift = mod_ref[0]
    scale = mod_ref[1]
    out_ref[...] = (
        (values - center) * lax.rsqrt(spread + EPSILON) * (1.0 + scale) + shift
    ).astype(jnp.bfloat16)


def start_shard(spot_ref, here, sent, start, weight_ref, sem):
    depth, width = here.shape[1:]
    owner = spot_ref[0] == spot_ref[3]
    for role, shard in ((owner, here), (jnp.logical_not(owner), sent)):

        @pl.when(role)
        def _():
            for k in range(3):
                pltpu.make_async_copy(
                    shard.at[k],
                    weight_ref.at[pl.ds(start, depth), pl.ds(k * width, width)],
                    sem.at[k],
                ).start()


def wait_shard(here, start, weight_ref, sem):
    depth, width = here.shape[1:]
    for k in range(3):
        pltpu.make_async_copy(
            here.at[k],
            weight_ref.at[pl.ds(start, depth), pl.ds(k * width, width)],
            sem.at[k],
        ).wait()


def early_kernel(spot_ref, *refs):
    tiles = refs[0:4]
    here = refs[4:7]
    sent = refs[7:10]
    total_ref, last_ref = refs[10:12]
    rows_ref, weight_ref, tile_sem, weight_sem = refs[12:]
    tile_len = tiles[0].shape[0]
    depth = here[0].shape[1]
    count = 4 * tile_len
    z = spot_ref[2]
    columns = [pl.multiple_of((z ^ d) * depth, HD) for d in range(4)]
    sources = [tiles[i].at[:, pl.ds(columns[d], depth)] for d in range(4) for i in range(4)]
    places = [
        rows_ref.at[pl.ds(i * tile_len, tile_len), pl.ds(d * depth, depth)]
        for d in range(3)
        for i in range(4)
    ]
    places += [last_ref.at[pl.ds(i * tile_len, tile_len)] for i in range(4)]
    copies = [
        pltpu.make_async_copy(source, place, tile_sem.at[n])
        for n, (source, place) in enumerate(zip(sources, places))
    ]
    for d in range(3):
        start_shard(spot_ref, here[d], sent[d], d * depth, weight_ref, weight_sem.at[d])
    for copy in copies:
        copy.start()
    for d in range(3):
        wait_shard(here[d], d * depth, weight_ref, weight_sem.at[d])
    for copy in copies:
        copy.wait()
    step = 2 * tile_len
    skip = weight_ref.shape[1] - total_ref.shape[1]
    for r in range(count // step):
        span = pl.ds(r * step, step)
        total_ref[span, :] = jnp.dot(
            rows_ref[span, :], weight_ref[:, skip:], preferred_element_type=jnp.float32
        )


def attend_kernel(spot_ref, len_ref, *refs):
    totals, lasts, here, sent = refs[0:2], refs[2:4], refs[4:8], refs[8:12]
    out_refs = refs[12:16]
    weight_ref, out_weight_ref, query_ref, key_ref, value_ref, weight_sem, out_sem = refs[16:]
    count = key_ref.shape[0]
    width = query_ref.shape[1]
    tile_len = out_refs[0].shape[0]
    x, y, z, core = (spot_ref[i] for i in range(4))
    start_shard(spot_ref, here[3], sent[3], 0, weight_ref, weight_sem)
    owner = x == core
    places = [
        out_weight_ref.at[:, pl.ds(pl.multiple_of((z ^ d) * width, HD), width)] for d in range(4)
    ]
    for role, shards in ((owner, here), (jnp.logical_not(owner), sent)):

        @pl.when(role)
        def _():
            for d in range(4):
                pltpu.make_async_copy(shards[d].at[3], places[d], out_sem.at[d]).start()

    limit = len_ref[0]
    lane = lax.broadcasted_iota(jnp.int32, (1, tile_len), 1)
    bias = []
    for dx, dy, dc in SHIFTS:
        base = ((x ^ dx) * 4 + (y ^ dy) * 2 + (core ^ dc)) * tile_len
        bias.append(jnp.where(base + lane < limit, 0.0, FLOOR))
    bias = jnp.concatenate(bias, axis=1)
    for h in range(width // HD):
        value_ref[h, :, HD:] = jnp.ones((count, HD), jnp.bfloat16)
    wait_shard(here[3], 0, weight_ref, weight_sem)
    step = 2 * tile_len
    rate = HD ** (-0.5) * math.log2(math.e)
    half = count // step // 2
    for r in range(count // step):
        span = pl.ds((r % half) * step, step)
        rows = pl.ds(r * step, step)
        skip = 0 if r < half else width
        mixed = (
            totals[r // half][span, :]
            + jnp.dot(
                lasts[r // half][span, :],
                weight_ref[:, skip:],
                preferred_element_type=jnp.float32,
            )
        ).astype(jnp.bfloat16)
        if r < half:
            query_ref[rows, :] = mixed[:, :width]
        key_ref[rows, :] = mixed[:, width - skip : 2 * width - skip]
        for h in range(width // HD):
            at = 2 * width - skip + h * HD
            value_ref[h, rows, :HD] = mixed[:, at : at + HD]
    for d in range(4):
        pltpu.make_async_copy(here[d].at[3], places[d], out_sem.at[d]).wait()
    for r in range(half):
        heads = []
        for h in range(width // HD):
            column = slice(h * HD, (h + 1) * HD)
            scores = lax.dot_general(
                query_ref[pl.ds(r * step, step), column],
                key_ref[:, column],
                (((1,), (1,)), ((), ())),
                preferred_element_type=jnp.float32,
            )
            scores = scores + bias
            peak = jnp.max(scores, axis=-1, keepdims=True)
            probs = jnp.exp2((scores - peak) * rate).astype(jnp.bfloat16)
            sums = jnp.dot(probs, value_ref[h], preferred_element_type=jnp.float32)
            heads.append((sums[:, :HD] / sums[:, HD:]).astype(jnp.bfloat16))
        part = jnp.dot(
            jnp.concatenate(heads, axis=1),
            out_weight_ref[...],
            preferred_element_type=jnp.float32,
        )
        for i in range(2):
            out = out_refs[2 * r + i]
            out[...] = part[i * tile_len : (i + 1) * tile_len].astype(out.dtype)


def tiled_body(hidden_states, modulation, w_qkv, w_out, lengths):
    tile_len, width = hidden_states.shape[1:]
    depth, _, local_cols = w_qkv.shape
    states = hidden_states[0]
    x = lax.axis_index("patch")
    z = lax.axis_index("wrow")
    w = lax.axis_index("wcol")
    core = w % 2
    owner = x == core
    spot = jnp.stack([x, w // 2, z, core]).astype(jnp.int32)
    everywhere = ("patch", "wrow", "wcol")

    def index(a, b, c):
        return (a * 4 + b) * 4 + c

    def swap(array, axis, d, n):
        return lax.ppermute(array, axis, [(i, i ^ d) for i in range(n)])

    def owners_swap(array, d):
        pairs = [
            (index(a, b, c), index(a, b ^ d, c))
            for a in range(2)
            for b in range(4)
            for c in range(4)
            if c % 2 == a
        ]
        return lax.ppermute(array, everywhere, pairs)

    def core_swap(array):
        return swap(array, "wcol", 1, 4)

    full = pl.BlockSpec(memory_space=pltpu.VMEM)
    scalar = pl.BlockSpec(memory_space=pltpu.SMEM)
    anywhere = pl.BlockSpec(memory_space=pl.ANY)
    params = pltpu.CompilerParams(vmem_limit_bytes=VMEM_LIMIT)
    count = 8 * tile_len

    mod = jnp.transpose(modulation, (1, 0, 2))
    normed = pl.pallas_call(
        norm_kernel,
        out_shape=jax.ShapeDtypeStruct((tile_len, width), jnp.bfloat16),
        in_specs=[full, full],
        out_specs=full,
        name="norm",
    )(states, mod)
    kinds = jnp.transpose(w_qkv, (1, 0, 2))

    four = jnp.concatenate([kinds, w_out[None]], axis=0)
    far = owners_swap(four, 2)
    near = owners_swap(four, 1)
    along_x = swap(normed, "patch", 1, 2)
    along_y = swap(normed, "wcol", 2, 4)
    along_xy = swap(along_y, "patch", 1, 2)
    far, near, along_x, along_y, along_xy, normed, four = lax.optimization_barrier(
        (far, near, along_x, along_y, along_xy, normed, four)
    )
    last = owners_swap(far, 1)
    tiles = [normed, along_y, along_x, along_xy]
    tiles_sent = [core_swap(tile) for tile in tiles]
    early_here = [four, near, far]
    early_sent = [core_swap(shard) for shard in early_here]

    def early(rows, columns):
        return pl.pallas_call(
            early_kernel,
            out_shape=(
                jax.ShapeDtypeStruct((count // 2, columns), jnp.float32),
                jax.ShapeDtypeStruct((count // 2, depth), jnp.bfloat16),
            ),
            in_specs=[scalar] + [anywhere] * 10,
            out_specs=(full, full),
            scratch_shapes=[
                pltpu.VMEM((count // 2, 3 * depth), jnp.bfloat16),
                pltpu.VMEM((3 * depth, 3 * local_cols), jnp.bfloat16),
                pltpu.SemaphoreType.DMA((16,)),
                pltpu.SemaphoreType.DMA((3, 3)),
            ],
            compiler_params=params,
            name="early",
        )(spot, *rows, *early_here, *early_sent)

    total_a, rows_a = early(tiles, 3 * local_cols)
    total_b, rows_b = early(tiles_sent, 2 * local_cols)
    last, total_a, total_b = lax.optimization_barrier((last, total_a, total_b))
    last_sent = core_swap(last)

    sent = jax.ShapeDtypeStruct((tile_len, width), jnp.bfloat16)
    part_own, part_y, part_x, part_xy = pl.pallas_call(
        attend_kernel,
        out_shape=(jax.ShapeDtypeStruct((tile_len, width), jnp.float32), sent, sent, sent),
        in_specs=[scalar, scalar] + [full] * 4 + [anywhere] * 8,
        out_specs=(full,) * 4,
        scratch_shapes=[
            pltpu.VMEM((depth, 3 * local_cols), jnp.bfloat16),
            pltpu.VMEM((local_cols, width), jnp.bfloat16),
            pltpu.VMEM((count // 2, local_cols), jnp.bfloat16),
            pltpu.VMEM((count, local_cols), jnp.bfloat16),
            pltpu.VMEM((local_cols // HD, count, 2 * HD), jnp.bfloat16),
            pltpu.SemaphoreType.DMA((3,)),
            pltpu.SemaphoreType.DMA((4,)),
        ],
        compiler_params=params,
        name="attend",
    )(spot, lengths, total_a, total_b, rows_a, rows_b, *early_here, last, *early_sent, last_sent)
    diagonal = [(a * 4 + c, (a ^ 1) * 4 + (c ^ 2)) for a in range(2) for c in range(4)]
    got_xy = lax.ppermute(part_xy, ("patch", "wcol"), diagonal)
    got_x = swap(part_x, "patch", 1, 2)
    got_y = swap(part_y, "wcol", 2, 4)
    out_proj = (
        part_own
        + got_x.astype(jnp.float32)
        + got_y.astype(jnp.float32)
        + got_xy.astype(jnp.float32)
    )
    updated = states.astype(jnp.float32) + mod[2] * out_proj
    return updated.astype(jnp.bfloat16)[None]


def body(hidden_states, modulation, w_qkv, w_out, lengths, *, sizes):
    fits = sizes == (2, 4, 4) and hidden_states.shape[0] == 1 and w_qkv.shape[2] == 3 * HD
    if fits and hidden_states.shape[1] % HD == 0:
        return tiled_body(hidden_states, modulation, w_qkv, w_out, lengths)
    return general_body(hidden_states, modulation, w_qkv, w_out, lengths)


def solution(mesh):
    placed = (
        P("wrow", ("patch", "wcol"), None),
        P("wrow", None, None),
        P("wrow", None, "wcol"),
        P("wcol", "wrow"),
        P("wrow"),
    )
    sizes = tuple(mesh.shape[name] for name in ("patch", "wrow", "wcol"))
    return jax.shard_map(
        functools.partial(body, sizes=sizes),
        mesh=mesh,
        in_specs=placed,
        out_specs=P("wrow", ("patch", "wcol"), None),
        check_vma=False,
    )
```

```python
import functools
import math

import jax
import jax.numpy as jnp
from jax import lax
from jax.experimental import pallas as pl
from jax.experimental.pallas import tpu as pltpu
from jax.sharding import PartitionSpec as P

HD = 128


EPSILON = 1e-06
FLOOR = -1e30


def modulated_norm(states, shift, scale):
    values = states.astype(jnp.float32)
    center = jnp.mean(values, axis=-1, keepdims=True)
    spread = jnp.mean(jnp.square(values - center), axis=-1, keepdims=True)
    return ((values - center) * lax.rsqrt(spread + EPSILON) * (1.0 + scale) + shift).astype(
        jnp.bfloat16
    )


def absorb(carry, keys, values, first, queries, limits):
    peak, weight_sum, numer = carry
    videos_here = keys.shape[0]
    count = keys.shape[1]
    heads_here = queries.shape[2]
    head_size = queries.shape[3]
    key_heads = keys.reshape(videos_here, count, heads_here, head_size)
    value_heads = values.reshape(videos_here, count, heads_here, head_size)
    scores = jnp.einsum(
        "vqhd,vkhd->vhqk", queries, key_heads, preferred_element_type=jnp.float32
    ) * head_size ** (-0.5)
    position = first + jnp.arange(count, dtype=jnp.int32)
    valid = (position[None, :] < limits[:, None])[:, None, None, :]
    scores = jnp.where(valid, scores, FLOOR)
    new_peak = jnp.maximum(peak, jnp.max(scores, axis=-1))
    factor = jnp.exp(peak - new_peak)
    probs = jnp.exp(scores - new_peak[..., None]) * valid.astype(jnp.float32)
    weight_sum = weight_sum * factor + jnp.sum(probs, axis=-1)
    numer = numer * factor[..., None] + jnp.einsum(
        "vhqk,vkhd->vhqd",
        probs.astype(jnp.bfloat16),
        value_heads,
        preferred_element_type=jnp.float32,
    )
    return (new_peak, weight_sum, numer)


def general_body(hidden_states, modulation, w_qkv, w_out, lengths):
    videos_here = hidden_states.shape[0]
    width = hidden_states.shape[2]
    shift = modulation[:, 0][:, None, :]
    scale = modulation[:, 1][:, None, :]
    gate = modulation[:, 2][:, None, :]
    normed = modulated_norm(hidden_states, shift, scale)
    tile_rows = lax.all_gather(normed, "wcol", axis=1, tiled=True)
    tile_len = tile_rows.shape[1]
    local_cols = w_qkv.shape[2]
    flat_rows = tile_rows.reshape(videos_here * tile_len, width)
    piece = lax.all_gather(w_qkv, "wrow", axis=0, tiled=True)
    mixed = jnp.dot(
        flat_rows, piece.reshape(piece.shape[0], 3 * local_cols), preferred_element_type=jnp.float32
    )
    mixed = mixed.reshape(videos_here, tile_len, 3 * local_cols)
    mixed = mixed.astype(jnp.bfloat16).reshape(videos_here, tile_len, 3, local_cols)
    heads_here = local_cols // HD
    queries = mixed[:, :, 0].reshape(videos_here, tile_len, heads_here, HD)
    keys = mixed[:, :, 1]
    values = mixed[:, :, 2]
    start_peak = jnp.full((videos_here, heads_here, tile_len), FLOOR, jnp.float32)
    start_sum = jnp.zeros((videos_here, heads_here, tile_len), jnp.float32)
    start_numer = jnp.zeros((videos_here, heads_here, tile_len, HD), jnp.float32)
    key_piece = lax.all_gather(keys, "patch", axis=1, tiled=True)
    value_piece = lax.all_gather(values, "patch", axis=1, tiled=True)
    count = key_piece.shape[1]
    block_len = 512

    def one_block(index, inner):
        offset = index * block_len
        key_block = lax.dynamic_slice_in_dim(key_piece, offset, block_len, 1)
        value_block = lax.dynamic_slice_in_dim(value_piece, offset, block_len, 1)
        return absorb(inner, key_block, value_block, offset, queries, lengths)

    peak, weight_sum, numer = lax.fori_loop(
        0, count // block_len, one_block, (start_peak, start_sum, start_numer)
    )
    attended = (numer / weight_sum[..., None]).astype(jnp.bfloat16)
    attended = jnp.transpose(attended, (0, 2, 1, 3)).reshape(videos_here * tile_len, local_cols)
    partial_out = jnp.dot(
        attended,
        lax.all_gather(w_out, "wrow", axis=1, tiled=True),
        preferred_element_type=jnp.float32,
    )
    partial_out = partial_out.reshape(videos_here, tile_len, width)
    out_proj = lax.psum_scatter(
        partial_out.astype(jnp.bfloat16), "wcol", scatter_dimension=1, tiled=True
    ).astype(jnp.float32)
    return (hidden_states.astype(jnp.float32) + gate * out_proj).astype(jnp.bfloat16)


SHIFTS = ((0, 0, 0), (0, 1, 0), (1, 0, 0), (1, 1, 0), (0, 0, 1), (0, 1, 1), (1, 0, 1), (1, 1, 1))
VMEM_LIMIT = 18 * 1024 * 1024


def start_shard(spot_ref, here, sent, start, weight_ref, sem):
    depth, width = here.shape[1:]
    owner = spot_ref[0] == spot_ref[3]
    for role, shard in ((owner, here), (jnp.logical_not(owner), sent)):

        @pl.when(role)
        def _():
            for k in range(3):
                pltpu.make_async_copy(
                    shard.at[k],
                    weight_ref.at[pl.ds(start, depth), pl.ds(k * width, width)],
                    sem.at[k],
                ).start()


def wait_shard(here, start, weight_ref, sem):
    depth, width = here.shape[1:]
    for k in range(3):
        pltpu.make_async_copy(
            here.at[k],
            weight_ref.at[pl.ds(start, depth), pl.ds(k * width, width)],
            sem.at[k],
        ).wait()


def norm_kernel(spot_ref, mod_ref, *refs):
    tiles, out_ref, tile_ref = refs[0:4], refs[4], refs[5]
    tile_len, width = tiles[0].shape
    depth = width // 4
    shift = mod_ref[0]
    scale = 1.0 + mod_ref[1]
    for i in range(4):
        rows = pl.ds(i * tile_len, tile_len)
        values = tiles[i][...].astype(jnp.float32)
        center = jnp.mean(values, axis=-1, keepdims=True)
        values = values - center
        spread = jnp.mean(jnp.square(values), axis=-1, keepdims=True)
        tile_ref[...] = (values * lax.rsqrt(spread + EPSILON) * scale + shift).astype(jnp.bfloat16)
        for d in range(4):
            start = pl.multiple_of((spot_ref[2] ^ d) * depth, HD)
            out_ref[rows, d * depth : (d + 1) * depth] = tile_ref[:, pl.ds(start, depth)]


def start_out_weights(spot_ref, here, sent, place, sem):
    owner = spot_ref[0] == spot_ref[3]
    for role, shard in ((owner, here), (jnp.logical_not(owner), sent)):

        @pl.when(role)
        def _():
            pltpu.make_async_copy(shard.at[3], place, sem).start()


def early_kernel(spot_ref, own_rows_ref, other_rows_ref, *refs):
    here, sent = refs[0:3], refs[3:6]
    own_ref, other_ref, out_weight_ref, weight_ref, weight_sem, out_sem = refs[6:]
    depth = here[0].shape[1]
    for d in range(3):
        start_shard(spot_ref, here[d], sent[d], d * depth, weight_ref, weight_sem.at[d])
    for d in range(3):
        start_out_weights(spot_ref, here[d], sent[d], out_weight_ref.at[d], out_sem.at[d])
    for d in range(3):
        wait_shard(here[d], d * depth, weight_ref, weight_sem.at[d])
    step = own_ref.shape[0] // 2
    skip = weight_ref.shape[1] - other_ref.shape[1]
    for r in range(2):
        span = pl.ds(r * step, step)
        own_ref[span, :] = jnp.dot(
            own_rows_ref[span, : 3 * depth], weight_ref[...], preferred_element_type=jnp.float32
        )
    for r in range(2):
        span = pl.ds(r * step, step)
        other_ref[span, :] = jnp.dot(
            other_rows_ref[span, : 3 * depth],
            weight_ref[:, skip:],
            preferred_element_type=jnp.float32,
        )
    for d in range(3):
        pltpu.make_async_copy(here[d].at[3], out_weight_ref.at[d], out_sem.at[d]).wait()


def attend_kernel(spot_ref, len_ref, *refs):
    totals, rows_refs, (out_known_ref, here, sent) = refs[0:2], refs[2:4], refs[4:7]
    out_refs = refs[7:11]
    weight_ref, out_weight_ref, query_ref, key_ref, value_ref, weight_sem, out_sem = refs[11:]
    count = key_ref.shape[0]
    width = query_ref.shape[1]
    depth = weight_ref.shape[0]
    tile_len = out_refs[0].shape[0]
    x, y, z, core = (spot_ref[i] for i in range(4))
    start_shard(spot_ref, here, sent, 0, weight_ref, weight_sem)
    places = [
        out_weight_ref.at[:, pl.ds(pl.multiple_of((z ^ d) * width, HD), width)] for d in range(4)
    ]
    start_out_weights(spot_ref, here, sent, places[3], out_sem.at[3])
    known = [
        pltpu.make_async_copy(out_known_ref.at[d], places[d], out_sem.at[d]) for d in range(3)
    ]
    for copy in known:
        copy.start()
    limit = len_ref[0]
    lane = lax.broadcasted_iota(jnp.int32, (1, tile_len), 1)
    bias = []
    for dx, dy, dc in SHIFTS:
        base = ((x ^ dx) * 4 + (y ^ dy) * 2 + (core ^ dc)) * tile_len
        bias.append(jnp.where(base + lane < limit, 0.0, FLOOR))
    bias = jnp.concatenate(bias, axis=1)
    for h in range(width // HD):
        value_ref[h, :, HD:] = jnp.ones((count, HD), jnp.bfloat16)
    wait_shard(here, 0, weight_ref, weight_sem)
    step = 2 * tile_len
    rate = HD ** (-0.5) * math.log2(math.e)
    half = count // step // 2
    for r in range(count // step):
        span = pl.ds((r % half) * step, step)
        rows = pl.ds(r * step, step)
        skip = 0 if r < half else width
        mixed = (
            totals[r // half][span, :]
            + jnp.dot(
                rows_refs[r // half][span, 3 * depth :],
                weight_ref[:, skip:],
                preferred_element_type=jnp.float32,
            )
        ).astype(jnp.bfloat16)
        if r < half:
            query_ref[rows, :] = mixed[:, :width]
        key_ref[rows, :] = mixed[:, width - skip : 2 * width - skip]
        for h in range(width // HD):
            at = 2 * width - skip + h * HD
            value_ref[h, rows, :HD] = mixed[:, at : at + HD]
    for copy in known:
        copy.wait()
    pltpu.make_async_copy(here.at[3], places[3], out_sem.at[3]).wait()
    for r in range(half):
        heads = []
        for h in range(width // HD):
            column = slice(h * HD, (h + 1) * HD)
            scores = lax.dot_general(
                query_ref[pl.ds(r * step, step), column],
                key_ref[:, column],
                (((1,), (1,)), ((), ())),
                preferred_element_type=jnp.float32,
            )
            scores = scores + bias
            peak = jnp.max(scores, axis=-1, keepdims=True)
            probs = jnp.exp2((scores - peak) * rate).astype(jnp.bfloat16)
            sums = jnp.dot(probs, value_ref[h], preferred_element_type=jnp.float32)
            heads.append((sums[:, :HD] / sums[:, HD:]).astype(jnp.bfloat16))
        part = jnp.dot(
            jnp.concatenate(heads, axis=1),
            out_weight_ref[...],
            preferred_element_type=jnp.float32,
        )
        for i in range(2):
            out = out_refs[2 * r + i]
            out[...] = part[i * tile_len : (i + 1) * tile_len].astype(out.dtype)


def tiled_body(hidden_states, modulation, w_qkv, w_out, lengths):
    tile_len, width = hidden_states.shape[1:]
    depth, _, local_cols = w_qkv.shape
    states = hidden_states[0]
    x = lax.axis_index("patch")
    z = lax.axis_index("wrow")
    w = lax.axis_index("wcol")
    core = w % 2
    owner = x == core
    spot = jnp.stack([x, w // 2, z, core]).astype(jnp.int32)
    everywhere = ("patch", "wrow", "wcol")

    def index(a, b, c):
        return (a * 4 + b) * 4 + c

    def swap(array, axis, d, n):
        return lax.ppermute(array, axis, [(i, i ^ d) for i in range(n)])

    def owners_swap(array, d):
        pairs = [
            (index(a, b, c), index(a, b ^ d, c))
            for a in range(2)
            for b in range(4)
            for c in range(4)
            if c % 2 == a
        ]
        return lax.ppermute(array, everywhere, pairs)

    def core_swap(array):
        return swap(array, "wcol", 1, 4)

    full = pl.BlockSpec(memory_space=pltpu.VMEM)
    scalar = pl.BlockSpec(memory_space=pltpu.SMEM)
    anywhere = pl.BlockSpec(memory_space=pl.ANY)
    params = pltpu.CompilerParams(vmem_limit_bytes=VMEM_LIMIT)
    count = 8 * tile_len

    mod = jnp.transpose(modulation, (1, 0, 2))
    kinds = jnp.transpose(w_qkv, (1, 0, 2))

    four = jnp.concatenate([kinds, w_out[None]], axis=0)
    far = owners_swap(four, 2)
    near = owners_swap(four, 1)
    along_x = swap(states, "patch", 1, 2)
    along_y = swap(states, "wcol", 2, 4)
    diagonal = [(a * 4 + c, (a ^ 1) * 4 + (c ^ 2)) for a in range(2) for c in range(4)]
    along_xy = lax.ppermute(states, ("patch", "wcol"), diagonal)
    tiles = [states, along_y, along_x, along_xy]
    own_rows = pl.pallas_call(
        norm_kernel,
        out_shape=jax.ShapeDtypeStruct((count // 2, width), jnp.bfloat16),
        in_specs=[scalar] + [full] * 5,
        out_specs=full,
        scratch_shapes=[pltpu.VMEM((tile_len, width), jnp.bfloat16)],
        compiler_params=params,
        name="norm",
    )(spot, mod, *tiles)
    other_rows = core_swap(own_rows)

    last = owners_swap(far, 1)
    shards = [four, near, far]
    total_own, total_other, out_known = pl.pallas_call(
        early_kernel,
        out_shape=(
            jax.ShapeDtypeStruct((count // 2, 3 * local_cols), jnp.float32),
            jax.ShapeDtypeStruct((count // 2, 2 * local_cols), jnp.float32),
            jax.ShapeDtypeStruct((3,) + w_out.shape, jnp.bfloat16),
        ),
        in_specs=[scalar] + [full] * 2 + [anywhere] * 6,
        out_specs=(full,) * 3,
        scratch_shapes=[
            pltpu.VMEM((3 * depth, 3 * local_cols), jnp.bfloat16),
            pltpu.SemaphoreType.DMA((3, 3)),
            pltpu.SemaphoreType.DMA((3,)),
        ],
        compiler_params=params,
        name="early",
    )(spot, own_rows, other_rows, *shards, *(core_swap(shard) for shard in shards))
    last, total_own = lax.optimization_barrier((last, total_own))
    last_sent = core_swap(last)

    sent = jax.ShapeDtypeStruct((tile_len, width), jnp.bfloat16)
    part_own, part_y, part_x, part_xy = pl.pallas_call(
        attend_kernel,
        out_shape=(jax.ShapeDtypeStruct((tile_len, width), jnp.float32), sent, sent, sent),
        in_specs=[scalar, scalar] + [full] * 5 + [anywhere] * 2,
        out_specs=(full,) * 4,
        scratch_shapes=[
            pltpu.VMEM((depth, 3 * local_cols), jnp.bfloat16),
            pltpu.VMEM((local_cols, width), jnp.bfloat16),
            pltpu.VMEM((count // 2, local_cols), jnp.bfloat16),
            pltpu.VMEM((count, local_cols), jnp.bfloat16),
            pltpu.VMEM((local_cols // HD, count, 2 * HD), jnp.bfloat16),
            pltpu.SemaphoreType.DMA((3,)),
            pltpu.SemaphoreType.DMA((4,)),
        ],
        compiler_params=params,
        name="attend",
    )(spot, lengths, total_own, total_other, own_rows, other_rows, out_known, last, last_sent)
    got_xy = lax.ppermute(part_xy, ("patch", "wcol"), diagonal)
    got_x = swap(part_x, "patch", 1, 2)
    got_y = swap(part_y, "wcol", 2, 4)
    out_proj = (
        part_own
        + got_x.astype(jnp.float32)
        + got_y.astype(jnp.float32)
        + got_xy.astype(jnp.float32)
    )
    updated = states.astype(jnp.float32) + mod[2] * out_proj
    return updated.astype(jnp.bfloat16)[None]


def body(hidden_states, modulation, w_qkv, w_out, lengths, *, sizes):
    fits = sizes == (2, 4, 4) and hidden_states.shape[0] == 1 and w_qkv.shape[2] == 3 * HD
    if fits and hidden_states.shape[1] % HD == 0:
        return tiled_body(hidden_states, modulation, w_qkv, w_out, lengths)
    return general_body(hidden_states, modulation, w_qkv, w_out, lengths)


def solution(mesh):
    placed = (
        P("wrow", ("patch", "wcol"), None),
        P("wrow", None, None),
        P("wrow", None, "wcol"),
        P("wcol", "wrow"),
        P("wrow"),
    )
    sizes = tuple(mesh.shape[name] for name in ("patch", "wrow", "wcol"))
    return jax.shard_map(
        functools.partial(body, sizes=sizes),
        mesh=mesh,
        in_specs=placed,
        out_specs=P("wrow", ("patch", "wcol"), None),
        check_vma=False,
    )
```

```python
import functools
import math

import jax
import jax.numpy as jnp
from jax import lax
from jax.experimental import pallas as pl
from jax.experimental.pallas import tpu as pltpu
from jax.sharding import PartitionSpec as P

HD = 128


EPSILON = 1e-06
FLOOR = -1e30


def modulated_norm(states, shift, scale):
    values = states.astype(jnp.float32)
    center = jnp.mean(values, axis=-1, keepdims=True)
    spread = jnp.mean(jnp.square(values - center), axis=-1, keepdims=True)
    return ((values - center) * lax.rsqrt(spread + EPSILON) * (1.0 + scale) + shift).astype(
        jnp.bfloat16
    )


def absorb(carry, keys, values, first, queries, limits):
    peak, weight_sum, numer = carry
    videos_here = keys.shape[0]
    count = keys.shape[1]
    heads_here = queries.shape[2]
    head_size = queries.shape[3]
    key_heads = keys.reshape(videos_here, count, heads_here, head_size)
    value_heads = values.reshape(videos_here, count, heads_here, head_size)
    scores = jnp.einsum(
        "vqhd,vkhd->vhqk", queries, key_heads, preferred_element_type=jnp.float32
    ) * head_size ** (-0.5)
    position = first + jnp.arange(count, dtype=jnp.int32)
    valid = (position[None, :] < limits[:, None])[:, None, None, :]
    scores = jnp.where(valid, scores, FLOOR)
    new_peak = jnp.maximum(peak, jnp.max(scores, axis=-1))
    factor = jnp.exp(peak - new_peak)
    probs = jnp.exp(scores - new_peak[..., None]) * valid.astype(jnp.float32)
    weight_sum = weight_sum * factor + jnp.sum(probs, axis=-1)
    numer = numer * factor[..., None] + jnp.einsum(
        "vhqk,vkhd->vhqd",
        probs.astype(jnp.bfloat16),
        value_heads,
        preferred_element_type=jnp.float32,
    )
    return (new_peak, weight_sum, numer)


def general_body(hidden_states, modulation, w_qkv, w_out, lengths):
    videos_here = hidden_states.shape[0]
    width = hidden_states.shape[2]
    shift = modulation[:, 0][:, None, :]
    scale = modulation[:, 1][:, None, :]
    gate = modulation[:, 2][:, None, :]
    normed = modulated_norm(hidden_states, shift, scale)
    tile_rows = lax.all_gather(normed, "wcol", axis=1, tiled=True)
    tile_len = tile_rows.shape[1]
    local_cols = w_qkv.shape[2]
    flat_rows = tile_rows.reshape(videos_here * tile_len, width)
    piece = lax.all_gather(w_qkv, "wrow", axis=0, tiled=True)
    mixed = jnp.dot(
        flat_rows, piece.reshape(piece.shape[0], 3 * local_cols), preferred_element_type=jnp.float32
    )
    mixed = mixed.reshape(videos_here, tile_len, 3 * local_cols)
    mixed = mixed.astype(jnp.bfloat16).reshape(videos_here, tile_len, 3, local_cols)
    heads_here = local_cols // HD
    queries = mixed[:, :, 0].reshape(videos_here, tile_len, heads_here, HD)
    keys = mixed[:, :, 1]
    values = mixed[:, :, 2]
    start_peak = jnp.full((videos_here, heads_here, tile_len), FLOOR, jnp.float32)
    start_sum = jnp.zeros((videos_here, heads_here, tile_len), jnp.float32)
    start_numer = jnp.zeros((videos_here, heads_here, tile_len, HD), jnp.float32)
    key_piece = lax.all_gather(keys, "patch", axis=1, tiled=True)
    value_piece = lax.all_gather(values, "patch", axis=1, tiled=True)
    count = key_piece.shape[1]
    block_len = 512

    def one_block(index, inner):
        offset = index * block_len
        key_block = lax.dynamic_slice_in_dim(key_piece, offset, block_len, 1)
        value_block = lax.dynamic_slice_in_dim(value_piece, offset, block_len, 1)
        return absorb(inner, key_block, value_block, offset, queries, lengths)

    peak, weight_sum, numer = lax.fori_loop(
        0, count // block_len, one_block, (start_peak, start_sum, start_numer)
    )
    attended = (numer / weight_sum[..., None]).astype(jnp.bfloat16)
    attended = jnp.transpose(attended, (0, 2, 1, 3)).reshape(videos_here * tile_len, local_cols)
    partial_out = jnp.dot(
        attended,
        lax.all_gather(w_out, "wrow", axis=1, tiled=True),
        preferred_element_type=jnp.float32,
    )
    partial_out = partial_out.reshape(videos_here, tile_len, width)
    out_proj = lax.psum_scatter(
        partial_out.astype(jnp.bfloat16), "wcol", scatter_dimension=1, tiled=True
    ).astype(jnp.float32)
    return (hidden_states.astype(jnp.float32) + gate * out_proj).astype(jnp.bfloat16)


SHIFTS = ((0, 1, 0), (1, 0, 0), (0, 0, 0), (1, 1, 0), (0, 1, 1), (1, 0, 1), (0, 0, 1), (1, 1, 1))
VMEM_LIMIT = 18 * 1024 * 1024


def start_shard(spot_ref, here, sent, start, weight_ref, sem):
    depth, width = here.shape[1:]
    owner = spot_ref[0] == spot_ref[3]
    for role, shard in ((owner, here), (jnp.logical_not(owner), sent)):

        @pl.when(role)
        def _():
            for k in range(3):
                pltpu.make_async_copy(
                    shard.at[k],
                    weight_ref.at[pl.ds(start, depth), pl.ds(k * width, width)],
                    sem.at[k],
                ).start()


def wait_shard(here, start, weight_ref, sem):
    depth, width = here.shape[1:]
    for k in range(3):
        pltpu.make_async_copy(
            here.at[k],
            weight_ref.at[pl.ds(start, depth), pl.ds(k * width, width)],
            sem.at[k],
        ).wait()


def norm_kernel(spot_ref, mod_ref, *refs):
    tiles, out_ref, tile_ref = refs[0:4], refs[4], refs[5]
    tile_len, width = tiles[0].shape
    depth = width // 4
    shift = mod_ref[0]
    scale = 1.0 + mod_ref[1]
    for i in range(4):
        rows = pl.ds(i * tile_len, tile_len)
        values = tiles[i][...].astype(jnp.float32)
        center = jnp.mean(values, axis=-1, keepdims=True)
        values = values - center
        spread = jnp.mean(jnp.square(values), axis=-1, keepdims=True)
        tile_ref[...] = (values * lax.rsqrt(spread + EPSILON) * scale + shift).astype(jnp.bfloat16)
        for d in range(4):
            start = pl.multiple_of((spot_ref[2] ^ d) * depth, HD)
            out_ref[rows, d * depth : (d + 1) * depth] = tile_ref[:, pl.ds(start, depth)]


def start_out_weights(spot_ref, here, sent, place, sem):
    owner = spot_ref[0] == spot_ref[3]
    for role, shard in ((owner, here), (jnp.logical_not(owner), sent)):

        @pl.when(role)
        def _():
            pltpu.make_async_copy(shard.at[3], place, sem).start()


def early_kernel(spot_ref, own_rows_ref, other_rows_ref, *refs):
    here, sent = refs[0:3], refs[3:6]
    own_ref, other_ref, out_weight_ref, weight_ref, weight_sem, out_sem = refs[6:]
    depth = here[0].shape[1]
    for d in range(3):
        start_shard(spot_ref, here[d], sent[d], d * depth, weight_ref, weight_sem.at[d])
    for d in range(3):
        start_out_weights(spot_ref, here[d], sent[d], out_weight_ref.at[d], out_sem.at[d])
    for d in range(3):
        wait_shard(here[d], d * depth, weight_ref, weight_sem.at[d])
    step = own_ref.shape[0] // 2
    skip = weight_ref.shape[1] - other_ref.shape[1]
    for r in range(2):
        span = pl.ds(r * step, step)
        own_ref[span, :] = jnp.dot(
            own_rows_ref[span, : 3 * depth], weight_ref[...], preferred_element_type=jnp.float32
        )
    for r in range(2):
        span = pl.ds(r * step, step)
        other_ref[span, :] = jnp.dot(
            other_rows_ref[span, : 3 * depth],
            weight_ref[:, skip:],
            preferred_element_type=jnp.float32,
        )
    for d in range(3):
        pltpu.make_async_copy(here[d].at[3], out_weight_ref.at[d], out_sem.at[d]).wait()


def key_bias(spot_ref, len_ref, tile_len):
    x, y, core = spot_ref[0], spot_ref[1], spot_ref[3]
    lane = lax.broadcasted_iota(jnp.int32, (1, tile_len), 1)
    bias = []
    for dx, dy, dc in SHIFTS:
        base = ((x ^ dx) * 4 + (y ^ dy) * 2 + (core ^ dc)) * tile_len
        bias.append(jnp.where(base + lane < len_ref[0], 0.0, FLOOR))
    return jnp.concatenate(bias, axis=1)


def project(queries, key_ref, value_ref, out_weight_ref, bias, out_refs):
    rate = HD ** (-0.5) * math.log2(math.e)
    heads = []
    for h in range(queries.shape[1] // HD):
        column = slice(h * HD, (h + 1) * HD)
        scores = lax.dot_general(
            queries[:, column],
            key_ref[:, column],
            (((1,), (1,)), ((), ())),
            preferred_element_type=jnp.float32,
        )
        scores = scores + bias
        peak = jnp.max(scores, axis=-1, keepdims=True)
        probs = jnp.exp2((scores - peak) * rate).astype(jnp.bfloat16)
        sums = jnp.dot(probs, value_ref[h], preferred_element_type=jnp.float32)
        heads.append((sums[:, :HD] / sums[:, HD:]).astype(jnp.bfloat16))
    part = jnp.dot(
        jnp.concatenate(heads, axis=1), out_weight_ref[...], preferred_element_type=jnp.float32
    )
    tile_len = out_refs[0].shape[0]
    for i, out in enumerate(out_refs):
        out[...] = part[i * tile_len : (i + 1) * tile_len].astype(out.dtype)


def attend_kernel(spot_ref, len_ref, *refs):
    totals, rows_refs, (out_known_ref, here, sent) = refs[0:2], refs[2:4], refs[4:7]
    out_refs, (query_ref, key_ref, value_ref, out_weight_ref) = refs[7:9], refs[9:13]
    weight_ref, weight_sem, out_sem = refs[13:]
    count, width = key_ref.shape
    depth = weight_ref.shape[0]
    z = spot_ref[2]
    start_shard(spot_ref, here, sent, 0, weight_ref, weight_sem)
    places = [
        out_weight_ref.at[:, pl.ds(pl.multiple_of((z ^ d) * width, HD), width)] for d in range(4)
    ]
    start_out_weights(spot_ref, here, sent, places[3], out_sem.at[3])
    known = [
        pltpu.make_async_copy(out_known_ref.at[d], places[d], out_sem.at[d]) for d in range(3)
    ]
    for copy in known:
        copy.start()
    bias = key_bias(spot_ref, len_ref, count // 8)
    for h in range(width // HD):
        value_ref[h, :, HD:] = jnp.ones((count, HD), jnp.bfloat16)
    wait_shard(here, 0, weight_ref, weight_sem)
    step = count // 4
    queries = None
    for r in range(4):
        span = pl.ds((r % 2) * step, step)
        rows = pl.ds(r * step, step)
        skip = 0 if r < 2 else width
        mixed = (
            totals[r // 2][span, :]
            + jnp.dot(
                rows_refs[r // 2][span, 3 * depth :],
                weight_ref[:, skip:],
                preferred_element_type=jnp.float32,
            )
        ).astype(jnp.bfloat16)
        if r == 0:
            queries = mixed[:, :width]
        elif r == 1:
            query_ref[...] = mixed[:, :width]
        key_ref[rows, :] = mixed[:, width - skip : 2 * width - skip]
        for h in range(width // HD):
            at = 2 * width - skip + h * HD
            value_ref[h, rows, :HD] = mixed[:, at : at + HD]
    for copy in known:
        copy.wait()
    pltpu.make_async_copy(here.at[3], places[3], out_sem.at[3]).wait()
    project(queries, key_ref, value_ref, out_weight_ref, bias, out_refs)


def attend_rest_kernel(spot_ref, len_ref, query_ref, key_ref, value_ref, out_weight_ref, *out_refs):
    bias = key_bias(spot_ref, len_ref, key_ref.shape[0] // 8)
    project(query_ref[...], key_ref, value_ref, out_weight_ref, bias, out_refs)


def tiled_body(hidden_states, modulation, w_qkv, w_out, lengths):
    tile_len, width = hidden_states.shape[1:]
    depth, _, local_cols = w_qkv.shape
    states = hidden_states[0]
    x = lax.axis_index("patch")
    z = lax.axis_index("wrow")
    w = lax.axis_index("wcol")
    core = w % 2
    owner = x == core
    spot = jnp.stack([x, w // 2, z, core]).astype(jnp.int32)
    everywhere = ("patch", "wrow", "wcol")

    def index(a, b, c):
        return (a * 4 + b) * 4 + c

    def swap(array, axis, d, n):
        return lax.ppermute(array, axis, [(i, i ^ d) for i in range(n)])

    def owners_swap(array, d):
        pairs = [
            (index(a, b, c), index(a, b ^ d, c))
            for a in range(2)
            for b in range(4)
            for c in range(4)
            if c % 2 == a
        ]
        return lax.ppermute(array, everywhere, pairs)

    def core_swap(array):
        return swap(array, "wcol", 1, 4)

    full = pl.BlockSpec(memory_space=pltpu.VMEM)
    scalar = pl.BlockSpec(memory_space=pltpu.SMEM)
    anywhere = pl.BlockSpec(memory_space=pl.ANY)
    params = pltpu.CompilerParams(vmem_limit_bytes=VMEM_LIMIT)
    count = 8 * tile_len

    mod = jnp.transpose(modulation, (1, 0, 2))
    kinds = jnp.transpose(w_qkv, (1, 0, 2))

    four = jnp.concatenate([kinds, w_out[None]], axis=0)
    far = owners_swap(four, 2)
    near = owners_swap(four, 1)
    along_x = swap(states, "patch", 1, 2)
    along_y = swap(states, "wcol", 2, 4)
    diagonal = [(a * 4 + c, (a ^ 1) * 4 + (c ^ 2)) for a in range(2) for c in range(4)]
    along_xy = lax.ppermute(states, ("patch", "wcol"), diagonal)
    tiles = [along_y, along_x, states, along_xy]
    own_rows = pl.pallas_call(
        norm_kernel,
        out_shape=jax.ShapeDtypeStruct((count // 2, width), jnp.bfloat16),
        in_specs=[scalar] + [full] * 5,
        out_specs=full,
        scratch_shapes=[pltpu.VMEM((tile_len, width), jnp.bfloat16)],
        compiler_params=params,
        name="norm",
    )(spot, mod, *tiles)
    other_rows = core_swap(own_rows)

    last = owners_swap(far, 1)
    shards = [four, near, far]
    total_own, total_other, out_known = pl.pallas_call(
        early_kernel,
        out_shape=(
            jax.ShapeDtypeStruct((count // 2, 3 * local_cols), jnp.float32),
            jax.ShapeDtypeStruct((count // 2, 2 * local_cols), jnp.float32),
            jax.ShapeDtypeStruct((3,) + w_out.shape, jnp.bfloat16),
        ),
        in_specs=[scalar] + [full] * 2 + [anywhere] * 6,
        out_specs=(full,) * 3,
        scratch_shapes=[
            pltpu.VMEM((3 * depth, 3 * local_cols), jnp.bfloat16),
            pltpu.SemaphoreType.DMA((3, 3)),
            pltpu.SemaphoreType.DMA((3,)),
        ],
        compiler_params=params,
        name="early",
    )(spot, own_rows, other_rows, *shards, *(core_swap(shard) for shard in shards))
    last, total_own = lax.optimization_barrier((last, total_own))
    last_sent = core_swap(last)

    sent = jax.ShapeDtypeStruct((tile_len, width), jnp.bfloat16)
    part_y, part_x, *kept = pl.pallas_call(
        attend_kernel,
        out_shape=(
            sent,
            sent,
            jax.ShapeDtypeStruct((count // 4, local_cols), jnp.bfloat16),
            jax.ShapeDtypeStruct((count, local_cols), jnp.bfloat16),
            jax.ShapeDtypeStruct((local_cols // HD, count, 2 * HD), jnp.bfloat16),
            jax.ShapeDtypeStruct((local_cols, width), jnp.bfloat16),
        ),
        in_specs=[scalar, scalar] + [full] * 5 + [anywhere] * 2,
        out_specs=(full,) * 6,
        scratch_shapes=[
            pltpu.VMEM((depth, 3 * local_cols), jnp.bfloat16),
            pltpu.SemaphoreType.DMA((3,)),
            pltpu.SemaphoreType.DMA((4,)),
        ],
        compiler_params=params,
        name="attend",
    )(spot, lengths, total_own, total_other, own_rows, other_rows, out_known, last, last_sent)
    got_x = swap(part_x, "patch", 1, 2)
    got_y = swap(part_y, "wcol", 2, 4)
    part_own, part_xy = pl.pallas_call(
        attend_rest_kernel,
        out_shape=(jax.ShapeDtypeStruct((tile_len, width), jnp.float32), sent),
        in_specs=[scalar, scalar] + [full] * 4,
        out_specs=(full,) * 2,
        compiler_params=params,
        name="attend_rest",
    )(spot, lengths, *kept)
    got_xy = lax.ppermute(part_xy, ("patch", "wcol"), diagonal)
    near_sum = part_own + got_x.astype(jnp.float32) + got_y.astype(jnp.float32)
    near_sum, got_xy = lax.optimization_barrier((near_sum, got_xy))
    updated = states.astype(jnp.float32) + mod[2] * (near_sum + got_xy.astype(jnp.float32))
    return updated.astype(jnp.bfloat16)[None]


def body(hidden_states, modulation, w_qkv, w_out, lengths, *, sizes):
    fits = sizes == (2, 4, 4) and hidden_states.shape[0] == 1 and w_qkv.shape[2] == 3 * HD
    if fits and hidden_states.shape[1] % HD == 0:
        return tiled_body(hidden_states, modulation, w_qkv, w_out, lengths)
    return general_body(hidden_states, modulation, w_qkv, w_out, lengths)


def solution(mesh):
    placed = (
        P("wrow", ("patch", "wcol"), None),
        P("wrow", None, None),
        P("wrow", None, "wcol"),
        P("wcol", "wrow"),
        P("wrow"),
    )
    sizes = tuple(mesh.shape[name] for name in ("patch", "wrow", "wcol"))
    return jax.shard_map(
        functools.partial(body, sizes=sizes),
        mesh=mesh,
        in_specs=placed,
        out_specs=P("wrow", ("patch", "wcol"), None),
        check_vma=False,
    )
```

```python
import functools
import math

import jax
import jax.numpy as jnp
from jax import lax
from jax.experimental import pallas as pl
from jax.experimental.pallas import tpu as pltpu
from jax.sharding import PartitionSpec as P

HD = 128


EPSILON = 1e-06
FLOOR = -1e30


def modulated_norm(states, shift, scale):
    values = states.astype(jnp.float32)
    center = jnp.mean(values, axis=-1, keepdims=True)
    spread = jnp.mean(jnp.square(values - center), axis=-1, keepdims=True)
    return ((values - center) * lax.rsqrt(spread + EPSILON) * (1.0 + scale) + shift).astype(
        jnp.bfloat16
    )


def absorb(carry, keys, values, first, queries, limits):
    peak, weight_sum, numer = carry
    videos_here = keys.shape[0]
    count = keys.shape[1]
    heads_here = queries.shape[2]
    head_size = queries.shape[3]
    key_heads = keys.reshape(videos_here, count, heads_here, head_size)
    value_heads = values.reshape(videos_here, count, heads_here, head_size)
    scores = jnp.einsum(
        "vqhd,vkhd->vhqk", queries, key_heads, preferred_element_type=jnp.float32
    ) * head_size ** (-0.5)
    position = first + jnp.arange(count, dtype=jnp.int32)
    valid = (position[None, :] < limits[:, None])[:, None, None, :]
    scores = jnp.where(valid, scores, FLOOR)
    new_peak = jnp.maximum(peak, jnp.max(scores, axis=-1))
    factor = jnp.exp(peak - new_peak)
    probs = jnp.exp(scores - new_peak[..., None]) * valid.astype(jnp.float32)
    weight_sum = weight_sum * factor + jnp.sum(probs, axis=-1)
    numer = numer * factor[..., None] + jnp.einsum(
        "vhqk,vkhd->vhqd",
        probs.astype(jnp.bfloat16),
        value_heads,
        preferred_element_type=jnp.float32,
    )
    return (new_peak, weight_sum, numer)


def general_body(hidden_states, modulation, w_qkv, w_out, lengths):
    videos_here = hidden_states.shape[0]
    width = hidden_states.shape[2]
    shift = modulation[:, 0][:, None, :]
    scale = modulation[:, 1][:, None, :]
    gate = modulation[:, 2][:, None, :]
    normed = modulated_norm(hidden_states, shift, scale)
    tile_rows = lax.all_gather(normed, "wcol", axis=1, tiled=True)
    tile_len = tile_rows.shape[1]
    local_cols = w_qkv.shape[2]
    flat_rows = tile_rows.reshape(videos_here * tile_len, width)
    piece = lax.all_gather(w_qkv, "wrow", axis=0, tiled=True)
    mixed = jnp.dot(
        flat_rows, piece.reshape(piece.shape[0], 3 * local_cols), preferred_element_type=jnp.float32
    )
    mixed = mixed.reshape(videos_here, tile_len, 3 * local_cols)
    mixed = mixed.astype(jnp.bfloat16).reshape(videos_here, tile_len, 3, local_cols)
    heads_here = local_cols // HD
    queries = mixed[:, :, 0].reshape(videos_here, tile_len, heads_here, HD)
    keys = mixed[:, :, 1]
    values = mixed[:, :, 2]
    start_peak = jnp.full((videos_here, heads_here, tile_len), FLOOR, jnp.float32)
    start_sum = jnp.zeros((videos_here, heads_here, tile_len), jnp.float32)
    start_numer = jnp.zeros((videos_here, heads_here, tile_len, HD), jnp.float32)
    key_piece = lax.all_gather(keys, "patch", axis=1, tiled=True)
    value_piece = lax.all_gather(values, "patch", axis=1, tiled=True)
    count = key_piece.shape[1]
    block_len = 512

    def one_block(index, inner):
        offset = index * block_len
        key_block = lax.dynamic_slice_in_dim(key_piece, offset, block_len, 1)
        value_block = lax.dynamic_slice_in_dim(value_piece, offset, block_len, 1)
        return absorb(inner, key_block, value_block, offset, queries, lengths)

    peak, weight_sum, numer = lax.fori_loop(
        0, count // block_len, one_block, (start_peak, start_sum, start_numer)
    )
    attended = (numer / weight_sum[..., None]).astype(jnp.bfloat16)
    attended = jnp.transpose(attended, (0, 2, 1, 3)).reshape(videos_here * tile_len, local_cols)
    partial_out = jnp.dot(
        attended,
        lax.all_gather(w_out, "wrow", axis=1, tiled=True),
        preferred_element_type=jnp.float32,
    )
    partial_out = partial_out.reshape(videos_here, tile_len, width)
    out_proj = lax.psum_scatter(
        partial_out.astype(jnp.bfloat16), "wcol", scatter_dimension=1, tiled=True
    ).astype(jnp.float32)
    return (hidden_states.astype(jnp.float32) + gate * out_proj).astype(jnp.bfloat16)


SHIFTS = ((0, 0, 0), (1, 1, 0), (0, 1, 0), (1, 0, 0), (0, 0, 1), (1, 1, 1), (0, 1, 1), (1, 0, 1))
VMEM_LIMIT = 18 * 1024 * 1024


def start_shard(spot_ref, here, sent, start, weight_ref, sem):
    depth, width = here.shape[1:]
    owner = spot_ref[0] == spot_ref[3]
    for role, shard in ((owner, here), (jnp.logical_not(owner), sent)):

        @pl.when(role)
        def _():
            for k in range(3):
                pltpu.make_async_copy(
                    shard.at[k],
                    weight_ref.at[pl.ds(start, depth), pl.ds(k * width, width)],
                    sem.at[k],
                ).start()


def wait_shard(here, start, weight_ref, sem):
    depth, width = here.shape[1:]
    for k in range(3):
        pltpu.make_async_copy(
            here.at[k],
            weight_ref.at[pl.ds(start, depth), pl.ds(k * width, width)],
            sem.at[k],
        ).wait()


def norm_kernel(spot_ref, mod_ref, *refs):
    tiles, out_ref, tile_ref = refs[0:4], refs[4], refs[5]
    tile_len, width = tiles[0].shape
    depth = width // 4
    shift = mod_ref[0]
    scale = 1.0 + mod_ref[1]
    for i in range(4):
        rows = pl.ds(i * tile_len, tile_len)
        values = tiles[i][...].astype(jnp.float32)
        center = jnp.mean(values, axis=-1, keepdims=True)
        values = values - center
        spread = jnp.mean(jnp.square(values), axis=-1, keepdims=True)
        tile_ref[...] = (values * lax.rsqrt(spread + EPSILON) * scale + shift).astype(jnp.bfloat16)
        for d in range(4):
            start = pl.multiple_of((spot_ref[2] ^ d) * depth, HD)
            out_ref[rows, d * depth : (d + 1) * depth] = tile_ref[:, pl.ds(start, depth)]


def start_out_weights(spot_ref, here, sent, place, sem):
    owner = spot_ref[0] == spot_ref[3]
    for role, shard in ((owner, here), (jnp.logical_not(owner), sent)):

        @pl.when(role)
        def _():
            pltpu.make_async_copy(shard.at[3], place, sem).start()


def early_kernel(spot_ref, own_rows_ref, other_rows_ref, *refs):
    here, sent = refs[0:3], refs[3:6]
    own_ref, other_ref, out_weight_ref, weight_ref, weight_sem, out_sem = refs[6:]
    depth = here[0].shape[1]
    for d in range(3):
        start_shard(spot_ref, here[d], sent[d], d * depth, weight_ref, weight_sem.at[d])
    for d in range(3):
        start_out_weights(spot_ref, here[d], sent[d], out_weight_ref.at[d], out_sem.at[d])
    for d in range(3):
        wait_shard(here[d], d * depth, weight_ref, weight_sem.at[d])
    step = own_ref.shape[0] // 2
    skip = weight_ref.shape[1] - other_ref.shape[1]
    for r in range(2):
        span = pl.ds(r * step, step)
        own_ref[span, :] = jnp.dot(
            own_rows_ref[span, : 3 * depth], weight_ref[...], preferred_element_type=jnp.float32
        )
    for r in range(2):
        span = pl.ds(r * step, step)
        other_ref[span, :] = jnp.dot(
            other_rows_ref[span, : 3 * depth],
            weight_ref[:, skip:],
            preferred_element_type=jnp.float32,
        )
    for d in range(3):
        pltpu.make_async_copy(here[d].at[3], out_weight_ref.at[d], out_sem.at[d]).wait()


def key_bias(spot_ref, len_ref, tile_len):
    x, y, core = spot_ref[0], spot_ref[1], spot_ref[3]
    lane = lax.broadcasted_iota(jnp.int32, (1, tile_len), 1)
    bias = []
    for dx, dy, dc in SHIFTS:
        base = ((x ^ dx) * 4 + (y ^ dy) * 2 + (core ^ dc)) * tile_len
        bias.append(jnp.where(base + lane < len_ref[0], 0.0, FLOOR))
    return jnp.concatenate(bias, axis=1)


def project(queries, key_ref, value_ref, out_weight_ref, bias):
    rate = HD ** (-0.5) * math.log2(math.e)
    heads = []
    for h in range(queries.shape[1] // HD):
        column = slice(h * HD, (h + 1) * HD)
        scores = lax.dot_general(
            queries[:, column],
            key_ref[:, column],
            (((1,), (1,)), ((), ())),
            preferred_element_type=jnp.float32,
        )
        scores = scores + bias
        peak = jnp.max(scores, axis=-1, keepdims=True)
        probs = jnp.exp2((scores - peak) * rate).astype(jnp.bfloat16)
        sums = jnp.dot(probs, value_ref[h], preferred_element_type=jnp.float32)
        heads.append((sums[:, :HD] / sums[:, HD:]).astype(jnp.bfloat16))
    part = jnp.dot(
        jnp.concatenate(heads, axis=1), out_weight_ref[...], preferred_element_type=jnp.float32
    )
    return part[: part.shape[0] // 2], part[part.shape[0] // 2 :]


def attend_kernel(spot_ref, len_ref, *refs):
    totals, rows_refs, (out_known_ref, here, sent) = refs[0:2], refs[2:4], refs[4:7]
    own_ref, left_ref, right_ref, query_ref, key_ref, value_ref, out_weight_ref = refs[7:14]
    weight_ref, weight_sem, out_sem = refs[14:]
    count, width = key_ref.shape
    depth = weight_ref.shape[0]
    z = spot_ref[2]
    start_shard(spot_ref, here, sent, 0, weight_ref, weight_sem)
    places = [
        out_weight_ref.at[:, pl.ds(pl.multiple_of((z ^ d) * width, HD), width)] for d in range(4)
    ]
    start_out_weights(spot_ref, here, sent, places[3], out_sem.at[3])
    known = [
        pltpu.make_async_copy(out_known_ref.at[d], places[d], out_sem.at[d]) for d in range(3)
    ]
    for copy in known:
        copy.start()
    bias = key_bias(spot_ref, len_ref, count // 8)
    for h in range(width // HD):
        value_ref[h, :, HD:] = jnp.ones((count, HD), jnp.bfloat16)
    wait_shard(here, 0, weight_ref, weight_sem)
    step = count // 4
    queries = None
    for r in range(4):
        span = pl.ds((r % 2) * step, step)
        rows = pl.ds(r * step, step)
        skip = 0 if r < 2 else width
        mixed = (
            totals[r // 2][span, :]
            + jnp.dot(
                rows_refs[r // 2][span, 3 * depth :],
                weight_ref[:, skip:],
                preferred_element_type=jnp.float32,
            )
        ).astype(jnp.bfloat16)
        if r == 0:
            queries = mixed[:, :width]
        elif r == 1:
            query_ref[...] = mixed[:, :width]
        key_ref[rows, :] = mixed[:, width - skip : 2 * width - skip]
        for h in range(width // HD):
            at = 2 * width - skip + h * HD
            value_ref[h, rows, :HD] = mixed[:, at : at + HD]
    for copy in known:
        copy.wait()
    pltpu.make_async_copy(here.at[3], places[3], out_sem.at[3]).wait()
    own, diagonal = project(queries, key_ref, value_ref, out_weight_ref, bias)
    own_ref[...] = own
    middle = left_ref.shape[1]
    left_ref[...] = diagonal[:, :middle].astype(jnp.bfloat16)
    right_ref[...] = diagonal[:, middle:].astype(jnp.bfloat16)


def attend_rest_kernel(
    spot_ref, len_ref, query_ref, key_ref, value_ref, out_weight_ref, *out_refs
):
    y_left_ref, y_right_ref, x_left_ref, x_right_ref = out_refs
    bias = key_bias(spot_ref, len_ref, key_ref.shape[0] // 8)
    along_y, along_x = project(query_ref[...], key_ref, value_ref, out_weight_ref, bias)
    middle = y_left_ref.shape[1]
    y_left_ref[...] = along_y[:, :middle]
    y_right_ref[...] = along_y[:, middle:].astype(jnp.bfloat16)
    x_left_ref[...] = along_x[:, :middle].astype(jnp.bfloat16)
    x_right_ref[...] = along_x[:, middle:]


def tiled_body(hidden_states, modulation, w_qkv, w_out, lengths):
    tile_len, width = hidden_states.shape[1:]
    depth, _, local_cols = w_qkv.shape
    states = hidden_states[0]
    x = lax.axis_index("patch")
    z = lax.axis_index("wrow")
    w = lax.axis_index("wcol")
    core = w % 2
    owner = x == core
    spot = jnp.stack([x, w // 2, z, core]).astype(jnp.int32)
    everywhere = ("patch", "wrow", "wcol")

    def index(a, b, c):
        return (a * 4 + b) * 4 + c

    def swap(array, axis, d, n):
        return lax.ppermute(array, axis, [(i, i ^ d) for i in range(n)])

    def owners_swap(array, d):
        pairs = [
            (index(a, b, c), index(a, b ^ d, c))
            for a in range(2)
            for b in range(4)
            for c in range(4)
            if c % 2 == a
        ]
        return lax.ppermute(array, everywhere, pairs)

    def core_swap(array):
        return swap(array, "wcol", 1, 4)

    full = pl.BlockSpec(memory_space=pltpu.VMEM)
    scalar = pl.BlockSpec(memory_space=pltpu.SMEM)
    anywhere = pl.BlockSpec(memory_space=pl.ANY)
    params = pltpu.CompilerParams(vmem_limit_bytes=VMEM_LIMIT)
    count = 8 * tile_len

    mod = jnp.transpose(modulation, (1, 0, 2))
    kinds = jnp.transpose(w_qkv, (1, 0, 2))

    four = jnp.concatenate([kinds, w_out[None]], axis=0)
    far = owners_swap(four, 2)
    near = owners_swap(four, 1)
    along_x = swap(states, "patch", 1, 2)
    along_y = swap(states, "wcol", 2, 4)
    diagonal = [(a * 4 + c, (a ^ 1) * 4 + (c ^ 2)) for a in range(2) for c in range(4)]
    along_xy = lax.ppermute(states, ("patch", "wcol"), diagonal)
    tiles = [states, along_xy, along_y, along_x]
    own_rows = pl.pallas_call(
        norm_kernel,
        out_shape=jax.ShapeDtypeStruct((count // 2, width), jnp.bfloat16),
        in_specs=[scalar] + [full] * 5,
        out_specs=full,
        scratch_shapes=[pltpu.VMEM((tile_len, width), jnp.bfloat16)],
        compiler_params=params,
        name="norm",
    )(spot, mod, *tiles)
    other_rows = core_swap(own_rows)

    last = owners_swap(far, 1)
    shards = [four, near, far]
    total_own, total_other, out_known = pl.pallas_call(
        early_kernel,
        out_shape=(
            jax.ShapeDtypeStruct((count // 2, 3 * local_cols), jnp.float32),
            jax.ShapeDtypeStruct((count // 2, 2 * local_cols), jnp.float32),
            jax.ShapeDtypeStruct((3,) + w_out.shape, jnp.bfloat16),
        ),
        in_specs=[scalar] + [full] * 2 + [anywhere] * 6,
        out_specs=(full,) * 3,
        scratch_shapes=[
            pltpu.VMEM((3 * depth, 3 * local_cols), jnp.bfloat16),
            pltpu.SemaphoreType.DMA((3, 3)),
            pltpu.SemaphoreType.DMA((3,)),
        ],
        compiler_params=params,
        name="early",
    )(spot, own_rows, other_rows, *shards, *(core_swap(shard) for shard in shards))
    last, total_own = lax.optimization_barrier((last, total_own))
    last_sent = core_swap(last)

    half = jax.ShapeDtypeStruct((tile_len, width // 2), jnp.bfloat16)
    half_f32 = jax.ShapeDtypeStruct((tile_len, width // 2), jnp.float32)
    part_own, xy_left, xy_right, *kept = pl.pallas_call(
        attend_kernel,
        out_shape=(
            jax.ShapeDtypeStruct((tile_len, width), jnp.float32),
            half,
            half,
            jax.ShapeDtypeStruct((count // 4, local_cols), jnp.bfloat16),
            jax.ShapeDtypeStruct((count, local_cols), jnp.bfloat16),
            jax.ShapeDtypeStruct((local_cols // HD, count, 2 * HD), jnp.bfloat16),
            jax.ShapeDtypeStruct((local_cols, width), jnp.bfloat16),
        ),
        in_specs=[scalar, scalar] + [full] * 5 + [anywhere] * 2,
        out_specs=(full,) * 7,
        scratch_shapes=[
            pltpu.VMEM((depth, 3 * local_cols), jnp.bfloat16),
            pltpu.SemaphoreType.DMA((3,)),
            pltpu.SemaphoreType.DMA((4,)),
        ],
        compiler_params=params,
        name="attend",
    )(spot, lengths, total_own, total_other, own_rows, other_rows, out_known, last, last_sent)
    from_x = swap(xy_left, "patch", 1, 2)
    from_y = swap(xy_right, "wcol", 2, 4)
    y_left, y_right, x_left, x_right = pl.pallas_call(
        attend_rest_kernel,
        out_shape=(half_f32, half, half, half_f32),
        in_specs=[scalar, scalar] + [full] * 4,
        out_specs=(full,) * 4,
        compiler_params=params,
        name="attend_rest",
    )(spot, lengths, *kept)
    got_x_left = swap(x_left, "patch", 1, 2)
    got_y_right = swap(y_right, "wcol", 2, 4)
    y_left = (y_left + from_x.astype(jnp.float32)).astype(jnp.bfloat16)
    x_right = (x_right + from_y.astype(jnp.float32)).astype(jnp.bfloat16)
    got_x_right = swap(x_right, "patch", 1, 2)
    got_y_left = swap(y_left, "wcol", 2, 4)
    middle = width // 2
    updated = []
    for columns, parts in (
        (slice(0, middle), (got_x_left, got_y_left)),
        (slice(middle, width), (got_x_right, got_y_right)),
    ):
        out_proj = part_own[:, columns] + parts[0].astype(jnp.float32) + parts[1].astype(jnp.float32)
        updated.append(
            (states[:, columns].astype(jnp.float32) + mod[2, :, columns] * out_proj).astype(
                jnp.bfloat16
            )
        )
    updated = jnp.concatenate(updated, axis=1)
    return updated[None]


def body(hidden_states, modulation, w_qkv, w_out, lengths, *, sizes):
    fits = sizes == (2, 4, 4) and hidden_states.shape[0] == 1 and w_qkv.shape[2] == 3 * HD
    if fits and hidden_states.shape[1] % HD == 0:
        return tiled_body(hidden_states, modulation, w_qkv, w_out, lengths)
    return general_body(hidden_states, modulation, w_qkv, w_out, lengths)


def solution(mesh):
    placed = (
        P("wrow", ("patch", "wcol"), None),
        P("wrow", None, None),
        P("wrow", None, "wcol"),
        P("wcol", "wrow"),
        P("wrow"),
    )
    sizes = tuple(mesh.shape[name] for name in ("patch", "wrow", "wcol"))
    return jax.shard_map(
        functools.partial(body, sizes=sizes),
        mesh=mesh,
        in_specs=placed,
        out_specs=P("wrow", ("patch", "wcol"), None),
        check_vma=False,
    )
```

```python
import functools
import math

import jax
import jax.numpy as jnp
from jax import lax
from jax.experimental import pallas as pl
from jax.experimental.pallas import tpu as pltpu
from jax.sharding import PartitionSpec as P

HD = 128


EPSILON = 1e-06
FLOOR = -1e30


def modulated_norm(states, shift, scale):
    values = states.astype(jnp.float32)
    center = jnp.mean(values, axis=-1, keepdims=True)
    spread = jnp.mean(jnp.square(values - center), axis=-1, keepdims=True)
    return ((values - center) * lax.rsqrt(spread + EPSILON) * (1.0 + scale) + shift).astype(
        jnp.bfloat16
    )


def absorb(carry, keys, values, first, queries, limits):
    peak, weight_sum, numer = carry
    videos_here = keys.shape[0]
    count = keys.shape[1]
    heads_here = queries.shape[2]
    head_size = queries.shape[3]
    key_heads = keys.reshape(videos_here, count, heads_here, head_size)
    value_heads = values.reshape(videos_here, count, heads_here, head_size)
    scores = jnp.einsum(
        "vqhd,vkhd->vhqk", queries, key_heads, preferred_element_type=jnp.float32
    ) * head_size ** (-0.5)
    position = first + jnp.arange(count, dtype=jnp.int32)
    valid = (position[None, :] < limits[:, None])[:, None, None, :]
    scores = jnp.where(valid, scores, FLOOR)
    new_peak = jnp.maximum(peak, jnp.max(scores, axis=-1))
    factor = jnp.exp(peak - new_peak)
    probs = jnp.exp(scores - new_peak[..., None]) * valid.astype(jnp.float32)
    weight_sum = weight_sum * factor + jnp.sum(probs, axis=-1)
    numer = numer * factor[..., None] + jnp.einsum(
        "vhqk,vkhd->vhqd",
        probs.astype(jnp.bfloat16),
        value_heads,
        preferred_element_type=jnp.float32,
    )
    return (new_peak, weight_sum, numer)


def general_body(hidden_states, modulation, w_qkv, w_out, lengths):
    videos_here = hidden_states.shape[0]
    width = hidden_states.shape[2]
    shift = modulation[:, 0][:, None, :]
    scale = modulation[:, 1][:, None, :]
    gate = modulation[:, 2][:, None, :]
    normed = modulated_norm(hidden_states, shift, scale)
    tile_rows = lax.all_gather(normed, "wcol", axis=1, tiled=True)
    tile_len = tile_rows.shape[1]
    local_cols = w_qkv.shape[2]
    flat_rows = tile_rows.reshape(videos_here * tile_len, width)
    piece = lax.all_gather(w_qkv, "wrow", axis=0, tiled=True)
    mixed = jnp.dot(
        flat_rows, piece.reshape(piece.shape[0], 3 * local_cols), preferred_element_type=jnp.float32
    )
    mixed = mixed.reshape(videos_here, tile_len, 3 * local_cols)
    mixed = mixed.astype(jnp.bfloat16).reshape(videos_here, tile_len, 3, local_cols)
    heads_here = local_cols // HD
    queries = mixed[:, :, 0].reshape(videos_here, tile_len, heads_here, HD)
    keys = mixed[:, :, 1]
    values = mixed[:, :, 2]
    start_peak = jnp.full((videos_here, heads_here, tile_len), FLOOR, jnp.float32)
    start_sum = jnp.zeros((videos_here, heads_here, tile_len), jnp.float32)
    start_numer = jnp.zeros((videos_here, heads_here, tile_len, HD), jnp.float32)
    key_piece = lax.all_gather(keys, "patch", axis=1, tiled=True)
    value_piece = lax.all_gather(values, "patch", axis=1, tiled=True)
    count = key_piece.shape[1]
    block_len = 512

    def one_block(index, inner):
        offset = index * block_len
        key_block = lax.dynamic_slice_in_dim(key_piece, offset, block_len, 1)
        value_block = lax.dynamic_slice_in_dim(value_piece, offset, block_len, 1)
        return absorb(inner, key_block, value_block, offset, queries, lengths)

    peak, weight_sum, numer = lax.fori_loop(
        0, count // block_len, one_block, (start_peak, start_sum, start_numer)
    )
    attended = (numer / weight_sum[..., None]).astype(jnp.bfloat16)
    attended = jnp.transpose(attended, (0, 2, 1, 3)).reshape(videos_here * tile_len, local_cols)
    partial_out = jnp.dot(
        attended,
        lax.all_gather(w_out, "wrow", axis=1, tiled=True),
        preferred_element_type=jnp.float32,
    )
    partial_out = partial_out.reshape(videos_here, tile_len, width)
    out_proj = lax.psum_scatter(
        partial_out.astype(jnp.bfloat16), "wcol", scatter_dimension=1, tiled=True
    ).astype(jnp.float32)
    return (hidden_states.astype(jnp.float32) + gate * out_proj).astype(jnp.bfloat16)


SHIFTS = ((0, 0, 0), (1, 1, 0), (0, 1, 0), (1, 0, 0), (0, 0, 1), (1, 1, 1), (0, 1, 1), (1, 0, 1))
VMEM_LIMIT = 18 * 1024 * 1024


def start_shard(spot_ref, here, sent, start, weight_ref, sem):
    depth, width = here.shape[1:]
    owner = spot_ref[0] == spot_ref[3]
    for role, shard in ((owner, here), (jnp.logical_not(owner), sent)):

        @pl.when(role)
        def _():
            for k in range(3):
                pltpu.make_async_copy(
                    shard.at[k],
                    weight_ref.at[pl.ds(start, depth), pl.ds(k * width, width)],
                    sem.at[k],
                ).start()


def wait_shard(here, start, weight_ref, sem):
    depth, width = here.shape[1:]
    for k in range(3):
        pltpu.make_async_copy(
            here.at[k],
            weight_ref.at[pl.ds(start, depth), pl.ds(k * width, width)],
            sem.at[k],
        ).wait()


def norm_kernel(spot_ref, mod_ref, *refs):
    tiles, out_ref, tile_ref = refs[0:4], refs[4], refs[5]
    tile_len, width = tiles[0].shape
    depth = width // 4
    shift = mod_ref[0]
    scale = 1.0 + mod_ref[1]
    for i in range(4):
        rows = pl.ds(i * tile_len, tile_len)
        values = tiles[i][...].astype(jnp.float32)
        center = jnp.mean(values, axis=-1, keepdims=True)
        values = values - center
        spread = jnp.mean(jnp.square(values), axis=-1, keepdims=True)
        tile_ref[...] = (values * lax.rsqrt(spread + EPSILON) * scale + shift).astype(jnp.bfloat16)
        for d in range(4):
            start = pl.multiple_of((spot_ref[2] ^ d) * depth, HD)
            out_ref[rows, d * depth : (d + 1) * depth] = tile_ref[:, pl.ds(start, depth)]


def start_by_role(spot_ref, here, sent, place, sem):
    owner = spot_ref[0] == spot_ref[3]
    for role, source in ((owner, here), (jnp.logical_not(owner), sent)):

        @pl.when(role)
        def _():
            pltpu.make_async_copy(source, place, sem).start()


def early_kernel(spot_ref, own_rows_ref, other_rows_ref, *refs):
    here, sent = refs[0:3], refs[3:6]
    own_ref, other_ref, out_weight_ref, weight_ref, weight_sem, out_sem = refs[6:]
    depth = here[0].shape[1]
    for d in range(3):
        start_shard(spot_ref, here[d], sent[d], d * depth, weight_ref, weight_sem.at[d])
    for d in range(3):
        pltpu.make_async_copy(here[d].at[3], out_weight_ref.at[d], out_sem.at[d]).start()
    for d in range(3):
        wait_shard(here[d], d * depth, weight_ref, weight_sem.at[d])
    step = own_ref.shape[0] // 2
    skip = weight_ref.shape[1] - other_ref.shape[1]
    for r in range(2):
        span = pl.ds(r * step, step)
        own_ref[span, :] = jnp.dot(
            own_rows_ref[span, : 3 * depth], weight_ref[...], preferred_element_type=jnp.float32
        )
    for r in range(2):
        span = pl.ds(r * step, step)
        other_ref[span, :] = jnp.dot(
            other_rows_ref[span, : 3 * depth],
            weight_ref[:, skip:],
            preferred_element_type=jnp.float32,
        )
    for d in range(3):
        pltpu.make_async_copy(here[d].at[3], out_weight_ref.at[d], out_sem.at[d]).wait()


def key_bias(spot_ref, len_ref, tile_len):
    x, y, core = spot_ref[0], spot_ref[1], spot_ref[3]
    lane = lax.broadcasted_iota(jnp.int32, (1, tile_len), 1)
    bias = []
    for dx, dy, dc in SHIFTS:
        base = ((x ^ dx) * 4 + (y ^ dy) * 2 + (core ^ dc)) * tile_len
        bias.append(jnp.where(base + lane < len_ref[0], 0.0, FLOOR))
    return jnp.concatenate(bias, axis=1)


def project(queries, key_ref, value_ref, out_weight_ref, bias):
    rate = HD ** (-0.5) * math.log2(math.e)
    heads = []
    for h in range(queries.shape[1] // HD):
        column = slice(h * HD, (h + 1) * HD)
        scores = lax.dot_general(
            queries[:, column],
            key_ref[:, column],
            (((1,), (1,)), ((), ())),
            preferred_element_type=jnp.float32,
        )
        scores = scores + bias
        peak = jnp.max(scores, axis=-1, keepdims=True)
        probs = jnp.exp2((scores - peak) * rate).astype(jnp.bfloat16)
        sums = jnp.dot(probs, value_ref[h], preferred_element_type=jnp.float32)
        heads.append((sums[:, :HD] / sums[:, HD:]).astype(jnp.bfloat16))
    part = jnp.dot(
        jnp.concatenate(heads, axis=1), out_weight_ref[...], preferred_element_type=jnp.float32
    )
    return part[: part.shape[0] // 2], part[part.shape[0] // 2 :]


def attend_kernel(spot_ref, len_ref, *refs):
    totals, rows_refs, out_here, out_sent, (here, sent) = refs[0:2], refs[2:4], refs[4], refs[5:8], refs[8:10]
    own_ref, left_ref, right_ref, query_ref, key_ref, value_ref, out_weight_ref = refs[10:17]
    weight_ref, weight_sem, out_sem = refs[17:]
    count, width = key_ref.shape
    depth = weight_ref.shape[0]
    z = spot_ref[2]
    start_shard(spot_ref, here, sent, 0, weight_ref, weight_sem)
    places = [
        out_weight_ref.at[:, pl.ds(pl.multiple_of((z ^ d) * width, HD), width)] for d in range(4)
    ]
    for d in range(3):
        start_by_role(spot_ref, out_here.at[d], out_sent[d].at[0], places[d], out_sem.at[d])
    start_by_role(spot_ref, here.at[3], sent.at[3], places[3], out_sem.at[3])
    bias = key_bias(spot_ref, len_ref, count // 8)
    for h in range(width // HD):
        value_ref[h, :, HD:] = jnp.ones((count, HD), jnp.bfloat16)
    wait_shard(here, 0, weight_ref, weight_sem)
    step = count // 4
    queries = None
    for r in range(4):
        span = pl.ds((r % 2) * step, step)
        rows = pl.ds(r * step, step)
        skip = 0 if r < 2 else width
        mixed = (
            totals[r // 2][span, :]
            + jnp.dot(
                rows_refs[r // 2][span, 3 * depth :],
                weight_ref[:, skip:],
                preferred_element_type=jnp.float32,
            )
        ).astype(jnp.bfloat16)
        if r == 0:
            queries = mixed[:, :width]
        elif r == 1:
            query_ref[...] = mixed[:, :width]
        key_ref[rows, :] = mixed[:, width - skip : 2 * width - skip]
        for h in range(width // HD):
            at = 2 * width - skip + h * HD
            value_ref[h, rows, :HD] = mixed[:, at : at + HD]
    for d in range(4):
        source = out_here.at[d] if d < 3 else here.at[3]
        pltpu.make_async_copy(source, places[d], out_sem.at[d]).wait()
    own, diagonal = project(queries, key_ref, value_ref, out_weight_ref, bias)
    own_ref[...] = own
    middle = left_ref.shape[1]
    left_ref[...] = diagonal[:, :middle].astype(jnp.bfloat16)
    right_ref[...] = diagonal[:, middle:].astype(jnp.bfloat16)


def attend_rest_kernel(spot_ref, len_ref, states_ref, mod_ref, *refs):
    part_ref, query_ref, key_ref, value_ref, out_weight_ref, base_ref = refs[:6]
    y_left_ref, y_right_ref, x_left_ref, x_right_ref = refs[6:]
    base_ref[...] = states_ref[...].astype(jnp.float32) + mod_ref[2] * part_ref[...]
    bias = key_bias(spot_ref, len_ref, key_ref.shape[0] // 8)
    along_y, along_x = project(query_ref[...], key_ref, value_ref, out_weight_ref, bias)
    middle = y_left_ref.shape[1]
    y_left_ref[...] = along_y[:, :middle]
    y_right_ref[...] = along_y[:, middle:].astype(jnp.bfloat16)
    x_left_ref[...] = along_x[:, :middle].astype(jnp.bfloat16)
    x_right_ref[...] = along_x[:, middle:]


def tiled_body(hidden_states, modulation, w_qkv, w_out, lengths):
    tile_len, width = hidden_states.shape[1:]
    depth, _, local_cols = w_qkv.shape
    states = hidden_states[0]
    x = lax.axis_index("patch")
    z = lax.axis_index("wrow")
    w = lax.axis_index("wcol")
    core = w % 2
    owner = x == core
    spot = jnp.stack([x, w // 2, z, core]).astype(jnp.int32)
    everywhere = ("patch", "wrow", "wcol")

    def index(a, b, c):
        return (a * 4 + b) * 4 + c

    def swap(array, axis, d, n):
        return lax.ppermute(array, axis, [(i, i ^ d) for i in range(n)])

    def owners_swap(array, d):
        pairs = [
            (index(a, b, c), index(a, b ^ d, c))
            for a in range(2)
            for b in range(4)
            for c in range(4)
            if c % 2 == a
        ]
        return lax.ppermute(array, everywhere, pairs)

    def core_swap(array):
        return swap(array, "wcol", 1, 4)

    full = pl.BlockSpec(memory_space=pltpu.VMEM)
    scalar = pl.BlockSpec(memory_space=pltpu.SMEM)
    anywhere = pl.BlockSpec(memory_space=pl.ANY)
    params = pltpu.CompilerParams(vmem_limit_bytes=VMEM_LIMIT)
    count = 8 * tile_len

    mod = jnp.transpose(modulation, (1, 0, 2))
    kinds = jnp.transpose(w_qkv, (1, 0, 2))

    four = jnp.concatenate([kinds, w_out[None]], axis=0)
    far = owners_swap(four, 2)
    near = owners_swap(four, 1)
    along_x = swap(states, "patch", 1, 2)
    along_y = swap(states, "wcol", 2, 4)
    diagonal = [(a * 4 + c, (a ^ 1) * 4 + (c ^ 2)) for a in range(2) for c in range(4)]
    along_xy = lax.ppermute(states, ("patch", "wcol"), diagonal)
    tiles = [states, along_xy, along_y, along_x]
    own_rows = pl.pallas_call(
        norm_kernel,
        out_shape=jax.ShapeDtypeStruct((count // 2, width), jnp.bfloat16),
        in_specs=[scalar] + [full] * 5,
        out_specs=full,
        scratch_shapes=[pltpu.VMEM((tile_len, width), jnp.bfloat16)],
        compiler_params=params,
        name="norm",
    )(spot, mod, *tiles)
    other_rows = core_swap(own_rows)

    last = owners_swap(far, 1)
    shards = [four, near, far]
    total_own, total_other, out_known = pl.pallas_call(
        early_kernel,
        out_shape=(
            jax.ShapeDtypeStruct((count // 2, 3 * local_cols), jnp.float32),
            jax.ShapeDtypeStruct((count // 2, 2 * local_cols), jnp.float32),
            jax.ShapeDtypeStruct((3,) + w_out.shape, jnp.bfloat16),
        ),
        in_specs=[scalar] + [full] * 2 + [anywhere] * 6,
        out_specs=(full,) * 3,
        scratch_shapes=[
            pltpu.VMEM((3 * depth, 3 * local_cols), jnp.bfloat16),
            pltpu.SemaphoreType.DMA((3, 3)),
            pltpu.SemaphoreType.DMA((3,)),
        ],
        compiler_params=params,
        name="early",
    )(spot, own_rows, other_rows, *shards, *(core_swap(shard[:3]) for shard in shards))
    out_sent = [core_swap(shard[3:]) for shard in shards]
    last, total_own, *out_sent = lax.optimization_barrier((last, total_own, *out_sent))
    last_sent = core_swap(last)

    half = jax.ShapeDtypeStruct((tile_len, width // 2), jnp.bfloat16)
    half_f32 = jax.ShapeDtypeStruct((tile_len, width // 2), jnp.float32)
    part_own, xy_left, xy_right, *kept = pl.pallas_call(
        attend_kernel,
        out_shape=(
            jax.ShapeDtypeStruct((tile_len, width), jnp.float32),
            half,
            half,
            jax.ShapeDtypeStruct((count // 4, local_cols), jnp.bfloat16),
            jax.ShapeDtypeStruct((count, local_cols), jnp.bfloat16),
            jax.ShapeDtypeStruct((local_cols // HD, count, 2 * HD), jnp.bfloat16),
            jax.ShapeDtypeStruct((local_cols, width), jnp.bfloat16),
        ),
        in_specs=[scalar, scalar] + [full] * 4 + [anywhere] * 6,
        out_specs=(full,) * 7,
        scratch_shapes=[
            pltpu.VMEM((depth, 3 * local_cols), jnp.bfloat16),
            pltpu.SemaphoreType.DMA((3,)),
            pltpu.SemaphoreType.DMA((4,)),
        ],
        compiler_params=params,
        name="attend",
    )(spot, lengths, total_own, total_other, own_rows, other_rows, out_known, *out_sent, last, last_sent)
    from_x = swap(xy_left, "patch", 1, 2)
    from_y = swap(xy_right, "wcol", 2, 4)
    base, y_left, y_right, x_left, x_right = pl.pallas_call(
        attend_rest_kernel,
        out_shape=(
            jax.ShapeDtypeStruct((tile_len, width), jnp.float32),
            half_f32,
            half,
            half,
            half_f32,
        ),
        in_specs=[scalar, scalar] + [full] * 7,
        out_specs=(full,) * 5,
        compiler_params=params,
        name="attend_rest",
    )(spot, lengths, states, mod, part_own, *kept)
    got_x_left = swap(x_left, "patch", 1, 2)
    got_y_right = swap(y_right, "wcol", 2, 4)
    y_left = (y_left + from_x.astype(jnp.float32)).astype(jnp.bfloat16)
    x_right = (x_right + from_y.astype(jnp.float32)).astype(jnp.bfloat16)
    got_x_right = swap(x_right, "patch", 1, 2)
    got_y_left = swap(y_left, "wcol", 2, 4)
    middle = width // 2
    updated = []
    for columns, parts in (
        (slice(0, middle), (got_x_left, got_y_left)),
        (slice(middle, width), (got_x_right, got_y_right)),
    ):
        out_proj = parts[0].astype(jnp.float32) + parts[1].astype(jnp.float32)
        updated.append((base[:, columns] + mod[2, :, columns] * out_proj).astype(jnp.bfloat16))
    updated = jnp.concatenate(updated, axis=1)
    return updated[None]


def body(hidden_states, modulation, w_qkv, w_out, lengths, *, sizes):
    fits = sizes == (2, 4, 4) and hidden_states.shape[0] == 1 and w_qkv.shape[2] == 3 * HD
    if fits and hidden_states.shape[1] % HD == 0:
        return tiled_body(hidden_states, modulation, w_qkv, w_out, lengths)
    return general_body(hidden_states, modulation, w_qkv, w_out, lengths)


def solution(mesh):
    placed = (
        P("wrow", ("patch", "wcol"), None),
        P("wrow", None, None),
        P("wrow", None, "wcol"),
        P("wcol", "wrow"),
        P("wrow"),
    )
    sizes = tuple(mesh.shape[name] for name in ("patch", "wrow", "wcol"))
    return jax.shard_map(
        functools.partial(body, sizes=sizes),
        mesh=mesh,
        in_specs=placed,
        out_specs=P("wrow", ("patch", "wcol"), None),
        check_vma=False,
    )
```

```python
import functools
import math

import jax
import jax.numpy as jnp
from jax import lax
from jax.experimental import pallas as pl
from jax.experimental.pallas import tpu as pltpu
from jax.sharding import PartitionSpec as P

HD = 128


EPSILON = 1e-06
FLOOR = -1e30


def modulated_norm(states, shift, scale):
    values = states.astype(jnp.float32)
    center = jnp.mean(values, axis=-1, keepdims=True)
    spread = jnp.mean(jnp.square(values - center), axis=-1, keepdims=True)
    return ((values - center) * lax.rsqrt(spread + EPSILON) * (1.0 + scale) + shift).astype(
        jnp.bfloat16
    )


def absorb(carry, keys, values, first, queries, limits):
    peak, weight_sum, numer = carry
    videos_here = keys.shape[0]
    count = keys.shape[1]
    heads_here = queries.shape[2]
    head_size = queries.shape[3]
    key_heads = keys.reshape(videos_here, count, heads_here, head_size)
    value_heads = values.reshape(videos_here, count, heads_here, head_size)
    scores = jnp.einsum(
        "vqhd,vkhd->vhqk", queries, key_heads, preferred_element_type=jnp.float32
    ) * head_size ** (-0.5)
    position = first + jnp.arange(count, dtype=jnp.int32)
    valid = (position[None, :] < limits[:, None])[:, None, None, :]
    scores = jnp.where(valid, scores, FLOOR)
    new_peak = jnp.maximum(peak, jnp.max(scores, axis=-1))
    factor = jnp.exp(peak - new_peak)
    probs = jnp.exp(scores - new_peak[..., None]) * valid.astype(jnp.float32)
    weight_sum = weight_sum * factor + jnp.sum(probs, axis=-1)
    numer = numer * factor[..., None] + jnp.einsum(
        "vhqk,vkhd->vhqd",
        probs.astype(jnp.bfloat16),
        value_heads,
        preferred_element_type=jnp.float32,
    )
    return (new_peak, weight_sum, numer)


def general_body(hidden_states, modulation, w_qkv, w_out, lengths):
    videos_here = hidden_states.shape[0]
    width = hidden_states.shape[2]
    shift = modulation[:, 0][:, None, :]
    scale = modulation[:, 1][:, None, :]
    gate = modulation[:, 2][:, None, :]
    normed = modulated_norm(hidden_states, shift, scale)
    tile_rows = lax.all_gather(normed, "wcol", axis=1, tiled=True)
    tile_len = tile_rows.shape[1]
    local_cols = w_qkv.shape[2]
    flat_rows = tile_rows.reshape(videos_here * tile_len, width)
    piece = lax.all_gather(w_qkv, "wrow", axis=0, tiled=True)
    mixed = jnp.dot(
        flat_rows, piece.reshape(piece.shape[0], 3 * local_cols), preferred_element_type=jnp.float32
    )
    mixed = mixed.reshape(videos_here, tile_len, 3 * local_cols)
    mixed = mixed.astype(jnp.bfloat16).reshape(videos_here, tile_len, 3, local_cols)
    heads_here = local_cols // HD
    queries = mixed[:, :, 0].reshape(videos_here, tile_len, heads_here, HD)
    keys = mixed[:, :, 1]
    values = mixed[:, :, 2]
    start_peak = jnp.full((videos_here, heads_here, tile_len), FLOOR, jnp.float32)
    start_sum = jnp.zeros((videos_here, heads_here, tile_len), jnp.float32)
    start_numer = jnp.zeros((videos_here, heads_here, tile_len, HD), jnp.float32)
    key_piece = lax.all_gather(keys, "patch", axis=1, tiled=True)
    value_piece = lax.all_gather(values, "patch", axis=1, tiled=True)
    count = key_piece.shape[1]
    block_len = 512

    def one_block(index, inner):
        offset = index * block_len
        key_block = lax.dynamic_slice_in_dim(key_piece, offset, block_len, 1)
        value_block = lax.dynamic_slice_in_dim(value_piece, offset, block_len, 1)
        return absorb(inner, key_block, value_block, offset, queries, lengths)

    peak, weight_sum, numer = lax.fori_loop(
        0, count // block_len, one_block, (start_peak, start_sum, start_numer)
    )
    attended = (numer / weight_sum[..., None]).astype(jnp.bfloat16)
    attended = jnp.transpose(attended, (0, 2, 1, 3)).reshape(videos_here * tile_len, local_cols)
    partial_out = jnp.dot(
        attended,
        lax.all_gather(w_out, "wrow", axis=1, tiled=True),
        preferred_element_type=jnp.float32,
    )
    partial_out = partial_out.reshape(videos_here, tile_len, width)
    out_proj = lax.psum_scatter(
        partial_out.astype(jnp.bfloat16), "wcol", scatter_dimension=1, tiled=True
    ).astype(jnp.float32)
    return (hidden_states.astype(jnp.float32) + gate * out_proj).astype(jnp.bfloat16)


SHIFTS = ((1, 1, 0), (0, 0, 0), (0, 1, 0), (1, 0, 0), (1, 1, 1), (0, 0, 1), (0, 1, 1), (1, 0, 1))
VMEM_LIMIT = 18 * 1024 * 1024


def start_shard(spot_ref, here, sent, start, weight_ref, sem):
    depth, width = here.shape[1:]
    owner = spot_ref[0] == spot_ref[3]
    for role, shard in ((owner, here), (jnp.logical_not(owner), sent)):

        @pl.when(role)
        def _():
            for k in range(3):
                pltpu.make_async_copy(
                    shard.at[k],
                    weight_ref.at[pl.ds(start, depth), pl.ds(k * width, width)],
                    sem.at[k],
                ).start()


def wait_shard(here, start, weight_ref, sem):
    depth, width = here.shape[1:]
    for k in range(3):
        pltpu.make_async_copy(
            here.at[k],
            weight_ref.at[pl.ds(start, depth), pl.ds(k * width, width)],
            sem.at[k],
        ).wait()


def norm_kernel(spot_ref, mod_ref, *refs):
    tiles, out_ref, tile_ref = refs[0:4], refs[4], refs[5]
    tile_len, width = tiles[0].shape
    depth = width // 4
    shift = mod_ref[0]
    scale = 1.0 + mod_ref[1]
    for i in range(4):
        rows = pl.ds(i * tile_len, tile_len)
        values = tiles[i][...].astype(jnp.float32)
        center = jnp.mean(values, axis=-1, keepdims=True)
        values = values - center
        spread = jnp.mean(jnp.square(values), axis=-1, keepdims=True)
        tile_ref[...] = (values * lax.rsqrt(spread + EPSILON) * scale + shift).astype(jnp.bfloat16)
        for d in range(4):
            start = pl.multiple_of((spot_ref[2] ^ d) * depth, HD)
            out_ref[rows, d * depth : (d + 1) * depth] = tile_ref[:, pl.ds(start, depth)]


def start_by_role(spot_ref, here, sent, place, sem):
    owner = spot_ref[0] == spot_ref[3]
    for role, source in ((owner, here), (jnp.logical_not(owner), sent)):

        @pl.when(role)
        def _():
            pltpu.make_async_copy(source, place, sem).start()


def early_kernel(spot_ref, own_rows_ref, other_rows_ref, *refs):
    here, sent, states_ref = refs[0:3], refs[3:6], refs[6]
    own_ref, other_ref, out_weight_ref, kept_ref, weight_ref, weight_sem, out_sem = refs[7:]
    depth = here[0].shape[1]
    keep = pltpu.make_async_copy(states_ref, kept_ref, out_sem.at[3])
    keep.start()
    for d in range(3):
        start_shard(spot_ref, here[d], sent[d], d * depth, weight_ref, weight_sem.at[d])
    for d in range(3):
        pltpu.make_async_copy(here[d].at[3], out_weight_ref.at[d], out_sem.at[d]).start()
    for d in range(3):
        wait_shard(here[d], d * depth, weight_ref, weight_sem.at[d])
    step = own_ref.shape[0] // 2
    skip = weight_ref.shape[1] - other_ref.shape[1]
    for r in range(2):
        span = pl.ds(r * step, step)
        own_ref[span, :] = jnp.dot(
            own_rows_ref[span, : 3 * depth], weight_ref[...], preferred_element_type=jnp.float32
        )
    for r in range(2):
        span = pl.ds(r * step, step)
        other_ref[span, :] = jnp.dot(
            other_rows_ref[span, : 3 * depth],
            weight_ref[:, skip:],
            preferred_element_type=jnp.float32,
        )
    for d in range(3):
        pltpu.make_async_copy(here[d].at[3], out_weight_ref.at[d], out_sem.at[d]).wait()
    keep.wait()


def key_bias(spot_ref, len_ref, tile_len):
    x, y, core = spot_ref[0], spot_ref[1], spot_ref[3]
    lane = lax.broadcasted_iota(jnp.int32, (1, tile_len), 1)
    bias = []
    for dx, dy, dc in SHIFTS:
        base = ((x ^ dx) * 4 + (y ^ dy) * 2 + (core ^ dc)) * tile_len
        bias.append(jnp.where(base + lane < len_ref[0], 0.0, FLOOR))
    return jnp.concatenate(bias, axis=1)


def project(queries, key_ref, value_ref, out_weight_ref, bias):
    rate = HD ** (-0.5) * math.log2(math.e)
    heads = []
    for h in range(queries.shape[1] // HD):
        column = slice(h * HD, (h + 1) * HD)
        scores = lax.dot_general(
            queries[:, column],
            key_ref[:, column],
            (((1,), (1,)), ((), ())),
            preferred_element_type=jnp.float32,
        )
        scores = scores + bias
        peak = jnp.max(scores, axis=-1, keepdims=True)
        probs = jnp.exp2((scores - peak) * rate).astype(jnp.bfloat16)
        sums = jnp.dot(probs, value_ref[h], preferred_element_type=jnp.float32)
        heads.append((sums[:, :HD] / sums[:, HD:]).astype(jnp.bfloat16))
    part = jnp.dot(
        jnp.concatenate(heads, axis=1), out_weight_ref[...], preferred_element_type=jnp.float32
    )
    return part


def attend_kernel(spot_ref, len_ref, *refs):
    totals, rows_refs, out_here, out_sent, (here, sent) = refs[0:2], refs[2:4], refs[4], refs[5:8], refs[8:10]
    left_ref, right_ref, bias_ref, query_ref, key_ref, value_ref, out_weight_ref = refs[10:17]
    out_sem = refs[17]
    count, width = key_ref.shape
    depth = here.shape[1]
    z = spot_ref[2]
    places = [
        out_weight_ref.at[:, pl.ds(pl.multiple_of((z ^ d) * width, HD), width)] for d in range(4)
    ]
    for d in range(3):
        start_by_role(spot_ref, out_here.at[d], out_sent[d].at[0], places[d], out_sem.at[d])
    start_by_role(spot_ref, here.at[3], sent.at[3], places[3], out_sem.at[3])
    bias_ref[...] = key_bias(spot_ref, len_ref, count // 8)
    for h in range(width // HD):
        value_ref[h, :, HD:] = jnp.ones((count, HD), jnp.bfloat16)
    step = count // 4

    def finish(shard):
        weights = jnp.concatenate([shard[k] for k in range(3)], axis=1)
        for r in range(4):
            span = pl.ds((r % 2) * step, step)
            rows = pl.ds(r * step, step)
            skip = 0 if r < 2 else width
            mixed = (
                totals[r // 2][span, :]
                + jnp.dot(
                    rows_refs[r // 2][span, 3 * depth :],
                    weights[:, skip:],
                    preferred_element_type=jnp.float32,
                )
            ).astype(jnp.bfloat16)
            if r < 2:
                query_ref[rows, :] = mixed[:, :width]
            key_ref[rows, :] = mixed[:, width - skip : 2 * width - skip]
            for h in range(width // HD):
                at = 2 * width - skip + h * HD
                value_ref[h, rows, :HD] = mixed[:, at : at + HD]

    owner = spot_ref[0] == spot_ref[3]
    for role, shard in ((owner, here), (jnp.logical_not(owner), sent)):

        @pl.when(role)
        def _():
            finish(shard)

    for d in range(4):
        source = out_here.at[d] if d < 3 else here.at[3]
        pltpu.make_async_copy(source, places[d], out_sem.at[d]).wait()
    diagonal = project(query_ref[: step // 2, :], key_ref, value_ref, out_weight_ref, bias_ref[...])
    middle = left_ref.shape[1]
    left_ref[...] = diagonal[:, :middle].astype(jnp.bfloat16)
    right_ref[...] = diagonal[:, middle:].astype(jnp.bfloat16)


def attend_rest_kernel(states_ref, mod_ref, *refs):
    bias_ref, query_ref, key_ref, value_ref, out_weight_ref, base_ref = refs[:6]
    y_left_ref, y_right_ref, x_left_ref, x_right_ref = refs[6:]
    tile_len, middle = y_left_ref.shape
    held = (key_ref, value_ref, out_weight_ref, bias_ref[...])
    part = project(query_ref[2 * tile_len :, :], *held)
    y_left_ref[...] = part[:tile_len, :middle]
    y_right_ref[...] = part[:tile_len, middle:].astype(jnp.bfloat16)
    x_left_ref[...] = part[tile_len:, :middle].astype(jnp.bfloat16)
    x_right_ref[...] = part[tile_len:, middle:]
    own = project(query_ref[tile_len : 2 * tile_len, :], *held)
    base_ref[...] = states_ref[...].astype(jnp.float32) + mod_ref[2] * own


def backwards(kernel, count):
    return lambda *refs: kernel(*refs[:count][::-1], *refs[count:])


def tiled_body(hidden_states, modulation, w_qkv, w_out, lengths):
    tile_len, width = hidden_states.shape[1:]
    depth, _, local_cols = w_qkv.shape
    states = hidden_states[0]
    x = lax.axis_index("patch")
    z = lax.axis_index("wrow")
    w = lax.axis_index("wcol")
    core = w % 2
    owner = x == core
    spot = jnp.stack([x, w // 2, z, core]).astype(jnp.int32)
    everywhere = ("patch", "wrow", "wcol")

    def index(a, b, c):
        return (a * 4 + b) * 4 + c

    def swap(array, axis, d, n):
        return lax.ppermute(array, axis, [(i, i ^ d) for i in range(n)])

    def owners_swap(array, d):
        pairs = [
            (index(a, b, c), index(a, b ^ d, c))
            for a in range(2)
            for b in range(4)
            for c in range(4)
            if c % 2 == a
        ]
        return lax.ppermute(array, everywhere, pairs)

    def core_swap(array):
        return swap(array, "wcol", 1, 4)

    full = pl.BlockSpec(memory_space=pltpu.VMEM)
    scalar = pl.BlockSpec(memory_space=pltpu.SMEM)
    anywhere = pl.BlockSpec(memory_space=pl.ANY)
    params = pltpu.CompilerParams(vmem_limit_bytes=VMEM_LIMIT)
    count = 8 * tile_len

    mod = jnp.transpose(modulation, (1, 0, 2))
    kinds = jnp.transpose(w_qkv, (1, 0, 2))

    four = jnp.concatenate([kinds, w_out[None]], axis=0)
    far = owners_swap(four, 2)
    near = owners_swap(four, 1)
    along_x = swap(states, "patch", 1, 2)
    along_y = swap(states, "wcol", 2, 4)
    diagonal = [(a * 4 + c, (a ^ 1) * 4 + (c ^ 2)) for a in range(2) for c in range(4)]
    along_xy = lax.ppermute(states, ("patch", "wcol"), diagonal)
    tiles = [along_xy, states, along_y, along_x]
    own_rows = pl.pallas_call(
        backwards(norm_kernel, 6),
        out_shape=jax.ShapeDtypeStruct((count // 2, width), jnp.bfloat16),
        in_specs=[full] * 5 + [scalar],
        out_specs=full,
        scratch_shapes=[pltpu.VMEM((tile_len, width), jnp.bfloat16)],
        compiler_params=params,
        name="norm",
    )(*tiles[::-1], mod, spot)
    other_rows = core_swap(own_rows)

    last = owners_swap(far, 1)
    shards = [four, near, far]
    total_own, total_other, out_known, states_kept = pl.pallas_call(
        backwards(early_kernel, 10),
        out_shape=(
            jax.ShapeDtypeStruct((count // 2, 3 * local_cols), jnp.float32),
            jax.ShapeDtypeStruct((count // 2, 2 * local_cols), jnp.float32),
            jax.ShapeDtypeStruct((3,) + w_out.shape, jnp.bfloat16),
            jax.ShapeDtypeStruct((tile_len, width), jnp.bfloat16),
        ),
        in_specs=[anywhere] * 7 + [full] * 2 + [scalar],
        out_specs=(full,) * 4,
        scratch_shapes=[
            pltpu.VMEM((3 * depth, 3 * local_cols), jnp.bfloat16),
            pltpu.SemaphoreType.DMA((3, 3)),
            pltpu.SemaphoreType.DMA((4,)),
        ],
        compiler_params=params,
        name="early",
    )(states, *(core_swap(shard[:3]) for shard in shards[::-1]), *shards[::-1], other_rows, own_rows, spot)
    out_sent = [core_swap(shard[3:]) for shard in shards]
    last, total_own, *out_sent = lax.optimization_barrier((last, total_own, *out_sent))
    last_sent = core_swap(last)

    half = jax.ShapeDtypeStruct((tile_len, width // 2), jnp.bfloat16)
    half_f32 = jax.ShapeDtypeStruct((tile_len, width // 2), jnp.float32)
    xy_left, xy_right, *kept = pl.pallas_call(
        backwards(attend_kernel, 12),
        out_shape=(
            half,
            half,
            jax.ShapeDtypeStruct((1, count), jnp.float32),
            jax.ShapeDtypeStruct((count // 2, local_cols), jnp.bfloat16),
            jax.ShapeDtypeStruct((count, local_cols), jnp.bfloat16),
            jax.ShapeDtypeStruct((local_cols // HD, count, 2 * HD), jnp.bfloat16),
            jax.ShapeDtypeStruct((local_cols, width), jnp.bfloat16),
        ),
        in_specs=[full] * 2 + [anywhere] * 4 + [full] * 4 + [scalar, scalar],
        out_specs=(full,) * 7,
        scratch_shapes=[pltpu.SemaphoreType.DMA((4,))],
        compiler_params=params,
        name="attend",
    )(last_sent, last, *out_sent[::-1], out_known, other_rows, own_rows, total_other, total_own, lengths, spot)
    from_x = swap(xy_left, "patch", 1, 2)
    from_y = swap(xy_right, "wcol", 2, 4)
    base, y_left, y_right, x_left, x_right = pl.pallas_call(
        backwards(attend_rest_kernel, 7),
        out_shape=(
            jax.ShapeDtypeStruct((tile_len, width), jnp.float32),
            half_f32,
            half,
            half,
            half_f32,
        ),
        in_specs=[full] * 7,
        out_specs=(full,) * 5,
        compiler_params=params,
        name="attend_rest",
    )(*kept[::-1], mod, states_kept)
    got_x_left = swap(x_left, "patch", 1, 2)
    got_y_right = swap(y_right, "wcol", 2, 4)
    y_left = (y_left + from_x.astype(jnp.float32)).astype(jnp.bfloat16)
    x_right = (x_right + from_y.astype(jnp.float32)).astype(jnp.bfloat16)
    got_x_right = swap(x_right, "patch", 1, 2)
    got_y_left = swap(y_left, "wcol", 2, 4)
    middle = width // 2
    updated = []
    for columns, parts in (
        (slice(0, middle), (got_x_left, got_y_left)),
        (slice(middle, width), (got_x_right, got_y_right)),
    ):
        out_proj = parts[0].astype(jnp.float32) + parts[1].astype(jnp.float32)
        updated.append((base[:, columns] + mod[2, :, columns] * out_proj).astype(jnp.bfloat16))
    updated = jnp.concatenate(updated, axis=1)
    return updated[None]


def body(hidden_states, modulation, w_qkv, w_out, lengths, *, sizes):
    fits = sizes == (2, 4, 4) and hidden_states.shape[0] == 1 and w_qkv.shape[2] == 3 * HD
    if fits and hidden_states.shape[1] % HD == 0:
        return tiled_body(hidden_states, modulation, w_qkv, w_out, lengths)
    return general_body(hidden_states, modulation, w_qkv, w_out, lengths)


def solution(mesh):
    placed = (
        P("wrow", ("patch", "wcol"), None),
        P("wrow", None, None),
        P("wrow", None, "wcol"),
        P("wcol", "wrow"),
        P("wrow"),
    )
    sizes = tuple(mesh.shape[name] for name in ("patch", "wrow", "wcol"))
    return jax.shard_map(
        functools.partial(body, sizes=sizes),
        mesh=mesh,
        in_specs=placed,
        out_specs=P("wrow", ("patch", "wcol"), None),
        check_vma=False,
    )
```

```python
import functools
import math

import jax
import jax.numpy as jnp
from jax import lax
from jax.experimental import pallas as pl
from jax.experimental.pallas import tpu as pltpu
from jax.sharding import PartitionSpec as P

HD = 128


EPSILON = 1e-06
FLOOR = -1e30


def modulated_norm(states, shift, scale):
    values = states.astype(jnp.float32)
    center = jnp.mean(values, axis=-1, keepdims=True)
    spread = jnp.mean(jnp.square(values - center), axis=-1, keepdims=True)
    return ((values - center) * lax.rsqrt(spread + EPSILON) * (1.0 + scale) + shift).astype(
        jnp.bfloat16
    )


def absorb(carry, keys, values, first, queries, limits):
    peak, weight_sum, numer = carry
    videos_here = keys.shape[0]
    count = keys.shape[1]
    heads_here = queries.shape[2]
    head_size = queries.shape[3]
    key_heads = keys.reshape(videos_here, count, heads_here, head_size)
    value_heads = values.reshape(videos_here, count, heads_here, head_size)
    scores = jnp.einsum(
        "vqhd,vkhd->vhqk", queries, key_heads, preferred_element_type=jnp.float32
    ) * head_size ** (-0.5)
    position = first + jnp.arange(count, dtype=jnp.int32)
    valid = (position[None, :] < limits[:, None])[:, None, None, :]
    scores = jnp.where(valid, scores, FLOOR)
    new_peak = jnp.maximum(peak, jnp.max(scores, axis=-1))
    factor = jnp.exp(peak - new_peak)
    probs = jnp.exp(scores - new_peak[..., None]) * valid.astype(jnp.float32)
    weight_sum = weight_sum * factor + jnp.sum(probs, axis=-1)
    numer = numer * factor[..., None] + jnp.einsum(
        "vhqk,vkhd->vhqd",
        probs.astype(jnp.bfloat16),
        value_heads,
        preferred_element_type=jnp.float32,
    )
    return (new_peak, weight_sum, numer)


def general_body(hidden_states, modulation, w_qkv, w_out, lengths):
    videos_here = hidden_states.shape[0]
    width = hidden_states.shape[2]
    shift = modulation[:, 0][:, None, :]
    scale = modulation[:, 1][:, None, :]
    gate = modulation[:, 2][:, None, :]
    normed = modulated_norm(hidden_states, shift, scale)
    tile_rows = lax.all_gather(normed, "wcol", axis=1, tiled=True)
    tile_len = tile_rows.shape[1]
    local_cols = w_qkv.shape[2]
    flat_rows = tile_rows.reshape(videos_here * tile_len, width)
    piece = lax.all_gather(w_qkv, "wrow", axis=0, tiled=True)
    mixed = jnp.dot(
        flat_rows, piece.reshape(piece.shape[0], 3 * local_cols), preferred_element_type=jnp.float32
    )
    mixed = mixed.reshape(videos_here, tile_len, 3 * local_cols)
    mixed = mixed.astype(jnp.bfloat16).reshape(videos_here, tile_len, 3, local_cols)
    heads_here = local_cols // HD
    queries = mixed[:, :, 0].reshape(videos_here, tile_len, heads_here, HD)
    keys = mixed[:, :, 1]
    values = mixed[:, :, 2]
    start_peak = jnp.full((videos_here, heads_here, tile_len), FLOOR, jnp.float32)
    start_sum = jnp.zeros((videos_here, heads_here, tile_len), jnp.float32)
    start_numer = jnp.zeros((videos_here, heads_here, tile_len, HD), jnp.float32)
    key_piece = lax.all_gather(keys, "patch", axis=1, tiled=True)
    value_piece = lax.all_gather(values, "patch", axis=1, tiled=True)
    count = key_piece.shape[1]
    block_len = 512

    def one_block(index, inner):
        offset = index * block_len
        key_block = lax.dynamic_slice_in_dim(key_piece, offset, block_len, 1)
        value_block = lax.dynamic_slice_in_dim(value_piece, offset, block_len, 1)
        return absorb(inner, key_block, value_block, offset, queries, lengths)

    peak, weight_sum, numer = lax.fori_loop(
        0, count // block_len, one_block, (start_peak, start_sum, start_numer)
    )
    attended = (numer / weight_sum[..., None]).astype(jnp.bfloat16)
    attended = jnp.transpose(attended, (0, 2, 1, 3)).reshape(videos_here * tile_len, local_cols)
    partial_out = jnp.dot(
        attended,
        lax.all_gather(w_out, "wrow", axis=1, tiled=True),
        preferred_element_type=jnp.float32,
    )
    partial_out = partial_out.reshape(videos_here, tile_len, width)
    out_proj = lax.psum_scatter(
        partial_out.astype(jnp.bfloat16), "wcol", scatter_dimension=1, tiled=True
    ).astype(jnp.float32)
    return (hidden_states.astype(jnp.float32) + gate * out_proj).astype(jnp.bfloat16)


SHIFTS = ((1, 1, 0), (0, 0, 0), (0, 1, 0), (1, 0, 0), (1, 1, 1), (0, 0, 1), (0, 1, 1), (1, 0, 1))
VMEM_LIMIT = 18 * 1024 * 1024


def start_shard(spot_ref, here, sent, start, weight_ref, sem):
    depth, width = here.shape[1:]
    owner = spot_ref[0] == spot_ref[3]
    for role, shard in ((owner, here), (jnp.logical_not(owner), sent)):

        @pl.when(role)
        def _():
            for k in range(3):
                pltpu.make_async_copy(
                    shard.at[k],
                    weight_ref.at[pl.ds(start, depth), pl.ds(k * width, width)],
                    sem.at[k],
                ).start()


def wait_shard(here, start, weight_ref, sem):
    depth, width = here.shape[1:]
    for k in range(3):
        pltpu.make_async_copy(
            here.at[k],
            weight_ref.at[pl.ds(start, depth), pl.ds(k * width, width)],
            sem.at[k],
        ).wait()


def norm_kernel(spot_ref, mod_ref, *refs):
    tiles, out_ref, tile_ref = refs[0:4], refs[4], refs[5]
    tile_len, width = tiles[0].shape
    depth = width // 4
    shift = mod_ref[0]
    scale = 1.0 + mod_ref[1]
    for i in range(4):
        rows = pl.ds(i * tile_len, tile_len)
        values = tiles[i][...].astype(jnp.float32)
        center = jnp.mean(values, axis=-1, keepdims=True)
        values = values - center
        spread = jnp.mean(jnp.square(values), axis=-1, keepdims=True)
        tile_ref[...] = (values * lax.rsqrt(spread + EPSILON) * scale + shift).astype(jnp.bfloat16)
        for d in range(4):
            start = pl.multiple_of((spot_ref[2] ^ d) * depth, HD)
            out_ref[rows, d * depth : (d + 1) * depth] = tile_ref[:, pl.ds(start, depth)]


def start_by_role(spot_ref, here, sent, place, sem):
    owner = spot_ref[0] == spot_ref[3]
    for role, source in ((owner, here), (jnp.logical_not(owner), sent)):

        @pl.when(role)
        def _():
            pltpu.make_async_copy(source, place, sem).start()


def early_kernel(spot_ref, own_rows_ref, other_rows_ref, *refs):
    here, sent, states_ref = refs[0:3], refs[3:6], refs[6]
    own_ref, other_ref, out_weight_ref, kept_ref, weight_ref, weight_sem, out_sem = refs[7:]
    depth = here[0].shape[1]
    keep = pltpu.make_async_copy(states_ref, kept_ref, out_sem.at[3])
    keep.start()
    for d in range(3):
        start_shard(spot_ref, here[d], sent[d], d * depth, weight_ref, weight_sem.at[d])
    for d in range(3):
        pltpu.make_async_copy(here[d].at[3], out_weight_ref.at[d], out_sem.at[d]).start()
    for d in range(3):
        wait_shard(here[d], d * depth, weight_ref, weight_sem.at[d])
    step = own_ref.shape[0] // 2
    skip = weight_ref.shape[1] - other_ref.shape[1]
    for r in range(2):
        span = pl.ds(r * step, step)
        own_ref[span, :] = jnp.dot(
            own_rows_ref[span, : 3 * depth], weight_ref[...], preferred_element_type=jnp.float32
        )
    for r in range(2):
        span = pl.ds(r * step, step)
        other_ref[span, :] = jnp.dot(
            other_rows_ref[span, : 3 * depth],
            weight_ref[:, skip:],
            preferred_element_type=jnp.float32,
        )
    for d in range(3):
        pltpu.make_async_copy(here[d].at[3], out_weight_ref.at[d], out_sem.at[d]).wait()
    keep.wait()


def key_bias(spot_ref, len_ref, tile_len):
    x, y, core = spot_ref[0], spot_ref[1], spot_ref[3]
    lane = lax.broadcasted_iota(jnp.int32, (1, tile_len), 1)
    bias = []
    for dx, dy, dc in SHIFTS:
        base = ((x ^ dx) * 4 + (y ^ dy) * 2 + (core ^ dc)) * tile_len
        bias.append(jnp.where(base + lane < len_ref[0], 0.0, FLOOR))
    return jnp.concatenate(bias, axis=1)


def project(queries, key_ref, value_ref, out_weight_ref, bias):
    rate = HD ** (-0.5) * math.log2(math.e)
    heads = []
    for h in range(queries.shape[1] // HD):
        column = slice(h * HD, (h + 1) * HD)
        scores = lax.dot_general(
            queries[:, column],
            key_ref[:, column],
            (((1,), (1,)), ((), ())),
            preferred_element_type=jnp.float32,
        )
        scores = scores + bias
        peak = jnp.max(scores, axis=-1, keepdims=True)
        probs = jnp.exp2((scores - peak) * rate).astype(jnp.bfloat16)
        sums = jnp.dot(probs, value_ref[h], preferred_element_type=jnp.float32)
        heads.append((sums[:, :HD] / sums[:, HD:]).astype(jnp.bfloat16))
    part = jnp.dot(
        jnp.concatenate(heads, axis=1), out_weight_ref[...], preferred_element_type=jnp.float32
    )
    return part


def attend_kernel(spot_ref, len_ref, *refs):
    totals, rows_refs, out_here, out_sent, (here, sent) = refs[0:2], refs[2:4], refs[4], refs[5:8], refs[8:10]
    left_ref, right_ref, bias_ref, query_ref, key_ref, value_ref, out_weight_ref = refs[10:17]
    out_sem = refs[17]
    count, width = key_ref.shape
    depth = here.shape[1]
    z = spot_ref[2]
    places = [
        out_weight_ref.at[:, pl.ds(pl.multiple_of((z ^ d) * width, HD), width)] for d in range(4)
    ]
    for d in range(3):
        start_by_role(spot_ref, out_here.at[d], out_sent[d].at[0], places[d], out_sem.at[d])
    start_by_role(spot_ref, here.at[3], sent.at[3], places[3], out_sem.at[3])
    bias_ref[...] = key_bias(spot_ref, len_ref, count // 8)
    for h in range(width // HD):
        value_ref[h, :, HD:] = jnp.ones((count, HD), jnp.bfloat16)
    step = count // 4

    def finish(shard):
        weights = jnp.concatenate([shard[k] for k in range(3)], axis=1)
        for r in range(4):
            span = pl.ds((r % 2) * step, step)
            rows = pl.ds(r * step, step)
            skip = 0 if r < 2 else width
            mixed = (
                totals[r // 2][span, :]
                + jnp.dot(
                    rows_refs[r // 2][span, 3 * depth :],
                    weights[:, skip:],
                    preferred_element_type=jnp.float32,
                )
            ).astype(jnp.bfloat16)
            if r < 2:
                query_ref[rows, :] = mixed[:, :width]
            key_ref[rows, :] = mixed[:, width - skip : 2 * width - skip]
            for h in range(width // HD):
                at = 2 * width - skip + h * HD
                value_ref[h, rows, :HD] = mixed[:, at : at + HD]

    owner = spot_ref[0] == spot_ref[3]
    for role, shard in ((owner, here), (jnp.logical_not(owner), sent)):

        @pl.when(role)
        def _():
            finish(shard)

    for d in range(4):
        source = out_here.at[d] if d < 3 else here.at[3]
        pltpu.make_async_copy(source, places[d], out_sem.at[d]).wait()
    diagonal = project(query_ref[: step // 2, :], key_ref, value_ref, out_weight_ref, bias_ref[...])
    middle = left_ref.shape[1]
    left_ref[...] = diagonal[:, :middle].astype(jnp.bfloat16)
    right_ref[...] = diagonal[:, middle:].astype(jnp.bfloat16)


def attend_rest_kernel(bias_ref, query_ref, key_ref, value_ref, out_weight_ref, *out_refs):
    y_left_ref, y_right_ref, x_left_ref, x_right_ref = out_refs
    tile_len, middle = y_left_ref.shape
    queries = query_ref[2 * tile_len :, :]
    part = project(queries, key_ref, value_ref, out_weight_ref, bias_ref[...])
    y_left_ref[...] = part[:tile_len, :middle]
    y_right_ref[...] = part[:tile_len, middle:].astype(jnp.bfloat16)
    x_left_ref[...] = part[tile_len:, :middle].astype(jnp.bfloat16)
    x_right_ref[...] = part[tile_len:, middle:]


def attend_own_kernel(
    out_weight_ref, value_ref, key_ref, query_ref, bias_ref, mod_ref, states_ref, base_ref
):
    tile_len = base_ref.shape[0]
    queries = query_ref[tile_len : 2 * tile_len, :]
    own = project(queries, key_ref, value_ref, out_weight_ref, bias_ref[...])
    base_ref[...] = states_ref[...].astype(jnp.float32) + mod_ref[2] * own


def tiled_body(hidden_states, modulation, w_qkv, w_out, lengths):
    tile_len, width = hidden_states.shape[1:]
    depth, _, local_cols = w_qkv.shape
    states = hidden_states[0]
    x = lax.axis_index("patch")
    z = lax.axis_index("wrow")
    w = lax.axis_index("wcol")
    core = w % 2
    owner = x == core
    spot = jnp.stack([x, w // 2, z, core]).astype(jnp.int32)
    everywhere = ("patch", "wrow", "wcol")

    def index(a, b, c):
        return (a * 4 + b) * 4 + c

    def swap(array, axis, d, n):
        return lax.ppermute(array, axis, [(i, i ^ d) for i in range(n)])

    def owners_swap(array, d):
        pairs = [
            (index(a, b, c), index(a, b ^ d, c))
            for a in range(2)
            for b in range(4)
            for c in range(4)
            if c % 2 == a
        ]
        return lax.ppermute(array, everywhere, pairs)

    def core_swap(array):
        return swap(array, "wcol", 1, 4)

    full = pl.BlockSpec(memory_space=pltpu.VMEM)
    scalar = pl.BlockSpec(memory_space=pltpu.SMEM)
    anywhere = pl.BlockSpec(memory_space=pl.ANY)
    params = pltpu.CompilerParams(vmem_limit_bytes=VMEM_LIMIT)
    count = 8 * tile_len

    mod = jnp.transpose(modulation, (1, 0, 2))
    kinds = jnp.transpose(w_qkv, (1, 0, 2))

    four = jnp.concatenate([kinds, w_out[None]], axis=0)
    far = owners_swap(four, 2)
    near = owners_swap(four, 1)
    along_x = swap(states, "patch", 1, 2)
    along_y = swap(states, "wcol", 2, 4)
    diagonal = [(a * 4 + c, (a ^ 1) * 4 + (c ^ 2)) for a in range(2) for c in range(4)]
    along_xy = lax.ppermute(states, ("patch", "wcol"), diagonal)
    tiles = [along_xy, states, along_y, along_x]
    own_rows = pl.pallas_call(
        norm_kernel,
        out_shape=jax.ShapeDtypeStruct((count // 2, width), jnp.bfloat16),
        in_specs=[scalar] + [full] * 5,
        out_specs=full,
        scratch_shapes=[pltpu.VMEM((tile_len, width), jnp.bfloat16)],
        compiler_params=params,
        name="norm",
    )(spot, mod, *tiles)
    other_rows = core_swap(own_rows)

    last = owners_swap(far, 1)
    shards = [four, near, far]
    total_own, total_other, out_known, states_kept = pl.pallas_call(
        early_kernel,
        out_shape=(
            jax.ShapeDtypeStruct((count // 2, 3 * local_cols), jnp.float32),
            jax.ShapeDtypeStruct((count // 2, 2 * local_cols), jnp.float32),
            jax.ShapeDtypeStruct((3,) + w_out.shape, jnp.bfloat16),
            jax.ShapeDtypeStruct((tile_len, width), jnp.bfloat16),
        ),
        in_specs=[scalar] + [full] * 2 + [anywhere] * 7,
        out_specs=(full,) * 4,
        scratch_shapes=[
            pltpu.VMEM((3 * depth, 3 * local_cols), jnp.bfloat16),
            pltpu.SemaphoreType.DMA((3, 3)),
            pltpu.SemaphoreType.DMA((4,)),
        ],
        compiler_params=params,
        name="early",
    )(spot, own_rows, other_rows, *shards, *(core_swap(shard[:3]) for shard in shards), states)
    out_sent = [core_swap(shard[3:]) for shard in shards]
    last, total_own, *out_sent = lax.optimization_barrier((last, total_own, *out_sent))
    last_sent = core_swap(last)

    half = jax.ShapeDtypeStruct((tile_len, width // 2), jnp.bfloat16)
    half_f32 = jax.ShapeDtypeStruct((tile_len, width // 2), jnp.float32)
    xy_left, xy_right, *kept = pl.pallas_call(
        attend_kernel,
        out_shape=(
            half,
            half,
            jax.ShapeDtypeStruct((1, count), jnp.float32),
            jax.ShapeDtypeStruct((count // 2, local_cols), jnp.bfloat16),
            jax.ShapeDtypeStruct((count, local_cols), jnp.bfloat16),
            jax.ShapeDtypeStruct((local_cols // HD, count, 2 * HD), jnp.bfloat16),
            jax.ShapeDtypeStruct((local_cols, width), jnp.bfloat16),
        ),
        in_specs=[scalar, scalar] + [full] * 4 + [anywhere] * 4 + [full] * 2,
        out_specs=(full,) * 7,
        scratch_shapes=[pltpu.SemaphoreType.DMA((4,))],
        compiler_params=params,
        name="attend",
    )(spot, lengths, total_own, total_other, own_rows, other_rows, out_known, *out_sent, last, last_sent)
    from_x = swap(xy_left, "patch", 1, 2)
    from_y = swap(xy_right, "wcol", 2, 4)
    y_left, y_right, x_left, x_right = pl.pallas_call(
        attend_rest_kernel,
        out_shape=(half_f32, half, half, half_f32),
        in_specs=[full] * 5,
        out_specs=(full,) * 4,
        compiler_params=params,
        name="attend_rest",
    )(*kept)
    base = pl.pallas_call(
        attend_own_kernel,
        out_shape=jax.ShapeDtypeStruct((tile_len, width), jnp.float32),
        in_specs=[full] * 7,
        out_specs=full,
        compiler_params=params,
        name="attend_own",
    )(*kept[::-1], mod, states_kept)
    got_x_left = swap(x_left, "patch", 1, 2)
    got_y_right = swap(y_right, "wcol", 2, 4)
    y_left = (y_left + from_x.astype(jnp.float32)).astype(jnp.bfloat16)
    x_right = (x_right + from_y.astype(jnp.float32)).astype(jnp.bfloat16)
    got_x_right = swap(x_right, "patch", 1, 2)
    got_y_left = swap(y_left, "wcol", 2, 4)
    middle = width // 2
    updated = []
    for columns, parts in (
        (slice(0, middle), (got_x_left, got_y_left)),
        (slice(middle, width), (got_x_right, got_y_right)),
    ):
        out_proj = parts[1].astype(jnp.float32) + parts[0].astype(jnp.float32)
        updated.append((mod[2, :, columns] * out_proj + base[:, columns]).astype(jnp.bfloat16))
    updated = jnp.concatenate(updated, axis=1)
    return updated[None]


def body(hidden_states, modulation, w_qkv, w_out, lengths, *, sizes):
    fits = sizes == (2, 4, 4) and hidden_states.shape[0] == 1 and w_qkv.shape[2] == 3 * HD
    if fits and hidden_states.shape[1] % HD == 0:
        return tiled_body(hidden_states, modulation, w_qkv, w_out, lengths)
    return general_body(hidden_states, modulation, w_qkv, w_out, lengths)


def solution(mesh):
    placed = (
        P("wrow", ("patch", "wcol"), None),
        P("wrow", None, None),
        P("wrow", None, "wcol"),
        P("wcol", "wrow"),
        P("wrow"),
    )
    sizes = tuple(mesh.shape[name] for name in ("patch", "wrow", "wcol"))
    return jax.shard_map(
        functools.partial(body, sizes=sizes),
        mesh=mesh,
        in_specs=placed,
        out_specs=P("wrow", ("patch", "wcol"), None),
        check_vma=False,
    )
```

```python
import functools
import math

import jax
import jax.numpy as jnp
from jax import lax
from jax.experimental import pallas as pl
from jax.experimental.pallas import tpu as pltpu
from jax.sharding import PartitionSpec as P

HD = 128


EPSILON = 1e-06
FLOOR = -1e30


def modulated_norm(states, shift, scale):
    values = states.astype(jnp.float32)
    center = jnp.mean(values, axis=-1, keepdims=True)
    spread = jnp.mean(jnp.square(values - center), axis=-1, keepdims=True)
    return ((values - center) * lax.rsqrt(spread + EPSILON) * (1.0 + scale) + shift).astype(
        jnp.bfloat16
    )


def absorb(carry, keys, values, first, queries, limits):
    peak, weight_sum, numer = carry
    videos_here = keys.shape[0]
    count = keys.shape[1]
    heads_here = queries.shape[2]
    head_size = queries.shape[3]
    key_heads = keys.reshape(videos_here, count, heads_here, head_size)
    value_heads = values.reshape(videos_here, count, heads_here, head_size)
    scores = jnp.einsum(
        "vqhd,vkhd->vhqk", queries, key_heads, preferred_element_type=jnp.float32
    ) * head_size ** (-0.5)
    position = first + jnp.arange(count, dtype=jnp.int32)
    valid = (position[None, :] < limits[:, None])[:, None, None, :]
    scores = jnp.where(valid, scores, FLOOR)
    new_peak = jnp.maximum(peak, jnp.max(scores, axis=-1))
    factor = jnp.exp(peak - new_peak)
    probs = jnp.exp(scores - new_peak[..., None]) * valid.astype(jnp.float32)
    weight_sum = weight_sum * factor + jnp.sum(probs, axis=-1)
    numer = numer * factor[..., None] + jnp.einsum(
        "vhqk,vkhd->vhqd",
        probs.astype(jnp.bfloat16),
        value_heads,
        preferred_element_type=jnp.float32,
    )
    return (new_peak, weight_sum, numer)


def general_body(hidden_states, modulation, w_qkv, w_out, lengths):
    videos_here = hidden_states.shape[0]
    width = hidden_states.shape[2]
    shift = modulation[:, 0][:, None, :]
    scale = modulation[:, 1][:, None, :]
    gate = modulation[:, 2][:, None, :]
    normed = modulated_norm(hidden_states, shift, scale)
    tile_rows = lax.all_gather(normed, "wcol", axis=1, tiled=True)
    tile_len = tile_rows.shape[1]
    local_cols = w_qkv.shape[2]
    flat_rows = tile_rows.reshape(videos_here * tile_len, width)
    piece = lax.all_gather(w_qkv, "wrow", axis=0, tiled=True)
    mixed = jnp.dot(
        flat_rows, piece.reshape(piece.shape[0], 3 * local_cols), preferred_element_type=jnp.float32
    )
    mixed = mixed.reshape(videos_here, tile_len, 3 * local_cols)
    mixed = mixed.astype(jnp.bfloat16).reshape(videos_here, tile_len, 3, local_cols)
    heads_here = local_cols // HD
    queries = mixed[:, :, 0].reshape(videos_here, tile_len, heads_here, HD)
    keys = mixed[:, :, 1]
    values = mixed[:, :, 2]
    start_peak = jnp.full((videos_here, heads_here, tile_len), FLOOR, jnp.float32)
    start_sum = jnp.zeros((videos_here, heads_here, tile_len), jnp.float32)
    start_numer = jnp.zeros((videos_here, heads_here, tile_len, HD), jnp.float32)
    key_piece = lax.all_gather(keys, "patch", axis=1, tiled=True)
    value_piece = lax.all_gather(values, "patch", axis=1, tiled=True)
    count = key_piece.shape[1]
    block_len = 512

    def one_block(index, inner):
        offset = index * block_len
        key_block = lax.dynamic_slice_in_dim(key_piece, offset, block_len, 1)
        value_block = lax.dynamic_slice_in_dim(value_piece, offset, block_len, 1)
        return absorb(inner, key_block, value_block, offset, queries, lengths)

    peak, weight_sum, numer = lax.fori_loop(
        0, count // block_len, one_block, (start_peak, start_sum, start_numer)
    )
    attended = (numer / weight_sum[..., None]).astype(jnp.bfloat16)
    attended = jnp.transpose(attended, (0, 2, 1, 3)).reshape(videos_here * tile_len, local_cols)
    partial_out = jnp.dot(
        attended,
        lax.all_gather(w_out, "wrow", axis=1, tiled=True),
        preferred_element_type=jnp.float32,
    )
    partial_out = partial_out.reshape(videos_here, tile_len, width)
    out_proj = lax.psum_scatter(
        partial_out.astype(jnp.bfloat16), "wcol", scatter_dimension=1, tiled=True
    ).astype(jnp.float32)
    return (hidden_states.astype(jnp.float32) + gate * out_proj).astype(jnp.bfloat16)


SHIFTS = ((1, 1, 0), (0, 0, 0), (0, 1, 0), (1, 0, 0), (1, 1, 1), (0, 0, 1), (0, 1, 1), (1, 0, 1))
VMEM_LIMIT = 18 * 1024 * 1024


def start_shard(spot_ref, here, sent, start, weight_ref, sem):
    depth, width = here.shape[1:]
    owner = spot_ref[0] == spot_ref[3]
    for role, shard in ((owner, here), (jnp.logical_not(owner), sent)):

        @pl.when(role)
        def _():
            for k in range(3):
                pltpu.make_async_copy(
                    shard.at[k],
                    weight_ref.at[pl.ds(start, depth), pl.ds(k * width, width)],
                    sem.at[k],
                ).start()


def wait_shard(here, start, weight_ref, sem):
    depth, width = here.shape[1:]
    for k in range(3):
        pltpu.make_async_copy(
            here.at[k],
            weight_ref.at[pl.ds(start, depth), pl.ds(k * width, width)],
            sem.at[k],
        ).wait()


def norm_kernel(spot_ref, mod_ref, *refs):
    tiles, out_ref, tile_ref = refs[0:4], refs[4], refs[5]
    tile_len, width = tiles[0].shape
    depth = width // 4
    shift = mod_ref[0]
    scale = 1.0 + mod_ref[1]
    for i in range(4):
        rows = pl.ds(i * tile_len, tile_len)
        values = tiles[i][...].astype(jnp.float32)
        center = jnp.mean(values, axis=-1, keepdims=True)
        values = values - center
        spread = jnp.mean(jnp.square(values), axis=-1, keepdims=True)
        tile_ref[...] = (values * lax.rsqrt(spread + EPSILON) * scale + shift).astype(jnp.bfloat16)
        for d in range(4):
            start = pl.multiple_of((spot_ref[2] ^ d) * depth, HD)
            out_ref[rows, d * depth : (d + 1) * depth] = tile_ref[:, pl.ds(start, depth)]


def start_by_role(spot_ref, here, sent, place, sem):
    owner = spot_ref[0] == spot_ref[3]
    for role, source in ((owner, here), (jnp.logical_not(owner), sent)):

        @pl.when(role)
        def _():
            pltpu.make_async_copy(source, place, sem).start()


def early_kernel(spot_ref, own_rows_ref, other_rows_ref, *refs):
    here, sent, states_ref = refs[0:3], refs[3:6], refs[6]
    own_ref, other_ref, out_weight_ref, kept_ref, weight_ref, weight_sem, out_sem = refs[7:]
    depth = here[0].shape[1]
    keep = pltpu.make_async_copy(states_ref, kept_ref, out_sem.at[3])
    keep.start()
    for d in range(3):
        start_shard(spot_ref, here[d], sent[d], d * depth, weight_ref, weight_sem.at[d])
    for d in range(3):
        pltpu.make_async_copy(here[d].at[3], out_weight_ref.at[d], out_sem.at[d]).start()
    for d in range(3):
        wait_shard(here[d], d * depth, weight_ref, weight_sem.at[d])
    step = own_ref.shape[0] // 2
    skip = weight_ref.shape[1] - other_ref.shape[1]
    for r in range(2):
        span = pl.ds(r * step, step)
        own_ref[span, :] = jnp.dot(
            own_rows_ref[span, : 3 * depth], weight_ref[...], preferred_element_type=jnp.float32
        )
    for r in range(2):
        span = pl.ds(r * step, step)
        other_ref[span, :] = jnp.dot(
            other_rows_ref[span, : 3 * depth],
            weight_ref[:, skip:],
            preferred_element_type=jnp.float32,
        )
    for d in range(3):
        pltpu.make_async_copy(here[d].at[3], out_weight_ref.at[d], out_sem.at[d]).wait()
    keep.wait()


def key_bias(spot_ref, len_ref, tile_len):
    x, y, core = spot_ref[0], spot_ref[1], spot_ref[3]
    lane = lax.broadcasted_iota(jnp.int32, (1, tile_len), 1)
    bias = []
    for dx, dy, dc in SHIFTS:
        base = ((x ^ dx) * 4 + (y ^ dy) * 2 + (core ^ dc)) * tile_len
        bias.append(jnp.where(base + lane < len_ref[0], 0.0, FLOOR))
    return jnp.concatenate(bias, axis=1)


def project(queries, key_ref, value_ref, out_weight_ref, bias):
    rate = HD ** (-0.5) * math.log2(math.e)
    heads = []
    for h in range(queries.shape[1] // HD):
        column = slice(h * HD, (h + 1) * HD)
        scores = lax.dot_general(
            queries[:, column],
            key_ref[:, column],
            (((1,), (1,)), ((), ())),
            preferred_element_type=jnp.float32,
        )
        scores = scores + bias
        peak = jnp.max(scores, axis=-1, keepdims=True)
        probs = jnp.exp2((scores - peak) * rate).astype(jnp.bfloat16)
        sums = jnp.dot(probs, value_ref[h], preferred_element_type=jnp.float32)
        heads.append((sums[:, :HD] / sums[:, HD:]).astype(jnp.bfloat16))
    part = jnp.dot(
        jnp.concatenate(heads, axis=1), out_weight_ref[...], preferred_element_type=jnp.float32
    )
    return part


def attend_kernel(spot_ref, len_ref, *refs):
    totals, rows_refs, out_here, out_sent, (here, sent) = refs[0:2], refs[2:4], refs[4], refs[5:8], refs[8:10]
    left_ref, right_ref, bias_ref, query_ref, key_ref, value_ref, out_weight_ref = refs[10:17]
    count, width = key_ref.shape
    depth = here.shape[1]
    z = spot_ref[2]
    bias_ref[...] = key_bias(spot_ref, len_ref, count // 8)
    for h in range(width // HD):
        value_ref[h, :, HD:] = jnp.ones((count, HD), jnp.bfloat16)
    step = count // 4

    def finish(shard):
        weights = jnp.concatenate([shard[k] for k in range(3)], axis=1)
        for r in range(4):
            span = pl.ds((r % 2) * step, step)
            rows = pl.ds(r * step, step)
            skip = 0 if r < 2 else width
            mixed = (
                totals[r // 2][span, :]
                + jnp.dot(
                    rows_refs[r // 2][span, 3 * depth :],
                    weights[:, skip:],
                    preferred_element_type=jnp.float32,
                )
            ).astype(jnp.bfloat16)
            if r < 2:
                query_ref[rows, :] = mixed[:, :width]
            key_ref[rows, :] = mixed[:, width - skip : 2 * width - skip]
            for h in range(width // HD):
                at = 2 * width - skip + h * HD
                value_ref[h, rows, :HD] = mixed[:, at : at + HD]

    owner = spot_ref[0] == spot_ref[3]
    held = [out_here.at[d] for d in range(3)], [part.at[0] for part in out_sent]
    for role, shard, parts in ((owner, here, held[0]), (jnp.logical_not(owner), sent, held[1])):

        @pl.when(role)
        def _():
            finish(shard)
            for d, part in enumerate(parts + [shard.at[3]]):
                start = pl.multiple_of((z ^ d) * width, HD)
                out_weight_ref[:, pl.ds(start, width)] = part[...]

    diagonal = project(query_ref[: step // 2, :], key_ref, value_ref, out_weight_ref, bias_ref[...])
    middle = left_ref.shape[1]
    left_ref[...] = diagonal[:, :middle].astype(jnp.bfloat16)
    right_ref[...] = diagonal[:, middle:].astype(jnp.bfloat16)


def attend_rest_kernel(bias_ref, query_ref, key_ref, value_ref, out_weight_ref, *out_refs):
    y_left_ref, y_right_ref, x_left_ref, x_right_ref = out_refs
    tile_len, middle = y_left_ref.shape
    queries = query_ref[2 * tile_len :, :]
    part = project(queries, key_ref, value_ref, out_weight_ref, bias_ref[...])
    y_left_ref[...] = part[:tile_len, :middle]
    y_right_ref[...] = part[:tile_len, middle:].astype(jnp.bfloat16)
    x_left_ref[...] = part[tile_len:, :middle].astype(jnp.bfloat16)
    x_right_ref[...] = part[tile_len:, middle:]


def attend_own_kernel(
    out_weight_ref, value_ref, key_ref, query_ref, bias_ref, mod_ref, states_ref, base_ref
):
    tile_len = base_ref.shape[0]
    queries = query_ref[tile_len : 2 * tile_len, :]
    own = project(queries, key_ref, value_ref, out_weight_ref, bias_ref[...])
    base_ref[...] = states_ref[...].astype(jnp.float32) + mod_ref[2] * own


def tiled_body(hidden_states, modulation, w_qkv, w_out, lengths):
    tile_len, width = hidden_states.shape[1:]
    depth, _, local_cols = w_qkv.shape
    states = hidden_states[0]
    x = lax.axis_index("patch")
    z = lax.axis_index("wrow")
    w = lax.axis_index("wcol")
    core = w % 2
    owner = x == core
    spot = jnp.stack([x, w // 2, z, core]).astype(jnp.int32)
    everywhere = ("patch", "wrow", "wcol")

    def index(a, b, c):
        return (a * 4 + b) * 4 + c

    def swap(array, axis, d, n):
        return lax.ppermute(array, axis, [(i, i ^ d) for i in range(n)])

    def owners_swap(array, d):
        pairs = [
            (index(a, b, c), index(a, b ^ d, c))
            for a in range(2)
            for b in range(4)
            for c in range(4)
            if c % 2 == a
        ]
        return lax.ppermute(array, everywhere, pairs)

    def core_swap(array):
        return swap(array, "wcol", 1, 4)

    full = pl.BlockSpec(memory_space=pltpu.VMEM)
    scalar = pl.BlockSpec(memory_space=pltpu.SMEM)
    anywhere = pl.BlockSpec(memory_space=pl.ANY)
    params = pltpu.CompilerParams(vmem_limit_bytes=VMEM_LIMIT)
    count = 8 * tile_len

    mod = jnp.transpose(modulation, (1, 0, 2))
    kinds = jnp.transpose(w_qkv, (1, 0, 2))

    four = jnp.concatenate([kinds, w_out[None]], axis=0)
    far = owners_swap(four, 2)
    near = owners_swap(four, 1)
    along_x = swap(states, "patch", 1, 2)
    along_y = swap(states, "wcol", 2, 4)
    diagonal = [(a * 4 + c, (a ^ 1) * 4 + (c ^ 2)) for a in range(2) for c in range(4)]
    along_xy = lax.ppermute(states, ("patch", "wcol"), diagonal)
    tiles = [along_xy, states, along_y, along_x]
    own_rows = pl.pallas_call(
        norm_kernel,
        out_shape=jax.ShapeDtypeStruct((count // 2, width), jnp.bfloat16),
        in_specs=[scalar] + [full] * 5,
        out_specs=full,
        scratch_shapes=[pltpu.VMEM((tile_len, width), jnp.bfloat16)],
        compiler_params=params,
        name="norm",
    )(spot, mod, *tiles)
    other_rows = core_swap(own_rows)

    last = owners_swap(far, 1)
    shards = [four, near, far]
    total_own, total_other, out_known, states_kept = pl.pallas_call(
        early_kernel,
        out_shape=(
            jax.ShapeDtypeStruct((count // 2, 3 * local_cols), jnp.float32),
            jax.ShapeDtypeStruct((count // 2, 2 * local_cols), jnp.float32),
            jax.ShapeDtypeStruct((3,) + w_out.shape, jnp.bfloat16),
            jax.ShapeDtypeStruct((tile_len, width), jnp.bfloat16),
        ),
        in_specs=[scalar] + [full] * 2 + [anywhere] * 7,
        out_specs=(full,) * 4,
        scratch_shapes=[
            pltpu.VMEM((3 * depth, 3 * local_cols), jnp.bfloat16),
            pltpu.SemaphoreType.DMA((3, 3)),
            pltpu.SemaphoreType.DMA((4,)),
        ],
        compiler_params=params,
        name="early",
    )(spot, own_rows, other_rows, *shards, *(core_swap(shard[:3]) for shard in shards), states)
    out_sent = [core_swap(shard[3:]) for shard in shards]
    last, total_own, *out_sent = lax.optimization_barrier((last, total_own, *out_sent))
    last_sent = core_swap(last)

    half = jax.ShapeDtypeStruct((tile_len, width // 2), jnp.bfloat16)
    half_f32 = jax.ShapeDtypeStruct((tile_len, width // 2), jnp.float32)
    xy_left, xy_right, *kept = pl.pallas_call(
        attend_kernel,
        out_shape=(
            half,
            half,
            jax.ShapeDtypeStruct((1, count), jnp.float32),
            jax.ShapeDtypeStruct((count // 2, local_cols), jnp.bfloat16),
            jax.ShapeDtypeStruct((count, local_cols), jnp.bfloat16),
            jax.ShapeDtypeStruct((local_cols // HD, count, 2 * HD), jnp.bfloat16),
            jax.ShapeDtypeStruct((local_cols, width), jnp.bfloat16),
        ),
        in_specs=[scalar, scalar] + [full] * 10,
        out_specs=(full,) * 7,
        compiler_params=params,
        name="attend",
    )(spot, lengths, total_own, total_other, own_rows, other_rows, out_known, *out_sent, last, last_sent)
    from_x = swap(xy_left, "patch", 1, 2)
    from_y = swap(xy_right, "wcol", 2, 4)
    y_left, y_right, x_left, x_right = pl.pallas_call(
        attend_rest_kernel,
        out_shape=(half_f32, half, half, half_f32),
        in_specs=[full] * 5,
        out_specs=(full,) * 4,
        compiler_params=params,
        name="attend_rest",
    )(*kept)
    base = pl.pallas_call(
        attend_own_kernel,
        out_shape=jax.ShapeDtypeStruct((tile_len, width), jnp.float32),
        in_specs=[full] * 7,
        out_specs=full,
        compiler_params=params,
        name="attend_own",
    )(*kept[::-1], mod, states_kept)
    got_x_left = swap(x_left, "patch", 1, 2)
    got_y_right = swap(y_right, "wcol", 2, 4)
    y_left = (y_left + from_x.astype(jnp.float32)).astype(jnp.bfloat16)
    x_right = (x_right + from_y.astype(jnp.float32)).astype(jnp.bfloat16)
    got_x_right = swap(x_right, "patch", 1, 2)
    got_y_left = swap(y_left, "wcol", 2, 4)
    middle = width // 2
    updated = []
    for columns, parts in (
        (slice(0, middle), (got_x_left, got_y_left)),
        (slice(middle, width), (got_x_right, got_y_right)),
    ):
        out_proj = parts[1].astype(jnp.float32) + parts[0].astype(jnp.float32)
        updated.append((mod[2, :, columns] * out_proj + base[:, columns]).astype(jnp.bfloat16))
    updated = jnp.concatenate(updated, axis=1)
    return updated[None]


def body(hidden_states, modulation, w_qkv, w_out, lengths, *, sizes):
    fits = sizes == (2, 4, 4) and hidden_states.shape[0] == 1 and w_qkv.shape[2] == 3 * HD
    if fits and hidden_states.shape[1] % HD == 0:
        return tiled_body(hidden_states, modulation, w_qkv, w_out, lengths)
    return general_body(hidden_states, modulation, w_qkv, w_out, lengths)


def solution(mesh):
    placed = (
        P("wrow", ("patch", "wcol"), None),
        P("wrow", None, None),
        P("wrow", None, "wcol"),
        P("wcol", "wrow"),
        P("wrow"),
    )
    sizes = tuple(mesh.shape[name] for name in ("patch", "wrow", "wcol"))
    return jax.shard_map(
        functools.partial(body, sizes=sizes),
        mesh=mesh,
        in_specs=placed,
        out_specs=P("wrow", ("patch", "wcol"), None),
        check_vma=False,
    )
```

```python
import functools
import math

import jax
import jax.numpy as jnp
from jax import lax
from jax.experimental import pallas as pl
from jax.experimental.pallas import tpu as pltpu
from jax.sharding import PartitionSpec as P

HD = 128


EPSILON = 1e-06
FLOOR = -1e30


def modulated_norm(states, shift, scale):
    values = states.astype(jnp.float32)
    center = jnp.mean(values, axis=-1, keepdims=True)
    spread = jnp.mean(jnp.square(values - center), axis=-1, keepdims=True)
    return ((values - center) * lax.rsqrt(spread + EPSILON) * (1.0 + scale) + shift).astype(
        jnp.bfloat16
    )


def absorb(carry, keys, values, first, queries, limits):
    peak, weight_sum, numer = carry
    videos_here = keys.shape[0]
    count = keys.shape[1]
    heads_here = queries.shape[2]
    head_size = queries.shape[3]
    key_heads = keys.reshape(videos_here, count, heads_here, head_size)
    value_heads = values.reshape(videos_here, count, heads_here, head_size)
    scores = jnp.einsum(
        "vqhd,vkhd->vhqk", queries, key_heads, preferred_element_type=jnp.float32
    ) * head_size ** (-0.5)
    position = first + jnp.arange(count, dtype=jnp.int32)
    valid = (position[None, :] < limits[:, None])[:, None, None, :]
    scores = jnp.where(valid, scores, FLOOR)
    new_peak = jnp.maximum(peak, jnp.max(scores, axis=-1))
    factor = jnp.exp(peak - new_peak)
    probs = jnp.exp(scores - new_peak[..., None]) * valid.astype(jnp.float32)
    weight_sum = weight_sum * factor + jnp.sum(probs, axis=-1)
    numer = numer * factor[..., None] + jnp.einsum(
        "vhqk,vkhd->vhqd",
        probs.astype(jnp.bfloat16),
        value_heads,
        preferred_element_type=jnp.float32,
    )
    return (new_peak, weight_sum, numer)


def general_body(hidden_states, modulation, w_qkv, w_out, lengths):
    videos_here = hidden_states.shape[0]
    width = hidden_states.shape[2]
    shift = modulation[:, 0][:, None, :]
    scale = modulation[:, 1][:, None, :]
    gate = modulation[:, 2][:, None, :]
    normed = modulated_norm(hidden_states, shift, scale)
    tile_rows = lax.all_gather(normed, "wcol", axis=1, tiled=True)
    tile_len = tile_rows.shape[1]
    local_cols = w_qkv.shape[2]
    flat_rows = tile_rows.reshape(videos_here * tile_len, width)
    piece = lax.all_gather(w_qkv, "wrow", axis=0, tiled=True)
    mixed = jnp.dot(
        flat_rows, piece.reshape(piece.shape[0], 3 * local_cols), preferred_element_type=jnp.float32
    )
    mixed = mixed.reshape(videos_here, tile_len, 3 * local_cols)
    mixed = mixed.astype(jnp.bfloat16).reshape(videos_here, tile_len, 3, local_cols)
    heads_here = local_cols // HD
    queries = mixed[:, :, 0].reshape(videos_here, tile_len, heads_here, HD)
    keys = mixed[:, :, 1]
    values = mixed[:, :, 2]
    start_peak = jnp.full((videos_here, heads_here, tile_len), FLOOR, jnp.float32)
    start_sum = jnp.zeros((videos_here, heads_here, tile_len), jnp.float32)
    start_numer = jnp.zeros((videos_here, heads_here, tile_len, HD), jnp.float32)
    key_piece = lax.all_gather(keys, "patch", axis=1, tiled=True)
    value_piece = lax.all_gather(values, "patch", axis=1, tiled=True)
    count = key_piece.shape[1]
    block_len = 512

    def one_block(index, inner):
        offset = index * block_len
        key_block = lax.dynamic_slice_in_dim(key_piece, offset, block_len, 1)
        value_block = lax.dynamic_slice_in_dim(value_piece, offset, block_len, 1)
        return absorb(inner, key_block, value_block, offset, queries, lengths)

    peak, weight_sum, numer = lax.fori_loop(
        0, count // block_len, one_block, (start_peak, start_sum, start_numer)
    )
    attended = (numer / weight_sum[..., None]).astype(jnp.bfloat16)
    attended = jnp.transpose(attended, (0, 2, 1, 3)).reshape(videos_here * tile_len, local_cols)
    partial_out = jnp.dot(
        attended,
        lax.all_gather(w_out, "wrow", axis=1, tiled=True),
        preferred_element_type=jnp.float32,
    )
    partial_out = partial_out.reshape(videos_here, tile_len, width)
    out_proj = lax.psum_scatter(
        partial_out.astype(jnp.bfloat16), "wcol", scatter_dimension=1, tiled=True
    ).astype(jnp.float32)
    return (hidden_states.astype(jnp.float32) + gate * out_proj).astype(jnp.bfloat16)


SHIFTS = ((1, 1, 0), (0, 0, 0), (0, 1, 0), (1, 0, 0), (1, 1, 1), (0, 0, 1), (0, 1, 1), (1, 0, 1))
VMEM_LIMIT = 18 * 1024 * 1024


def start_shard(spot_ref, here, sent, start, weight_ref, sem):
    depth, width = here.shape[1:]
    owner = spot_ref[0] == spot_ref[3]
    for role, shard in ((owner, here), (jnp.logical_not(owner), sent)):

        @pl.when(role)
        def _():
            for k in range(3):
                pltpu.make_async_copy(
                    shard.at[k],
                    weight_ref.at[pl.ds(start, depth), pl.ds(k * width, width)],
                    sem.at[k],
                ).start()


def wait_shard(here, start, weight_ref, sem):
    depth, width = here.shape[1:]
    for k in range(3):
        pltpu.make_async_copy(
            here.at[k],
            weight_ref.at[pl.ds(start, depth), pl.ds(k * width, width)],
            sem.at[k],
        ).wait()


def norm_kernel(spot_ref, mod_ref, *refs):
    tiles, out_ref, tile_ref = refs[0:4], refs[4], refs[5]
    tile_len, width = tiles[0].shape
    depth = width // 4
    shift = mod_ref[0]
    scale = 1.0 + mod_ref[1]
    for i in range(4):
        rows = pl.ds(i * tile_len, tile_len)
        values = tiles[i][...].astype(jnp.float32)
        center = jnp.mean(values, axis=-1, keepdims=True)
        values = values - center
        spread = jnp.mean(jnp.square(values), axis=-1, keepdims=True)
        tile_ref[...] = (values * lax.rsqrt(spread + EPSILON) * scale + shift).astype(jnp.bfloat16)
        for d in range(4):
            start = pl.multiple_of((spot_ref[2] ^ d) * depth, HD)
            out_ref[rows, d * depth : (d + 1) * depth] = tile_ref[:, pl.ds(start, depth)]


def start_by_role(spot_ref, here, sent, place, sem):
    owner = spot_ref[0] == spot_ref[3]
    for role, source in ((owner, here), (jnp.logical_not(owner), sent)):

        @pl.when(role)
        def _():
            pltpu.make_async_copy(source, place, sem).start()


def early_kernel(spot_ref, own_rows_ref, other_rows_ref, *refs):
    here, sent, states_ref = refs[0:3], refs[3:6], refs[6]
    own_ref, other_ref, out_weight_ref, kept_ref, weight_ref, weight_sem, out_sem = refs[7:]
    depth = here[0].shape[1]
    keep = pltpu.make_async_copy(states_ref, kept_ref, out_sem.at[3])
    keep.start()
    for d in range(3):
        start_shard(spot_ref, here[d], sent[d], d * depth, weight_ref, weight_sem.at[d])
    for d in range(3):
        pltpu.make_async_copy(here[d].at[3], out_weight_ref.at[d], out_sem.at[d]).start()
    for d in range(3):
        wait_shard(here[d], d * depth, weight_ref, weight_sem.at[d])
    step = own_ref.shape[0] // 2
    skip = weight_ref.shape[1] - other_ref.shape[1]
    for r in range(2):
        span = pl.ds(r * step, step)
        own_ref[span, :] = jnp.dot(
            own_rows_ref[span, : 3 * depth], weight_ref[...], preferred_element_type=jnp.float32
        )
    for r in range(2):
        span = pl.ds(r * step, step)
        other_ref[span, :] = jnp.dot(
            other_rows_ref[span, : 3 * depth],
            weight_ref[:, skip:],
            preferred_element_type=jnp.float32,
        )
    for d in range(3):
        pltpu.make_async_copy(here[d].at[3], out_weight_ref.at[d], out_sem.at[d]).wait()
    keep.wait()


def key_bias(spot_ref, len_ref, tile_len):
    x, y, core = spot_ref[0], spot_ref[1], spot_ref[3]
    lane = lax.broadcasted_iota(jnp.int32, (1, tile_len), 1)
    bias = []
    for dx, dy, dc in SHIFTS:
        base = ((x ^ dx) * 4 + (y ^ dy) * 2 + (core ^ dc)) * tile_len
        bias.append(jnp.where(base + lane < len_ref[0], 0.0, FLOOR))
    return jnp.concatenate(bias, axis=1)


def project(queries, key_ref, value_ref, out_weight_ref, bias):
    rate = HD ** (-0.5) * math.log2(math.e)
    heads = []
    for h in range(queries.shape[1] // HD):
        column = slice(h * HD, (h + 1) * HD)
        scores = lax.dot_general(
            queries[:, column],
            key_ref[:, column],
            (((1,), (1,)), ((), ())),
            preferred_element_type=jnp.float32,
        )
        scores = scores + bias
        peak = jnp.max(scores, axis=-1, keepdims=True)
        probs = jnp.exp2((scores - peak) * rate).astype(jnp.bfloat16)
        sums = jnp.dot(probs, value_ref[h], preferred_element_type=jnp.float32)
        heads.append((sums[:, :HD] / sums[:, HD:]).astype(jnp.bfloat16))
    part = jnp.dot(
        jnp.concatenate(heads, axis=1), out_weight_ref[...], preferred_element_type=jnp.float32
    )
    return part


def attend_kernel(spot_ref, len_ref, *refs):
    totals, rows_refs, out_here, out_sent, (here, sent) = refs[0:2], refs[2:4], refs[4], refs[5:8], refs[8:10]
    top_ref, bottom_ref, bias_ref, query_ref, key_ref, value_ref, out_weight_ref = refs[10:17]
    count, width = key_ref.shape
    depth = here.shape[1]
    z = spot_ref[2]
    bias_ref[...] = key_bias(spot_ref, len_ref, count // 8)
    for h in range(width // HD):
        value_ref[h, :, HD:] = jnp.ones((count, HD), jnp.bfloat16)
    step = count // 4

    def finish(shard):
        weights = jnp.concatenate([shard[k] for k in range(3)], axis=1)
        for r in range(4):
            span = pl.ds((r % 2) * step, step)
            rows = pl.ds(r * step, step)
            skip = 0 if r < 2 else width
            mixed = (
                totals[r // 2][span, :]
                + jnp.dot(
                    rows_refs[r // 2][span, 3 * depth :],
                    weights[:, skip:],
                    preferred_element_type=jnp.float32,
                )
            ).astype(jnp.bfloat16)
            if r < 2:
                query_ref[rows, :] = mixed[:, :width]
            key_ref[rows, :] = mixed[:, width - skip : 2 * width - skip]
            for h in range(width // HD):
                at = 2 * width - skip + h * HD
                value_ref[h, rows, :HD] = mixed[:, at : at + HD]

    owner = spot_ref[0] == spot_ref[3]
    held = [out_here.at[d] for d in range(3)], [part.at[0] for part in out_sent]
    for role, shard, parts in ((owner, here, held[0]), (jnp.logical_not(owner), sent, held[1])):

        @pl.when(role)
        def _():
            finish(shard)
            for d, part in enumerate(parts + [shard.at[3]]):
                start = pl.multiple_of((z ^ d) * width, HD)
                out_weight_ref[:, pl.ds(start, width)] = part[...]

    diagonal = project(query_ref[: step // 2, :], key_ref, value_ref, out_weight_ref, bias_ref[...])
    middle = top_ref.shape[0]
    top_ref[...] = diagonal[:middle].astype(jnp.bfloat16)
    bottom_ref[...] = diagonal[middle:].astype(jnp.bfloat16)


def attend_rest_kernel(bias_ref, query_ref, key_ref, value_ref, out_weight_ref, *out_refs):
    y_top_ref, y_bottom_ref, x_top_ref, x_bottom_ref = out_refs
    middle = y_top_ref.shape[0]
    tile_len = 2 * middle
    queries = query_ref[2 * tile_len :, :]
    part = project(queries, key_ref, value_ref, out_weight_ref, bias_ref[...])
    y_top_ref[...] = part[:middle]
    y_bottom_ref[...] = part[middle:tile_len].astype(jnp.bfloat16)
    x_top_ref[...] = part[tile_len : tile_len + middle].astype(jnp.bfloat16)
    x_bottom_ref[...] = part[tile_len + middle :]


def attend_own_kernel(
    out_weight_ref, value_ref, key_ref, query_ref, bias_ref, mod_ref, states_ref, base_ref
):
    tile_len = base_ref.shape[0]
    queries = query_ref[tile_len : 2 * tile_len, :]
    own = project(queries, key_ref, value_ref, out_weight_ref, bias_ref[...])
    base_ref[...] = states_ref[...].astype(jnp.float32) + mod_ref[2] * own


def tiled_body(hidden_states, modulation, w_qkv, w_out, lengths):
    tile_len, width = hidden_states.shape[1:]
    depth, _, local_cols = w_qkv.shape
    states = hidden_states[0]
    x = lax.axis_index("patch")
    z = lax.axis_index("wrow")
    w = lax.axis_index("wcol")
    core = w % 2
    owner = x == core
    spot = jnp.stack([x, w // 2, z, core]).astype(jnp.int32)
    everywhere = ("patch", "wrow", "wcol")

    def index(a, b, c):
        return (a * 4 + b) * 4 + c

    def swap(array, axis, d, n):
        return lax.ppermute(array, axis, [(i, i ^ d) for i in range(n)])

    def owners_swap(array, d):
        pairs = [
            (index(a, b, c), index(a, b ^ d, c))
            for a in range(2)
            for b in range(4)
            for c in range(4)
            if c % 2 == a
        ]
        return lax.ppermute(array, everywhere, pairs)

    def core_swap(array):
        return swap(array, "wcol", 1, 4)

    full = pl.BlockSpec(memory_space=pltpu.VMEM)
    scalar = pl.BlockSpec(memory_space=pltpu.SMEM)
    anywhere = pl.BlockSpec(memory_space=pl.ANY)
    params = pltpu.CompilerParams(vmem_limit_bytes=VMEM_LIMIT)
    count = 8 * tile_len

    mod = jnp.transpose(modulation, (1, 0, 2))
    kinds = jnp.transpose(w_qkv, (1, 0, 2))

    four = jnp.concatenate([kinds, w_out[None]], axis=0)
    far = owners_swap(four, 2)
    near = owners_swap(four, 1)
    along_x = swap(states, "patch", 1, 2)
    along_y = swap(states, "wcol", 2, 4)
    diagonal = [(a * 4 + c, (a ^ 1) * 4 + (c ^ 2)) for a in range(2) for c in range(4)]
    along_xy = lax.ppermute(states, ("patch", "wcol"), diagonal)
    tiles = [along_xy, states, along_y, along_x]
    own_rows = pl.pallas_call(
        norm_kernel,
        out_shape=jax.ShapeDtypeStruct((count // 2, width), jnp.bfloat16),
        in_specs=[scalar] + [full] * 5,
        out_specs=full,
        scratch_shapes=[pltpu.VMEM((tile_len, width), jnp.bfloat16)],
        compiler_params=params,
        name="norm",
    )(spot, mod, *tiles)
    other_rows = core_swap(own_rows)

    last = owners_swap(far, 1)
    shards = [four, near, far]
    total_own, total_other, out_known, states_kept = pl.pallas_call(
        early_kernel,
        out_shape=(
            jax.ShapeDtypeStruct((count // 2, 3 * local_cols), jnp.float32),
            jax.ShapeDtypeStruct((count // 2, 2 * local_cols), jnp.float32),
            jax.ShapeDtypeStruct((3,) + w_out.shape, jnp.bfloat16),
            jax.ShapeDtypeStruct((tile_len, width), jnp.bfloat16),
        ),
        in_specs=[scalar] + [full] * 2 + [anywhere] * 7,
        out_specs=(full,) * 4,
        scratch_shapes=[
            pltpu.VMEM((3 * depth, 3 * local_cols), jnp.bfloat16),
            pltpu.SemaphoreType.DMA((3, 3)),
            pltpu.SemaphoreType.DMA((4,)),
        ],
        compiler_params=params,
        name="early",
    )(spot, own_rows, other_rows, *shards, *(core_swap(shard[:3]) for shard in shards), states)
    out_sent = [core_swap(shard[3:]) for shard in shards]
    last, total_own, *out_sent = lax.optimization_barrier((last, total_own, *out_sent))
    last_sent = core_swap(last)

    half = jax.ShapeDtypeStruct((tile_len // 2, width), jnp.bfloat16)
    half_f32 = jax.ShapeDtypeStruct((tile_len // 2, width), jnp.float32)
    xy_top, xy_bottom, *kept = pl.pallas_call(
        attend_kernel,
        out_shape=(
            half,
            half,
            jax.ShapeDtypeStruct((1, count), jnp.float32),
            jax.ShapeDtypeStruct((count // 2, local_cols), jnp.bfloat16),
            jax.ShapeDtypeStruct((count, local_cols), jnp.bfloat16),
            jax.ShapeDtypeStruct((local_cols // HD, count, 2 * HD), jnp.bfloat16),
            jax.ShapeDtypeStruct((local_cols, width), jnp.bfloat16),
        ),
        in_specs=[scalar, scalar] + [full] * 10,
        out_specs=(full,) * 7,
        compiler_params=params,
        name="attend",
    )(spot, lengths, total_own, total_other, own_rows, other_rows, out_known, *out_sent, last, last_sent)
    from_x = swap(xy_top, "patch", 1, 2)
    from_y = swap(xy_bottom, "wcol", 2, 4)
    y_top, y_bottom, x_top, x_bottom = pl.pallas_call(
        attend_rest_kernel,
        out_shape=(half_f32, half, half, half_f32),
        in_specs=[full] * 5,
        out_specs=(full,) * 4,
        compiler_params=params,
        name="attend_rest",
    )(*kept)
    base = pl.pallas_call(
        attend_own_kernel,
        out_shape=jax.ShapeDtypeStruct((tile_len, width), jnp.float32),
        in_specs=[full] * 7,
        out_specs=full,
        compiler_params=params,
        name="attend_own",
    )(*kept[::-1], mod, states_kept)
    got_x_top = swap(x_top, "patch", 1, 2)
    got_y_bottom = swap(y_bottom, "wcol", 2, 4)
    y_top = (y_top + from_x.astype(jnp.float32)).astype(jnp.bfloat16)
    x_bottom = (x_bottom + from_y.astype(jnp.float32)).astype(jnp.bfloat16)
    got_x_bottom = swap(x_bottom, "patch", 1, 2)
    got_y_top = swap(y_top, "wcol", 2, 4)
    from_x = jnp.concatenate([got_x_top, got_x_bottom], axis=0)
    from_y = jnp.concatenate([got_y_top, got_y_bottom], axis=0)
    out_proj = from_y.astype(jnp.float32) + from_x.astype(jnp.float32)
    updated = (mod[2] * out_proj + base).astype(jnp.bfloat16)
    return updated[None]


def body(hidden_states, modulation, w_qkv, w_out, lengths, *, sizes):
    fits = sizes == (2, 4, 4) and hidden_states.shape[0] == 1 and w_qkv.shape[2] == 3 * HD
    if fits and hidden_states.shape[1] % HD == 0:
        return tiled_body(hidden_states, modulation, w_qkv, w_out, lengths)
    return general_body(hidden_states, modulation, w_qkv, w_out, lengths)


def solution(mesh):
    placed = (
        P("wrow", ("patch", "wcol"), None),
        P("wrow", None, None),
        P("wrow", None, "wcol"),
        P("wcol", "wrow"),
        P("wrow"),
    )
    sizes = tuple(mesh.shape[name] for name in ("patch", "wrow", "wcol"))
    return jax.shard_map(
        functools.partial(body, sizes=sizes),
        mesh=mesh,
        in_specs=placed,
        out_specs=P("wrow", ("patch", "wcol"), None),
        check_vma=False,
    )
```

```python
import functools
import math

import jax
import jax.numpy as jnp
from jax import lax
from jax.experimental import pallas as pl
from jax.experimental.pallas import tpu as pltpu
from jax.sharding import PartitionSpec as P

HD = 128


EPSILON = 1e-06
FLOOR = -1e30


def modulated_norm(states, shift, scale):
    values = states.astype(jnp.float32)
    center = jnp.mean(values, axis=-1, keepdims=True)
    spread = jnp.mean(jnp.square(values - center), axis=-1, keepdims=True)
    return ((values - center) * lax.rsqrt(spread + EPSILON) * (1.0 + scale) + shift).astype(
        jnp.bfloat16
    )


def absorb(carry, keys, values, first, queries, limits):
    peak, weight_sum, numer = carry
    videos_here = keys.shape[0]
    count = keys.shape[1]
    heads_here = queries.shape[2]
    head_size = queries.shape[3]
    key_heads = keys.reshape(videos_here, count, heads_here, head_size)
    value_heads = values.reshape(videos_here, count, heads_here, head_size)
    scores = jnp.einsum(
        "vqhd,vkhd->vhqk", queries, key_heads, preferred_element_type=jnp.float32
    ) * head_size ** (-0.5)
    position = first + jnp.arange(count, dtype=jnp.int32)
    valid = (position[None, :] < limits[:, None])[:, None, None, :]
    scores = jnp.where(valid, scores, FLOOR)
    new_peak = jnp.maximum(peak, jnp.max(scores, axis=-1))
    factor = jnp.exp(peak - new_peak)
    probs = jnp.exp(scores - new_peak[..., None]) * valid.astype(jnp.float32)
    weight_sum = weight_sum * factor + jnp.sum(probs, axis=-1)
    numer = numer * factor[..., None] + jnp.einsum(
        "vhqk,vkhd->vhqd",
        probs.astype(jnp.bfloat16),
        value_heads,
        preferred_element_type=jnp.float32,
    )
    return (new_peak, weight_sum, numer)


def general_body(hidden_states, modulation, w_qkv, w_out, lengths):
    videos_here = hidden_states.shape[0]
    width = hidden_states.shape[2]
    shift = modulation[:, 0][:, None, :]
    scale = modulation[:, 1][:, None, :]
    gate = modulation[:, 2][:, None, :]
    normed = modulated_norm(hidden_states, shift, scale)
    tile_rows = lax.all_gather(normed, "wcol", axis=1, tiled=True)
    tile_len = tile_rows.shape[1]
    local_cols = w_qkv.shape[2]
    flat_rows = tile_rows.reshape(videos_here * tile_len, width)
    piece = lax.all_gather(w_qkv, "wrow", axis=0, tiled=True)
    mixed = jnp.dot(
        flat_rows, piece.reshape(piece.shape[0], 3 * local_cols), preferred_element_type=jnp.float32
    )
    mixed = mixed.reshape(videos_here, tile_len, 3 * local_cols)
    mixed = mixed.astype(jnp.bfloat16).reshape(videos_here, tile_len, 3, local_cols)
    heads_here = local_cols // HD
    queries = mixed[:, :, 0].reshape(videos_here, tile_len, heads_here, HD)
    keys = mixed[:, :, 1]
    values = mixed[:, :, 2]
    start_peak = jnp.full((videos_here, heads_here, tile_len), FLOOR, jnp.float32)
    start_sum = jnp.zeros((videos_here, heads_here, tile_len), jnp.float32)
    start_numer = jnp.zeros((videos_here, heads_here, tile_len, HD), jnp.float32)
    key_piece = lax.all_gather(keys, "patch", axis=1, tiled=True)
    value_piece = lax.all_gather(values, "patch", axis=1, tiled=True)
    count = key_piece.shape[1]
    block_len = 512

    def one_block(index, inner):
        offset = index * block_len
        key_block = lax.dynamic_slice_in_dim(key_piece, offset, block_len, 1)
        value_block = lax.dynamic_slice_in_dim(value_piece, offset, block_len, 1)
        return absorb(inner, key_block, value_block, offset, queries, lengths)

    peak, weight_sum, numer = lax.fori_loop(
        0, count // block_len, one_block, (start_peak, start_sum, start_numer)
    )
    attended = (numer / weight_sum[..., None]).astype(jnp.bfloat16)
    attended = jnp.transpose(attended, (0, 2, 1, 3)).reshape(videos_here * tile_len, local_cols)
    partial_out = jnp.dot(
        attended,
        lax.all_gather(w_out, "wrow", axis=1, tiled=True),
        preferred_element_type=jnp.float32,
    )
    partial_out = partial_out.reshape(videos_here, tile_len, width)
    out_proj = lax.psum_scatter(
        partial_out.astype(jnp.bfloat16), "wcol", scatter_dimension=1, tiled=True
    ).astype(jnp.float32)
    return (hidden_states.astype(jnp.float32) + gate * out_proj).astype(jnp.bfloat16)


SHIFTS = ((1, 1, 0), (0, 0, 0), (0, 1, 0), (1, 0, 0), (1, 1, 1), (0, 0, 1), (0, 1, 1), (1, 0, 1))
VMEM_LIMIT = 18 * 1024 * 1024


def start_shard(spot_ref, here, sent, start, weight_ref, sem):
    depth, width = here.shape[1:]
    owner = spot_ref[0] == spot_ref[3]
    for role, shard in ((owner, here), (jnp.logical_not(owner), sent)):

        @pl.when(role)
        def _():
            for k in range(3):
                pltpu.make_async_copy(
                    shard.at[k],
                    weight_ref.at[pl.ds(start, depth), pl.ds(k * width, width)],
                    sem.at[k],
                ).start()


def wait_shard(here, start, weight_ref, sem):
    depth, width = here.shape[1:]
    for k in range(3):
        pltpu.make_async_copy(
            here.at[k],
            weight_ref.at[pl.ds(start, depth), pl.ds(k * width, width)],
            sem.at[k],
        ).wait()


def norm_kernel(spot_ref, mod_ref, *refs):
    tiles, out_ref, tile_ref = refs[0:4], refs[4], refs[5]
    tile_len, width = tiles[0].shape
    depth = width // 4
    shift = mod_ref[0]
    scale = 1.0 + mod_ref[1]
    for i in range(4):
        rows = pl.ds(i * tile_len, tile_len)
        values = tiles[i][...].astype(jnp.float32)
        center = jnp.mean(values, axis=-1, keepdims=True)
        values = values - center
        spread = jnp.mean(jnp.square(values), axis=-1, keepdims=True)
        tile_ref[...] = (values * lax.rsqrt(spread + EPSILON) * scale + shift).astype(jnp.bfloat16)
        for d in range(4):
            start = pl.multiple_of((spot_ref[2] ^ d) * depth, HD)
            out_ref[rows, d * depth : (d + 1) * depth] = tile_ref[:, pl.ds(start, depth)]


def start_by_role(spot_ref, here, sent, place, sem):
    owner = spot_ref[0] == spot_ref[3]
    for role, source in ((owner, here), (jnp.logical_not(owner), sent)):

        @pl.when(role)
        def _():
            pltpu.make_async_copy(source, place, sem).start()


def early_kernel(spot_ref, own_rows_ref, other_rows_ref, *refs):
    here, sent, states_ref = refs[0:3], refs[3:6], refs[6]
    own_ref, other_ref, out_weight_ref, kept_ref, weight_ref, weight_sem, out_sem = refs[7:]
    depth = here[0].shape[1]
    keep = pltpu.make_async_copy(states_ref, kept_ref, out_sem.at[3])
    keep.start()
    for d in range(3):
        start_shard(spot_ref, here[d], sent[d], d * depth, weight_ref, weight_sem.at[d])
    for d in range(3):
        pltpu.make_async_copy(here[d].at[3], out_weight_ref.at[d], out_sem.at[d]).start()
    for d in range(3):
        wait_shard(here[d], d * depth, weight_ref, weight_sem.at[d])
    step = own_ref.shape[0] // 2
    skip = weight_ref.shape[1] - other_ref.shape[1]
    for r in range(2):
        span = pl.ds(r * step, step)
        own_ref[span, :] = jnp.dot(
            own_rows_ref[span, : 3 * depth], weight_ref[...], preferred_element_type=jnp.float32
        )
    for r in range(2):
        span = pl.ds(r * step, step)
        other_ref[span, :] = jnp.dot(
            other_rows_ref[span, : 3 * depth],
            weight_ref[:, skip:],
            preferred_element_type=jnp.float32,
        )
    for d in range(3):
        pltpu.make_async_copy(here[d].at[3], out_weight_ref.at[d], out_sem.at[d]).wait()
    keep.wait()


def key_bias(spot_ref, len_ref, tile_len):
    x, y, core = spot_ref[0], spot_ref[1], spot_ref[3]
    lane = lax.broadcasted_iota(jnp.int32, (1, tile_len), 1)
    bias = []
    for dx, dy, dc in SHIFTS:
        base = ((x ^ dx) * 4 + (y ^ dy) * 2 + (core ^ dc)) * tile_len
        bias.append(jnp.where(base + lane < len_ref[0], 0.0, FLOOR))
    return jnp.concatenate(bias, axis=1)


def project(queries, key_ref, value_ref, out_weight_ref, bias):
    rate = HD ** (-0.5) * math.log2(math.e)
    heads = []
    for h in range(queries.shape[1] // HD):
        column = slice(h * HD, (h + 1) * HD)
        scores = lax.dot_general(
            queries[:, column],
            key_ref[:, column],
            (((1,), (1,)), ((), ())),
            preferred_element_type=jnp.float32,
        )
        scores = scores + bias
        peak = jnp.max(scores, axis=-1, keepdims=True)
        probs = jnp.exp2((scores - peak) * rate).astype(jnp.bfloat16)
        sums = jnp.dot(probs, value_ref[h], preferred_element_type=jnp.float32)
        heads.append((sums[:, :HD] * (1.0 / sums[:, HD:])).astype(jnp.bfloat16))
    part = jnp.dot(
        jnp.concatenate(heads, axis=1), out_weight_ref[...], preferred_element_type=jnp.float32
    )
    return part


def attend_kernel(spot_ref, len_ref, *refs):
    totals, rows_refs, out_here, out_sent, (here, sent) = refs[0:2], refs[2:4], refs[4], refs[5:8], refs[8:10]
    top_ref, bottom_ref, bias_ref, query_ref, key_ref, value_ref, out_weight_ref = refs[10:17]
    count, width = key_ref.shape
    depth = here.shape[1]
    z = spot_ref[2]
    bias_ref[...] = key_bias(spot_ref, len_ref, count // 8)
    for h in range(width // HD):
        value_ref[h, :, HD:] = jnp.ones((count, HD), jnp.bfloat16)
    step = count // 4

    def finish(shard):
        weights = jnp.concatenate([shard[k] for k in range(3)], axis=1)
        for r in range(4):
            span = pl.ds((r % 2) * step, step)
            rows = pl.ds(r * step, step)
            skip = 0 if r < 2 else width
            mixed = (
                totals[r // 2][span, :]
                + jnp.dot(
                    rows_refs[r // 2][span, 3 * depth :],
                    weights[:, skip:],
                    preferred_element_type=jnp.float32,
                )
            ).astype(jnp.bfloat16)
            if r < 2:
                query_ref[rows, :] = mixed[:, :width]
            key_ref[rows, :] = mixed[:, width - skip : 2 * width - skip]
            for h in range(width // HD):
                at = 2 * width - skip + h * HD
                value_ref[h, rows, :HD] = mixed[:, at : at + HD]

    owner = spot_ref[0] == spot_ref[3]
    held = [out_here.at[d] for d in range(3)], [part.at[0] for part in out_sent]
    for role, shard, parts in ((owner, here, held[0]), (jnp.logical_not(owner), sent, held[1])):

        @pl.when(role)
        def _():
            finish(shard)
            for d, part in enumerate(parts + [shard.at[3]]):
                start = pl.multiple_of((z ^ d) * width, HD)
                out_weight_ref[:, pl.ds(start, width)] = part[...]

    diagonal = project(query_ref[: step // 2, :], key_ref, value_ref, out_weight_ref, bias_ref[...])
    middle = top_ref.shape[0]
    top_ref[...] = diagonal[:middle].astype(jnp.bfloat16)
    bottom_ref[...] = diagonal[middle:].astype(jnp.bfloat16)


def attend_rest_kernel(bias_ref, query_ref, key_ref, value_ref, out_weight_ref, *out_refs):
    y_top_ref, y_bottom_ref, x_top_ref, x_bottom_ref = out_refs
    middle = y_top_ref.shape[0]
    tile_len = 2 * middle
    queries = query_ref[2 * tile_len :, :]
    part = project(queries, key_ref, value_ref, out_weight_ref, bias_ref[...])
    y_top_ref[...] = part[:middle]
    y_bottom_ref[...] = part[middle:tile_len].astype(jnp.bfloat16)
    x_top_ref[...] = part[tile_len : tile_len + middle].astype(jnp.bfloat16)
    x_bottom_ref[...] = part[tile_len + middle :]


def attend_own_kernel(
    out_weight_ref, value_ref, key_ref, query_ref, bias_ref, mod_ref, states_ref, base_ref
):
    tile_len = base_ref.shape[0]
    queries = query_ref[tile_len : 2 * tile_len, :]
    own = project(queries, key_ref, value_ref, out_weight_ref, bias_ref[...])
    base_ref[...] = states_ref[...].astype(jnp.float32) + mod_ref[2] * own


def tiled_body(hidden_states, modulation, w_qkv, w_out, lengths):
    tile_len, width = hidden_states.shape[1:]
    depth, _, local_cols = w_qkv.shape
    states = hidden_states[0]
    x = lax.axis_index("patch")
    z = lax.axis_index("wrow")
    w = lax.axis_index("wcol")
    core = w % 2
    owner = x == core
    spot = jnp.stack([x, w // 2, z, core]).astype(jnp.int32)
    everywhere = ("patch", "wrow", "wcol")

    def index(a, b, c):
        return (a * 4 + b) * 4 + c

    def swap(array, axis, d, n):
        return lax.ppermute(array, axis, [(i, i ^ d) for i in range(n)])

    def owners_swap(array, d):
        pairs = [
            (index(a, b, c), index(a, b ^ d, c))
            for a in range(2)
            for b in range(4)
            for c in range(4)
            if c % 2 == a
        ]
        return lax.ppermute(array, everywhere, pairs)

    def core_swap(array):
        return swap(array, "wcol", 1, 4)

    full = pl.BlockSpec(memory_space=pltpu.VMEM)
    scalar = pl.BlockSpec(memory_space=pltpu.SMEM)
    anywhere = pl.BlockSpec(memory_space=pl.ANY)
    params = pltpu.CompilerParams(vmem_limit_bytes=VMEM_LIMIT)
    count = 8 * tile_len

    mod = jnp.transpose(modulation, (1, 0, 2))
    kinds = jnp.transpose(w_qkv, (1, 0, 2))

    four = jnp.concatenate([kinds, w_out[None]], axis=0)
    far = owners_swap(four, 2)
    near = owners_swap(four, 1)
    along_x = swap(states, "patch", 1, 2)
    along_y = swap(states, "wcol", 2, 4)
    diagonal = [(a * 4 + c, (a ^ 1) * 4 + (c ^ 2)) for a in range(2) for c in range(4)]
    along_xy = lax.ppermute(states, ("patch", "wcol"), diagonal)
    tiles = [along_xy, states, along_y, along_x]
    own_rows = pl.pallas_call(
        norm_kernel,
        out_shape=jax.ShapeDtypeStruct((count // 2, width), jnp.bfloat16),
        in_specs=[scalar] + [full] * 5,
        out_specs=full,
        scratch_shapes=[pltpu.VMEM((tile_len, width), jnp.bfloat16)],
        compiler_params=params,
        name="norm",
    )(spot, mod, *tiles)
    other_rows = core_swap(own_rows)

    last = owners_swap(far, 1)
    shards = [four, near, far]
    total_own, total_other, out_known, states_kept = pl.pallas_call(
        early_kernel,
        out_shape=(
            jax.ShapeDtypeStruct((count // 2, 3 * local_cols), jnp.float32),
            jax.ShapeDtypeStruct((count // 2, 2 * local_cols), jnp.float32),
            jax.ShapeDtypeStruct((3,) + w_out.shape, jnp.bfloat16),
            jax.ShapeDtypeStruct((tile_len, width), jnp.bfloat16),
        ),
        in_specs=[scalar] + [full] * 2 + [anywhere] * 7,
        out_specs=(full,) * 4,
        scratch_shapes=[
            pltpu.VMEM((3 * depth, 3 * local_cols), jnp.bfloat16),
            pltpu.SemaphoreType.DMA((3, 3)),
            pltpu.SemaphoreType.DMA((4,)),
        ],
        compiler_params=params,
        name="early",
    )(spot, own_rows, other_rows, *shards, *(core_swap(shard[:3]) for shard in shards), states)
    out_sent = [core_swap(shard[3:]) for shard in shards]
    last, total_own, *out_sent = lax.optimization_barrier((last, total_own, *out_sent))
    last_sent = core_swap(last)

    half = jax.ShapeDtypeStruct((tile_len // 2, width), jnp.bfloat16)
    half_f32 = jax.ShapeDtypeStruct((tile_len // 2, width), jnp.float32)
    xy_top, xy_bottom, *kept = pl.pallas_call(
        attend_kernel,
        out_shape=(
            half,
            half,
            jax.ShapeDtypeStruct((1, count), jnp.float32),
            jax.ShapeDtypeStruct((count // 2, local_cols), jnp.bfloat16),
            jax.ShapeDtypeStruct((count, local_cols), jnp.bfloat16),
            jax.ShapeDtypeStruct((local_cols // HD, count, 2 * HD), jnp.bfloat16),
            jax.ShapeDtypeStruct((local_cols, width), jnp.bfloat16),
        ),
        in_specs=[scalar, scalar] + [full] * 10,
        out_specs=(full,) * 7,
        compiler_params=params,
        name="attend",
    )(spot, lengths, total_own, total_other, own_rows, other_rows, out_known, *out_sent, last, last_sent)
    from_x = swap(xy_top, "patch", 1, 2)
    from_y = swap(xy_bottom, "wcol", 2, 4)
    y_top, y_bottom, x_top, x_bottom = pl.pallas_call(
        attend_rest_kernel,
        out_shape=(half_f32, half, half, half_f32),
        in_specs=[full] * 5,
        out_specs=(full,) * 4,
        compiler_params=params,
        name="attend_rest",
    )(*kept)
    base = pl.pallas_call(
        attend_own_kernel,
        out_shape=jax.ShapeDtypeStruct((tile_len, width), jnp.float32),
        in_specs=[full] * 7,
        out_specs=full,
        compiler_params=params,
        name="attend_own",
    )(*kept[::-1], mod, states_kept)
    got_x_top = swap(x_top, "patch", 1, 2)
    got_y_bottom = swap(y_bottom, "wcol", 2, 4)
    y_top = (y_top + from_x.astype(jnp.float32)).astype(jnp.bfloat16)
    x_bottom = (x_bottom + from_y.astype(jnp.float32)).astype(jnp.bfloat16)
    got_x_bottom = swap(x_bottom, "patch", 1, 2)
    got_y_top = swap(y_top, "wcol", 2, 4)
    from_x = jnp.concatenate([got_x_top, got_x_bottom], axis=0)
    from_y = jnp.concatenate([got_y_top, got_y_bottom], axis=0)
    out_proj = from_y.astype(jnp.float32) + from_x.astype(jnp.float32)
    updated = (mod[2] * out_proj + base).astype(jnp.bfloat16)
    return updated[None]


def body(hidden_states, modulation, w_qkv, w_out, lengths, *, sizes):
    fits = sizes == (2, 4, 4) and hidden_states.shape[0] == 1 and w_qkv.shape[2] == 3 * HD
    if fits and hidden_states.shape[1] % HD == 0:
        return tiled_body(hidden_states, modulation, w_qkv, w_out, lengths)
    return general_body(hidden_states, modulation, w_qkv, w_out, lengths)


def solution(mesh):
    placed = (
        P("wrow", ("patch", "wcol"), None),
        P("wrow", None, None),
        P("wrow", None, "wcol"),
        P("wcol", "wrow"),
        P("wrow"),
    )
    sizes = tuple(mesh.shape[name] for name in ("patch", "wrow", "wcol"))
    return jax.shard_map(
        functools.partial(body, sizes=sizes),
        mesh=mesh,
        in_specs=placed,
        out_specs=P("wrow", ("patch", "wcol"), None),
        check_vma=False,
    )
```
